32 devices in a mesh: ctx: 8 (over z, y), fsdp: 4 (over x, core).
Axes of the slice: x: 2, y: 2, z: 4, core: 2. Of those that a mesh axis runs over, the one named last changes fastest.
Arguments:
- tokens: bfloat16 [2, 4096, 1024], P(None, ('fsdp', 'ctx')), may hold values from -6 to 6
- encoder: bfloat16 [2, 12288, 1024], P(None, ('fsdp', 'ctx')), may hold values from -6 to 6
- seq_lengths: int32 [4, 2, 3], P('fsdp'), may hold values from 1 to 768, 1024 in all within a row
- slot_ids: int32 [4, 2, 1024], P('fsdp', None, 'ctx'), may hold values from 0 to 1023, each once within a row
- enc_lengths: int32 [4, 2, 3], P('fsdp'), may hold values from 1 to 1024, 2048 in all within a row
- cotangent: bfloat16 [2, 4096, 1024], P(None, ('fsdp', 'ctx')), may hold values from -6 to 6
- self_in: bfloat16 [1024, 3072], P('fsdp'), may hold values from -0.1875 to 0.1875
- self_out: bfloat16 [1024, 1024], P('fsdp'), may hold values from -4 to 4
- cross_query: bfloat16 [1024, 1024], P('fsdp'), may hold values from -0.1875 to 0.1875
- cross_pair: bfloat16 [1024, 2048], P('fsdp'), may hold values from -0.1875 to 0.1875
- cross_out: bfloat16 [1024, 1024], P('fsdp'), may hold values from -3 to 3
- feed_up: bfloat16 [1024, 4096], P('fsdp'), may hold values from -0.1875 to 0.1875
- feed_down: bfloat16 [4096, 1024], P('fsdp'), may hold values from -0.09375 to 0.09375
- vectors: bfloat16 [1024, 12], P('fsdp'), as said below
- feed_bias: bfloat16 [4096], P('fsdp'), may hold values from -1.5 to 1.5
- self_bias: bfloat16 [1024], P('fsdp'), may hold values from -2.5 to 2.5
Outputs:
- layer_out: bfloat16 [2, 4096, 1024], P(None, ('fsdp', 'ctx'))
- grad_tokens: float32 [2, 4096, 1024], P(None, ('fsdp', 'ctx'))
- grad_encoder: float32 [2, 12288, 1024], P(None, ('fsdp', 'ctx'))
- grad_self_in: float32 [1024, 3072], P(('ctx', 'fsdp'))
- grad_self_out: float32 [1024, 1024], P(('ctx', 'fsdp'))
- grad_cross_query: float32 [1024, 1024], P(('ctx', 'fsdp'))
- grad_cross_pair: float32 [1024, 2048], P(('ctx', 'fsdp'))
- grad_cross_out: float32 [1024, 1024], P(('ctx', 'fsdp'))
- grad_feed_up: float32 [1024, 4096], P(('ctx', 'fsdp'))
- grad_feed_down: float32 [4096, 1024], P(('ctx', 'fsdp'))
- grad_vectors: float32 [1024, 12], P(('ctx', 'fsdp'))
- grad_feed_bias: float32 [4096], P(('ctx', 'fsdp'))
- grad_self_bias: float32 [1024], P(('ctx', 'fsdp'))
The draws below stay inside these ranges and needn't reach their ends.
Inputs may be any that keep to these rules, and one draw needn't show every extreme that they name: `seq_lengths`: each row sums to 1024; its longest sequence has exactly 768 tokens. `slot_ids`: each row is a permutation of the packed positions. `enc_lengths`: each row sums to 2048; its largest entry is exactly 1024. `vectors`: columns 0 to 2 are gains near one, the rest of order 0.3.
All inputs are finite; a program needn't handle non-finite values.
Results may differ from the reference program's by a relative error of at most 0.02.
The reference program's roundings to bfloat16 on the way count: a program that leaves them out, or rounds other values in their place, can miss the bound.
Values may be sent and summed in bfloat16 or wider, within the bound.
No kernel may reach another device: no remote copies, remote signals or barrier semaphores. Data moves between devices by JAX's collectives and lax.ppermute only.
A program may use at most 576 MiB of HBM per device.

```python
import math
import jax
import jax.numpy as jnp
import numpy as np
from jax import lax

D = 1024
H = 16
HD = 64
FF = 4096
ENC = 1024
NSEQ = 3
MICRO = 2
DEPTH = 6
CTXMB = 1024
TOKENS_MB = 4096
ENCTOK = 12288
N_CTX = 8
N_FSDP = 4


def draw_vectors(key, part):
    first_key, second_key = jax.random.split(jax.random.fold_in(key, 7))
    gains = 1.0 + 0.15 * jax.random.normal(first_key, (D, 3), jnp.float32)
    others = 0.3 * jax.random.normal(second_key, (D, 9), jnp.float32)
    return jnp.concatenate([gains, others], 1).astype(jnp.bfloat16)


def levels(own_key, dims, shards, low, largest):
    def one(position, shards_of):
        steps = jax.random.uniform(jax.random.fold_in(jax.random.fold_in(own_key, 6), position), (shards_of,), jnp.float32, low / len(shards), largest / len(shards))
        return jnp.repeat(jnp.exp(steps), dims[position] // shards_of).reshape((-1,) + (1,) * (len(dims) - position - 1))

    level = one(*shards[0])
    for cut in shards[1:]:
        level = level * one(*cut)
    return level


def split_up(amount, total, most, lean):
    portions = [(1 << 20) // math.isqrt(rank ** lean) + 1 for rank in range(2, amount + 1)]
    spare, counts = total - most - (amount - 1), [1] * (amount - 1)
    while spare > 0:
        free = [i for i in range(amount - 1) if counts[i] < most]
        mass, remaining = sum([portions[i] for i in free]), spare
        for i in free:
            more = min(most - counts[i], max(1, remaining * portions[i] // mass), spare)
            counts[i] = counts[i] + more
            spare = spare - more
    return np.array([most] + counts)


def ragged(stream_key, number_of, total, reach, skew):
    if number_of == 2:
        one = jax.random.randint(stream_key, (), max(1, total - reach), min(reach, total - 1) + 1)
        return jnp.stack([one, total - one])
    sizes = jnp.asarray(split_up(number_of, total, reach, skew), jnp.int32)
    couples = (number_of - 1) // 2
    donor, taker = sizes[1:1 + 2 * couples:2], sizes[2:2 + 2 * couples:2]
    margin = jnp.minimum(donor - 1, reach - taker)
    moved = jax.random.randint(jax.random.fold_in(stream_key, 1), (couples,), 0, 1 << 20) % (margin + 1)
    sizes = sizes.at[1:1 + 2 * couples:2].set(donor - moved).at[2:2 + 2 * couples:2].set(taker + moved)
    return sizes[jax.random.permutation(jax.random.fold_in(stream_key, 2), number_of)]


def noise(own_key, dims, spread, most, pieces=(), kind=jnp.bfloat16):
    values = jax.random.normal(own_key, dims, jnp.float32) * spread
    if len(pieces) > 0:
        values = levels(own_key, dims, pieces, -0.22, 0.18) * values
    return jnp.clip(values, min=-most, max=most).astype(kind)


def setup_inputs(seed: int = 0) -> dict:
    key_of = jax.random.split(jax.random.key(seed), 17)
    return {
        "tokens": noise(key_of[0], (MICRO, TOKENS_MB, D), 1.0, 6.0, ((1, 32),)),
        "encoder": noise(key_of[1], (MICRO, ENCTOK, D), 1.0, 6.0, ((1, 32),)),
        "seq_lengths": jax.vmap(lambda own: ragged(own, NSEQ, CTXMB, 3 * CTXMB // 4, 2))(jax.random.split(key_of[2], N_FSDP * MICRO)).reshape((N_FSDP, MICRO, NSEQ)).astype(jnp.int32),
        "slot_ids": jax.vmap(lambda own: jax.random.permutation(own, CTXMB))(jax.random.split(key_of[3], N_FSDP * MICRO)).reshape((N_FSDP, MICRO, CTXMB)).astype(jnp.int32),
        "enc_lengths": jax.vmap(lambda own: ragged(own, NSEQ, 2 * ENC, ENC, 1))(jax.random.split(key_of[4], N_FSDP * MICRO)).reshape((N_FSDP, MICRO, NSEQ)).astype(jnp.int32),
        "cotangent": noise(key_of[5], (MICRO, TOKENS_MB, D), 1.0, 6.0, ((1, 32),)),
        "self_in": noise(key_of[6], (D, 3 * D), D ** -0.5, 0.1875, ((0, 4),)),
        "self_out": noise(key_of[7], (D, D), (max(1, D // 512)) ** -0.5, 4.0, ((0, 4),)),
        "cross_query": noise(key_of[8], (D, D), D ** -0.5, 0.1875, ((0, 4),)),
        "cross_pair": noise(key_of[9], (D, 2 * D), D ** -0.5, 0.1875, ((0, 4),)),
        "cross_out": noise(key_of[10], (D, D), (max(1, D // 256)) ** -0.5, 3.0, ((0, 4),)),
        "feed_up": noise(key_of[11], (D, FF), D ** -0.5, 0.1875, ((0, 4),)),
        "feed_down": noise(key_of[12], (FF, D), FF ** -0.5, 0.09375, ((0, 4),)),
        "vectors": draw_vectors(jax.random.fold_in(key_of[16], 71), 0),
        "feed_bias": noise(key_of[14], (FF,), 0.3, 1.5, ((0, 4),)),
        "self_bias": noise(key_of[15], (D,), 0.5, 2.5, ((0, 4),)),
    }


@jax.custom_vjp
def low(v):
    return lax.optimization_barrier(v.astype(jnp.bfloat16)).astype(jnp.float32)

@jax.custom_vjp
def low_back(v):
    return v

def low_keep(v):
    return (low(v), None)

def low_pass(kept, grad):
    return (grad,)

def back_keep(v):
    return (v, None)

def back_low(kept, grad):
    return (low(grad),)
low.defvjp(low_keep, low_pass)
low_back.defvjp(back_keep, back_low)
EPSILON = 1e-05
MASKED = -1e+30
HIGHEST_PRECISION = lax.Precision.HIGHEST

def rounded(value):
    return low(low_back(value))

def matmul(left, right):
    return jnp.dot(left, right, precision=HIGHEST_PRECISION)

def layer_norm(resid, gain, offset):
    average = lax.optimization_barrier(jnp.mean(resid, -1, keepdims=True))
    centered = resid - average
    return centered * lax.rsqrt(lax.optimization_barrier(jnp.mean(centered * centered, -1, keepdims=True)) + EPSILON) * gain + offset

def attention(queries, keys, values, allow):
    number = queries.shape[0]
    query_heads = queries.reshape(number, H, HD)
    key_heads = keys.reshape(keys.shape[0], H, HD)
    value_heads = values.reshape(values.shape[0], H, HD)
    scores = low_back(jnp.einsum('qhd,khd->hqk', query_heads, key_heads, precision=HIGHEST_PRECISION) * HD ** (-0.5))
    scores = jnp.where(allow[None], scores, MASKED)
    maxima = lax.optimization_barrier(jnp.max(scores, -1, keepdims=True))
    exponent = jnp.exp(scores - maxima)
    probabilities = exponent / lax.optimization_barrier(jnp.sum(exponent, -1, keepdims=True))
    result = jnp.einsum('hqk,khd->qhd', low(probabilities), value_heads, precision=HIGHEST_PRECISION)
    return result.reshape(number, H * HD)

def blocked_attention(queries, keys, values, allow_rows, blocks):
    block_rows = queries.shape[0] // blocks

    def one_block(offset):
        block_queries = lax.dynamic_slice_in_dim(queries, offset * block_rows, block_rows, 0)
        return attention(block_queries, keys, values, allow_rows(offset * block_rows, block_rows))
    results = lax.map(jax.checkpoint(one_block), jnp.arange(blocks, dtype=jnp.int32))
    return results.reshape(queries.shape[0], -1)

def decoder_group(params, tokens_in, encoder_in, token_ids, lengths_in, limits_in):
    self_in, self_out, cross_query, cross_pair, cross_out, feed_up, feed_down, vectors, feed_bias, self_bias = params
    residual_scale = (3.0 * DEPTH) ** 0.25
    seq_ends = jnp.cumsum(lengths_in)
    seq_of = lax.optimization_barrier(jnp.sum((token_ids[:, None] >= seq_ends[None, :]).astype(jnp.int32), 1))
    zero_row = jnp.zeros((D,), tokens_in.dtype)
    qkv = rounded(matmul(tokens_in, self_in) + jnp.concatenate([vectors[:, 6], zero_row, vectors[:, 7]]))

    def self_allow(first, number):
        query_ids = lax.dynamic_slice_in_dim(token_ids, first, number, 0)
        query_seq = lax.dynamic_slice_in_dim(seq_of, first, number, 0)
        return (query_seq[:, None] == seq_of[None, :]) & (token_ids[None, :] <= query_ids[:, None])
    attended = rounded(blocked_attention(qkv[:, :D], qkv[:, D:2 * D], qkv[:, 2 * D:], self_allow, N_CTX))
    resid_one = residual_scale * tokens_in + low_back(matmul(attended, self_out) + self_bias)
    normed_one = layer_norm(resid_one, vectors[:, 0], vectors[:, 3])
    cross_queries = rounded(matmul(low(normed_one), cross_query) + vectors[:, 8])
    enc_pairs = rounded(matmul(encoder_in, cross_pair) + jnp.concatenate([zero_row, vectors[:, 9]]))
    enc_index = jnp.arange(NSEQ * ENC, dtype=jnp.int32)
    enc_seq = enc_index // ENC
    seq_index = jnp.arange(NSEQ, dtype=jnp.int32)
    enc_limit = lax.optimization_barrier(jnp.sum(jnp.where(enc_seq[:, None] == seq_index[None, :], limits_in[None, :], 0), 1))
    enc_live = enc_index % ENC < enc_limit

    def cross_allow(first, number):
        query_seq = lax.dynamic_slice_in_dim(seq_of, first, number, 0)
        return (query_seq[:, None] == enc_seq[None, :]) & enc_live[None, :]
    crossed = rounded(blocked_attention(cross_queries, enc_pairs[:, :D], enc_pairs[:, D:], cross_allow, N_CTX))
    resid_two = residual_scale * normed_one + low_back(matmul(crossed, cross_out) + vectors[:, 10])
    normed_two = layer_norm(resid_two, vectors[:, 1], vectors[:, 4])
    pre_active = low_back(matmul(low(normed_two), feed_up) + feed_bias)
    hidden = low(jax.nn.gelu(pre_active, approximate=False))
    resid_three = residual_scale * normed_two + low_back(matmul(hidden, feed_down) + vectors[:, 11])
    return layer_norm(resid_three, vectors[:, 2], vectors[:, 5])

def reference(tokens, encoder, seq_lengths, slot_ids, enc_lengths, cotangent, self_in, self_out, cross_query, cross_pair, cross_out, feed_up, feed_down, vectors, feed_bias, self_bias):
    params = tuple((weight.astype(jnp.float32) for weight in (self_in, self_out, cross_query, cross_pair, cross_out, feed_up, feed_down, vectors, feed_bias, self_bias)))
    groups = MICRO * N_FSDP
    tokens_all = tokens.astype(jnp.float32).reshape(groups, CTXMB, D)
    encoder_all = encoder.astype(jnp.float32).reshape(groups, NSEQ * ENC, D)
    ids_all = jnp.transpose(slot_ids, (1, 0, 2)).reshape(groups, CTXMB)
    lengths_all = jnp.transpose(seq_lengths, (1, 0, 2)).reshape(groups, NSEQ)
    limits_all = jnp.transpose(enc_lengths, (1, 0, 2)).reshape(groups, NSEQ)

    def forward(params_in, tokens_in, encoder_in):

        def group_step(unused_carry, group_items):
            tokens_row, encoder_row, ids_row, lengths_row, limits_row = group_items
            return (unused_carry, decoder_group(params_in, tokens_row, encoder_row, ids_row, lengths_row, limits_row))
        _, results = lax.scan(jax.checkpoint(group_step), jnp.zeros((), jnp.float32), (tokens_in, encoder_in, ids_all, lengths_all, limits_all))
        return results
    layer_all, pullback = jax.vjp(forward, params, tokens_all, encoder_all)
    grad_params, grad_tokens, grad_encoder = pullback(cotangent.astype(jnp.float32).reshape(groups, CTXMB, D))
    return (layer_all.reshape(MICRO, TOKENS_MB, D).astype(jnp.bfloat16), grad_tokens.reshape(MICRO, TOKENS_MB, D), grad_encoder.reshape(MICRO, ENCTOK, D), grad_params[0], grad_params[1], grad_params[2], grad_params[3], grad_params[4], grad_params[5], grad_params[6], grad_params[7], grad_params[8], grad_params[9])
```

```python
import functools

import jax
import jax.numpy as jnp
from jax import lax
from jax.experimental import pallas as pl
from jax.experimental.pallas import tpu as pltpu
from jax.sharding import Mesh
from jax.sharding import PartitionSpec as P

D = 1024
HD = 64
ENC = 1024
NSEQ = 3
MICRO = 2
DEPTH = 6

EPSILON = 1e-05
MASKED = -1e30
SCALE = HD ** (-0.5)
T_SIZE = 4
PAIR = 2
GROUP = ("y", "core")
ROWS = ("x", "core", "t", "s", "y")
BLOCKS = ("t", "s", "y", "x", "core")
MEMBERS = 4
WIDTH = D // MEMBERS
HEADS = WIDTH // HD
VMEM_LIMIT = 56 * 1024 * 1024


def norm_forward(resid, gain, offset):
    average = jnp.mean(resid, -1, keepdims=True)
    centered = resid - average
    inverse = lax.rsqrt(jnp.mean(centered * centered, -1, keepdims=True) + EPSILON)
    normed = centered * inverse
    return (normed * gain + offset, normed, inverse)


def norm_backward(grad_out, normed, inverse, gain):
    grad_normed = grad_out * gain
    first_mean = jnp.mean(grad_normed, -1, keepdims=True)
    second_mean = jnp.mean(grad_normed * normed, -1, keepdims=True)
    grad_resid = inverse * (grad_normed - first_mean - normed * second_mean)
    return (grad_resid, jnp.sum(grad_out * normed, 0), jnp.sum(grad_out, 0))


def gelu_slope(values):
    cumulative = 0.5 * (1.0 + jax.scipy.special.erf(values * 0.7071067811865476))
    density = jnp.exp(-0.5 * values * values) * 0.3989422804014327
    return cumulative + values * density


def column_sum(left, right):
    return lax.dot_general(
        left, right, (((0,), (0,)), ((), ())), preferred_element_type=jnp.float32
    )


def input_grad(grad_rows, weight):
    return lax.dot_general(
        grad_rows, weight, (((1,), (1,)), ((), ())), preferred_element_type=jnp.float32
    )


def linear(inputs, weight):
    return jnp.dot(inputs, weight, preferred_element_type=jnp.float32)


def pack_routes():
    straight, crossed = [], []
    for t in range(T_SIZE):
        for core in range(PAIR):
            here = t * PAIR + core
            straight.append((here, (2 * core + (t & 1)) * PAIR + (t >> 1)))
            crossed.append((here, (2 * core + 1 - (t & 1)) * PAIR + (t >> 1)))
    return straight, crossed


def to_packs(parts):
    straight, crossed = pack_routes()
    parity = lax.axis_index("t") & 1
    first = lax.dynamic_index_in_dim(parts, parity, 0, keepdims=False)
    second = lax.dynamic_index_in_dim(parts, 1 - parity, 0, keepdims=False)
    return (
        lax.ppermute(first, ("t", "core"), straight),
        lax.ppermute(second, ("t", "core"), crossed),
    )


def from_packs(first, second):
    straight, crossed = pack_routes()
    first = lax.ppermute(first, ("t", "core"), [(to, source) for source, to in straight])
    second = lax.ppermute(second, ("t", "core"), [(to, source) for source, to in crossed])
    parity = lax.axis_index("t") & 1
    return jnp.stack(
        [jnp.where(parity == 0, first, second), jnp.where(parity == 0, second, first)], 0
    )


def group_route(step):
    return [(member, member ^ step) for member in range(MEMBERS)]


def group_index():
    return lax.axis_index("y") * PAIR + lax.axis_index("core")


def share_in_group(block):
    return [block] + [
        lax.ppermute(block, GROUP, group_route(step)) for step in range(1, MEMBERS)
    ]


def to_heads(matrix):
    rows = matrix.shape[0]
    parts = matrix.shape[1] // D
    me = group_index()
    split = matrix.reshape(rows, parts, MEMBERS, WIDTH)
    blocks = []
    for step in range(MEMBERS):
        block = lax.dynamic_index_in_dim(split, me ^ step, 2, keepdims=False)
        block = block.reshape(rows, parts * WIDTH)
        blocks.append(block if step == 0 else lax.ppermute(block, GROUP, group_route(step)))
    return jnp.concatenate(blocks, 0)


def from_heads(matrix, parts):
    rows = matrix.shape[0] // MEMBERS
    me = group_index()
    blocks = []
    for step in range(MEMBERS):
        block = matrix[step * rows : (step + 1) * rows]
        blocks.append(block if step == 0 else lax.ppermute(block, GROUP, group_route(step)))
    table = jnp.stack(blocks, 0)
    columns = [
        lax.dynamic_index_in_dim(table, me ^ member, 0, keepdims=False) for member in range(MEMBERS)
    ]
    split = [block.reshape(rows, parts, WIDTH) for block in columns]
    return jnp.stack(split, 2).reshape(rows, parts * D)


def gather_sequence(matrix, count):
    if count == 1:
        return matrix
    return lax.all_gather(matrix, "s", axis=0, tiled=True)


def scatter_sequence(matrix, count):
    if count == 1:
        return matrix
    return lax.psum_scatter(matrix, "s", scatter_dimension=0, tiled=True)


def reduce_blocks(blocks, count, order):
    dtype = blocks.dtype
    names = ["t1", "t0", "s", "y", "x", "core"]
    sizes = [PAIR, PAIR, count, PAIR, PAIR, PAIR]
    value = blocks.reshape(tuple(sizes) + blocks.shape[1:])
    for name in order:
        place = names.index(name)
        names.pop(place)
        if name == "s":
            if count == 1:
                value = lax.squeeze(value, (place,))
            else:
                value = lax.psum_scatter(value, "s", scatter_dimension=place, tiled=False)
            continue
        axis = name[0] if name in ("t1", "t0") else name
        flip = {"t1": 2, "t0": 1}.get(name, 1)
        size = T_SIZE if axis == "t" else PAIR
        mine = lax.axis_index(axis)
        if name == "t1":
            mine = mine >> 1
        elif name == "t0":
            mine = mine & 1
        keep = lax.dynamic_index_in_dim(value, mine, place, keepdims=False)
        send = lax.dynamic_index_in_dim(value, 1 - mine, place, keepdims=False)
        arrived = lax.ppermute(send, axis, [(i, i ^ flip) for i in range(size)])
        value = (keep.astype(jnp.float32) + arrived.astype(jnp.float32)).astype(dtype)
    return value


def reduce_weight(gradient, count, order):
    blocks = T_SIZE * count * 8
    rows = gradient.shape[0] // blocks
    low = gradient.astype(jnp.bfloat16).reshape(blocks, rows, gradient.shape[1])
    return reduce_blocks(low, count, order).astype(jnp.float32)


def forward_kernel(
    chunk, flags_ref, q_ref, k_ref, v_ref, low_ref, high_ref, key_ref, out_ref, exact_ref, log_ref,
    masked_ref, top_ref, sum_ref, total_ref,
):
    step = pl.program_id(0)
    chunks = k_ref.shape[0] // chunk
    rows = q_ref.shape[0]
    lane = lax.broadcasted_iota(jnp.int32, (rows, 128), 1)
    for head in range(HEADS):
        pair = q_ref[:, (head // 2) * 128 : (head // 2 + 1) * 128] * SCALE
        masked_ref[head] = jnp.where((lane >= HD) == (head % 2 == 1), pair, 0).astype(jnp.bfloat16)
    top_ref[...] = jnp.full_like(top_ref, MASKED)
    sum_ref[...] = jnp.zeros_like(sum_ref)
    total_ref[...] = jnp.zeros_like(total_ref)

    def one_chunk(index, carry):
        @pl.when(flags_ref[step * chunks + index] != 0)
        def _():
            start = pl.multiple_of(index * chunk, chunk)
            keys = key_ref[:, pl.ds(start, chunk)]
            allow = (keys >= low_ref[...]) & (keys <= high_ref[...])
            bias = jnp.where(allow, 0.0, MASKED)
            for head in range(HEADS):
                columns = slice((head // 2) * 128, (head // 2 + 1) * 128)
                scores = lax.dot_general(
                    masked_ref[head],
                    k_ref[pl.ds(start, chunk), columns],
                    (((1,), (1,)), ((), ())),
                    preferred_element_type=jnp.float32,
                ) + bias
                before = top_ref[head]
                after = jnp.maximum(before, jnp.max(scores, 1, keepdims=True))
                exponent = jnp.exp(scores - after[:, :1])
                fade = jnp.exp(before - after)
                top_ref[head] = after
                sum_ref[head] = sum_ref[head] * fade + jnp.sum(exponent, 1, keepdims=True)
                total_ref[head] = total_ref[head] * fade + jnp.dot(
                    exponent.astype(jnp.bfloat16),
                    v_ref[pl.ds(start, chunk), columns],
                    preferred_element_type=jnp.float32,
                )

        return carry

    lax.fori_loop(0, chunks, one_chunk, 0)
    logs = jnp.zeros((rows, 128), jnp.float32)
    for head in range(0, HEADS, 2):
        first = total_ref[head] / sum_ref[head]
        second = total_ref[head + 1] / sum_ref[head + 1]
        both = jnp.where(lane < HD, first, second)
        columns = slice((head // 2) * 128, (head // 2 + 1) * 128)
        exact_ref[:, columns] = both
        out_ref[:, columns] = both.astype(jnp.bfloat16)
        for other in (head, head + 1):
            logs = jnp.where(lane == other, top_ref[other] + jnp.log(sum_ref[other]), logs)
    log_ref[...] = logs


def attend_forward(queries, keys, values, low, high, key_ids, flags, block, chunk):
    count, depth = queries[0].shape[0], keys[0].shape[0]
    whole = functools.partial(pl.BlockSpec, pipeline_mode=pl.Buffered(1))
    return pl.pallas_call(
        functools.partial(forward_kernel, chunk),
        grid_spec=pltpu.PrefetchScalarGridSpec(
            num_scalar_prefetch=1,
            grid=(count // block,),
            in_specs=[
                pl.BlockSpec((block, WIDTH), lambda i, f, c=queries[1]: (i, c)),
                whole((depth, WIDTH), lambda i, f, c=keys[1]: (0, c)),
                whole((depth, WIDTH), lambda i, f, c=values[1]: (0, c)),
                pl.BlockSpec((block, 1), lambda i, f: (i, 0)),
                pl.BlockSpec((block, 1), lambda i, f: (i, 0)),
                whole((1, depth), lambda i, f: (0, 0)),
            ],
            out_specs=[
                pl.BlockSpec((block, WIDTH), lambda i, f: (i, 0)),
                pl.BlockSpec((block, WIDTH), lambda i, f: (i, 0)),
                pl.BlockSpec((block, 128), lambda i, f: (i, 0)),
            ],
            scratch_shapes=[
                pltpu.VMEM((HEADS, block, 128), jnp.bfloat16),
                pltpu.VMEM((HEADS, block, 128), jnp.float32),
                pltpu.VMEM((HEADS, block, 128), jnp.float32),
                pltpu.VMEM((HEADS, block, 128), jnp.float32),
            ],
        ),
        out_shape=[
            jax.ShapeDtypeStruct((count, WIDTH), jnp.bfloat16),
            jax.ShapeDtypeStruct((count, WIDTH), jnp.float32),
            jax.ShapeDtypeStruct((count, 128), jnp.float32),
        ],
        compiler_params=pltpu.CompilerParams(vmem_limit_bytes=VMEM_LIMIT),
        cost_estimate=pl.CostEstimate(
            flops=4 * count * depth * WIDTH,
            bytes_accessed=8 * (count + depth) * WIDTH,
            transcendentals=count * depth * HEADS,
        ),
    )(flags.reshape(-1), queries[0], keys[0], values[0], low[:, None], high[:, None], key_ids[None, :])


def backward_kernel(
    chunk, flags_ref, q_ref, k_ref, v_ref, g_ref, log_ref, delta_ref, low_ref, high_ref, key_ref,
    dq_ref, dk_ref, dv_ref, q_masked, g_masked, turned_ref, dq_sum, dk_sum, dv_sum,
):
    step = pl.program_id(0)
    chunks = k_ref.shape[0] // chunk
    rows = q_ref.shape[0]
    lane = lax.broadcasted_iota(jnp.int32, (rows, 128), 1)

    @pl.when(step == 0)
    def _():
        dk_sum[...] = jnp.zeros_like(dk_sum)
        dv_sum[...] = jnp.zeros_like(dv_sum)

        def turn(index, carry):
            start = pl.multiple_of(index * chunk, chunk)
            turned_ref[:, pl.ds(start, chunk)] = k_ref[pl.ds(start, chunk), :].T
            return carry

        lax.fori_loop(0, chunks, turn, 0)

    for head in range(HEADS):
        columns = slice((head // 2) * 128, (head // 2 + 1) * 128)
        chosen = (lane >= HD) == (head % 2 == 1)
        q_masked[head] = jnp.where(chosen, q_ref[:, columns] * SCALE, 0).astype(jnp.bfloat16)
        g_masked[head] = jnp.where(chosen, g_ref[:, columns], 0).astype(jnp.bfloat16)
    dq_sum[...] = jnp.zeros_like(dq_sum)

    def one_chunk(index, carry):
        @pl.when(flags_ref[step * chunks + index] != 0)
        def _():
            start = pl.multiple_of(index * chunk, chunk)
            here = pl.ds(start, chunk)
            keys = key_ref[here, :]
            allow = (keys >= low_ref[...]) & (keys <= high_ref[...])
            bias = jnp.where(allow, 0.0, MASKED)
            for head in range(HEADS):
                columns = slice((head // 2) * 128, (head // 2 + 1) * 128)
                scores = lax.dot_general(
                    k_ref[here, columns],
                    q_masked[head],
                    (((1,), (1,)), ((), ())),
                    preferred_element_type=jnp.float32,
                )
                chances = jnp.exp(scores + bias - log_ref[head : head + 1, :])
                grads = lax.dot_general(
                    v_ref[here, columns],
                    g_masked[head],
                    (((1,), (1,)), ((), ())),
                    preferred_element_type=jnp.float32,
                )
                slopes = (chances * (grads - delta_ref[head : head + 1, :])).astype(jnp.bfloat16)
                dk_sum[here, columns] += jnp.dot(
                    slopes, q_masked[head], preferred_element_type=jnp.float32
                )
                dv_sum[here, columns] += jnp.dot(
                    chances.astype(jnp.bfloat16), g_masked[head], preferred_element_type=jnp.float32
                )
                dq_sum[head * HD : (head + 1) * HD, :] += jnp.dot(
                    turned_ref[head * HD : (head + 1) * HD, here],
                    slopes,
                    preferred_element_type=jnp.float32,
                )

        return carry

    lax.fori_loop(0, chunks, one_chunk, 0)
    dq_ref[...] = (dq_sum[...] * SCALE).T.astype(jnp.bfloat16)

    @pl.when(step == pl.num_programs(0) - 1)
    def _():
        dk_ref[...] = dk_sum[...].astype(jnp.bfloat16)
        dv_ref[...] = dv_sum[...].astype(jnp.bfloat16)


def attend_backward(
    queries, keys, values, grads, logs, delta, low, high, key_ids, flags, block, chunk
):
    count, depth = queries[0].shape[0], keys[0].shape[0]
    whole = functools.partial(pl.BlockSpec, pipeline_mode=pl.Buffered(1))
    return pl.pallas_call(
        functools.partial(backward_kernel, chunk),
        grid_spec=pltpu.PrefetchScalarGridSpec(
            num_scalar_prefetch=1,
            grid=(count // block,),
            in_specs=[
                pl.BlockSpec((block, WIDTH), lambda i, f, c=queries[1]: (i, c)),
                whole((depth, WIDTH), lambda i, f, c=keys[1]: (0, c)),
                whole((depth, WIDTH), lambda i, f, c=values[1]: (0, c)),
                pl.BlockSpec((block, WIDTH), lambda i, f: (i, 0)),
                pl.BlockSpec((HEADS, block), lambda i, f: (0, i)),
                pl.BlockSpec((HEADS, block), lambda i, f: (0, i)),
                pl.BlockSpec((1, block), lambda i, f: (0, i)),
                pl.BlockSpec((1, block), lambda i, f: (0, i)),
                whole((depth, 1), lambda i, f: (0, 0)),
            ],
            out_specs=[
                pl.BlockSpec((block, WIDTH), lambda i, f: (i, 0)),
                whole((depth, WIDTH), lambda i, f: (0, 0)),
                whole((depth, WIDTH), lambda i, f: (0, 0)),
            ],
            scratch_shapes=[
                pltpu.VMEM((HEADS, block, 128), jnp.bfloat16),
                pltpu.VMEM((HEADS, block, 128), jnp.bfloat16),
                pltpu.VMEM((WIDTH, depth), jnp.bfloat16),
                pltpu.VMEM((WIDTH, block), jnp.float32),
                pltpu.VMEM((depth, WIDTH), jnp.float32),
                pltpu.VMEM((depth, WIDTH), jnp.float32),
            ],
        ),
        out_shape=[
            jax.ShapeDtypeStruct((count, WIDTH), jnp.bfloat16),
            jax.ShapeDtypeStruct((depth, WIDTH), jnp.bfloat16),
            jax.ShapeDtypeStruct((depth, WIDTH), jnp.bfloat16),
        ],
        compiler_params=pltpu.CompilerParams(vmem_limit_bytes=VMEM_LIMIT),
        cost_estimate=pl.CostEstimate(
            flops=10 * count * depth * WIDTH,
            bytes_accessed=10 * (count + depth) * WIDTH,
            transcendentals=count * depth * HEADS,
        ),
    )(
        flags.reshape(-1), queries[0], keys[0], values[0], grads, logs, delta, low[None, :],
        high[None, :], key_ids[:, None],
    )


def needed_chunks(low, high, key_ids, block, chunk):
    first = jnp.min(low.reshape(-1, block), 1)[:, None]
    last = jnp.max(high.reshape(-1, block), 1)[:, None]
    smallest = jnp.min(key_ids.reshape(-1, chunk), 1)[None, :]
    largest = jnp.max(key_ids.reshape(-1, chunk), 1)[None, :]
    return ((largest >= first) & (smallest <= last)).astype(jnp.int32)


def log_rows(logs):
    return jnp.transpose(logs[:, :HEADS])


def delta_rows(grads, exact):
    products = grads.astype(jnp.float32) * exact
    return jnp.transpose(jnp.sum(products.reshape(-1, HEADS, HD), -1))


def on_device(
    count,
    tokens,
    encoder,
    seq_lengths,
    slot_ids,
    enc_lengths,
    cotangent,
    self_in,
    self_out,
    cross_query,
    cross_pair,
    cross_out,
    feed_up,
    feed_down,
    vectors,
    feed_bias,
    self_bias,
):
    residual_scale = (3.0 * DEPTH) ** 0.25
    fsdp = ("x", "core")

    def fetch(weight):
        return lax.all_gather(weight, fsdp, axis=0, tiled=True)

    full_self_in = fetch(self_in)
    facts = jnp.concatenate([slot_ids[0], seq_lengths[0], enc_lengths[0]], 1)
    slots = slot_ids.shape[2]
    facts_one, facts_two = to_packs(facts)
    tokens_in = jnp.concatenate(to_packs(tokens), 0)
    small = jnp.concatenate(
        [vectors.T, feed_bias.reshape(D // 4, 4).T, self_bias[None, :]], 0
    )
    full_small = lax.all_gather(small, fsdp, axis=1, tiled=True)
    encoder_in = jnp.concatenate(to_packs(encoder), 0)
    full_cross_pair = fetch(cross_pair)
    full_self_out = fetch(self_out)
    full_cross_q = fetch(cross_query)
    full_cross_out = fetch(cross_out)
    full_up = fetch(feed_up)
    full_down = fetch(feed_down)
    grad_in = jnp.concatenate(to_packs(cotangent), 0)

    vec = full_small[:12].astype(jnp.float32)
    bias_row = full_small[12:16].T.reshape(4 * D).astype(jnp.float32)
    self_bias_row = full_small[16].astype(jnp.float32)
    zero_row = jnp.zeros((D,), jnp.float32)

    lengths = facts_one[slots : slots + NSEQ]
    limits = facts_one[slots + NSEQ : slots + 2 * NSEQ]
    own_ids = jnp.concatenate([facts_one[:slots], facts_two[:slots]])
    ids = jnp.concatenate(share_in_group(own_ids))
    ends = jnp.cumsum(lengths)
    key_ids = gather_sequence(ids, count)
    rank = jnp.sum((ids[None, :] < ids[:, None]).astype(jnp.int32), 1)
    places = jnp.arange(ids.shape[0], dtype=jnp.int32)
    sorter = (places[:, None] == rank[None, :]).astype(jnp.bfloat16)
    sorted_ids = jnp.sum(jnp.where(places[:, None] == rank[None, :], ids[None, :], 0), 1)
    key_order = gather_sequence(sorted_ids, count)
    seq_of = jnp.sum((sorted_ids[:, None] >= ends[None, :]).astype(jnp.int32), 1)
    starts = jnp.concatenate([jnp.zeros((1,), jnp.int32), ends[:-1]])
    picked = seq_of[:, None] == jnp.arange(NSEQ, dtype=jnp.int32)[None, :]
    self_low = jnp.sum(jnp.where(picked, starts[None, :], 0), 1)
    self_high = sorted_ids
    cross_low = seq_of * ENC
    cross_high = cross_low + jnp.sum(jnp.where(picked, limits[None, :], 0), 1) - 1
    enc_rows = encoder.shape[1]
    micro = lax.axis_index("t") & 1
    enc_ids = []
    for place in range(count):
        index_s = place if count > 1 else 0
        for step in range(MEMBERS):
            core = lax.axis_index("core") ^ (step & 1)
            y_index = lax.axis_index("y") ^ (step >> 1)
            for part in range(2):
                t_index = 2 * core + (micro ^ part)
                row = ((t_index * count + index_s) * PAIR + y_index) * enc_rows
                enc_ids.append(row + jnp.arange(enc_rows, dtype=jnp.int32))
    enc_ids = jnp.concatenate(enc_ids)
    block = 256
    self_chunk, cross_chunk = 256, 384
    self_flags = needed_chunks(self_low, self_high, key_order, block, self_chunk)
    cross_flags = needed_chunks(cross_low, cross_high, enc_ids, block, cross_chunk)

    def sort_rows(matrix):
        return jnp.dot(sorter, matrix, preferred_element_type=jnp.float32).astype(jnp.bfloat16)

    def unsort_rows(matrix):
        return column_sum(sorter, matrix).astype(jnp.bfloat16)

    qkv = (
        linear(tokens_in, full_self_in) + jnp.concatenate([vec[6], zero_row, vec[7]])
    ).astype(jnp.bfloat16)
    own_heads = sort_rows(to_heads(qkv))
    if count > 1:
        pairs = gather_sequence(own_heads[:, WIDTH:], count)
        self_keys, self_values = (pairs, 0), (pairs, 1)
    else:
        self_keys, self_values = (own_heads, 1), (own_heads, 2)
    attended_heads, exact_self, log_self = attend_forward(
        (own_heads, 0), self_keys, self_values, self_low, self_high, key_order, self_flags,
        block, self_chunk,
    )
    attended = from_heads(unsort_rows(attended_heads), 1)

    enc_pairs = (
        linear(encoder_in, full_cross_pair) + jnp.concatenate([zero_row, vec[9]])
    ).astype(jnp.bfloat16)
    enc_heads = gather_sequence(to_heads(enc_pairs), count)

    resid_one = (
        residual_scale * tokens_in.astype(jnp.float32)
        + linear(attended, full_self_out)
        + self_bias_row
    )
    normed_one, unit_one, inverse_one = norm_forward(resid_one, vec[0], vec[3])
    normed_one_low = normed_one.astype(jnp.bfloat16)
    cross_queries = (linear(normed_one_low, full_cross_q) + vec[8]).astype(jnp.bfloat16)
    cross_heads = sort_rows(to_heads(cross_queries))
    crossed_heads, exact_cross, log_cross = attend_forward(
        (cross_heads, 0), (enc_heads, 0), (enc_heads, 1), cross_low, cross_high, enc_ids,
        cross_flags, block, cross_chunk,
    )
    crossed = from_heads(unsort_rows(crossed_heads), 1)
    resid_two = residual_scale * normed_one + linear(crossed, full_cross_out) + vec[10]
    normed_two, unit_two, inverse_two = norm_forward(resid_two, vec[1], vec[4])
    normed_two_low = normed_two.astype(jnp.bfloat16)
    pre_active = linear(normed_two_low, full_up) + bias_row
    hidden = jax.nn.gelu(pre_active, approximate=False).astype(jnp.bfloat16)
    resid_three = residual_scale * normed_two + linear(hidden, full_down) + vec[11]
    layer_value, unit_three, inverse_three = norm_forward(resid_three, vec[2], vec[5])
    layer_low = layer_value.astype(jnp.bfloat16)
    half = tokens_in.shape[0] // 2
    layer_out = from_packs(layer_low[:half], layer_low[half:])

    order_x = ("core", "x", "y", "t1", "t0", "s")
    order_y = ("core", "y", "x", "t1", "t0", "s")
    grad_three, gain_three, offset_three = norm_backward(
        grad_in.astype(jnp.float32), unit_three, inverse_three, vec[2]
    )
    grad_branch = grad_three.astype(jnp.bfloat16)
    grad_down = reduce_weight(column_sum(hidden, grad_branch), count, order_x)
    bias_down = jnp.sum(grad_branch.astype(jnp.float32), 0)
    grad_hidden = input_grad(grad_branch, full_down)
    grad_pre = (grad_hidden * gelu_slope(pre_active)).astype(jnp.bfloat16)
    grad_up = reduce_weight(column_sum(normed_two_low, grad_pre), count, order_y)
    bias_up = jnp.sum(grad_pre.astype(jnp.float32), 0)
    grad_two_in = residual_scale * grad_three + input_grad(grad_pre, full_up)
    grad_two, gain_two, offset_two = norm_backward(grad_two_in, unit_two, inverse_two, vec[1])
    grad_crossed_out = grad_two.astype(jnp.bfloat16)
    grad_cross_out = reduce_weight(column_sum(crossed, grad_crossed_out), count, order_x)
    bias_cross_out = jnp.sum(grad_crossed_out.astype(jnp.float32), 0)
    grad_crossed = input_grad(grad_crossed_out, full_cross_out).astype(jnp.bfloat16)
    grad_crossed_heads = sort_rows(to_heads(grad_crossed))
    dq_heads, dk_heads, dv_heads = attend_backward(
        (cross_heads, 0), (enc_heads, 0), (enc_heads, 1), grad_crossed_heads, log_rows(log_cross),
        delta_rows(grad_crossed_heads, exact_cross), cross_low, cross_high, enc_ids, cross_flags,
        block, cross_chunk,
    )
    grad_enc_heads = scatter_sequence(jnp.concatenate([dk_heads, dv_heads], 1), count)
    grad_enc_pairs = from_heads(grad_enc_heads, 2)
    grad_cross_queries = from_heads(unsort_rows(dq_heads), 1)
    grad_cross_q = reduce_weight(column_sum(normed_one_low, grad_cross_queries), count, order_y)
    bias_cross_q = jnp.sum(grad_cross_queries.astype(jnp.float32), 0)
    grad_cross_pair = reduce_weight(column_sum(encoder_in, grad_enc_pairs), count, order_x)
    bias_cross_value = jnp.sum(grad_enc_pairs[:, D:].astype(jnp.float32), 0)
    grad_enc = input_grad(grad_enc_pairs, full_cross_pair).astype(jnp.bfloat16)
    half_enc = encoder_in.shape[0] // 2
    grad_encoder = from_packs(grad_enc[:half_enc], grad_enc[half_enc:]).astype(jnp.float32)
    grad_one_in = residual_scale * grad_two + input_grad(grad_cross_queries, full_cross_q)
    grad_one, gain_one, offset_one = norm_backward(grad_one_in, unit_one, inverse_one, vec[0])
    grad_attended_out = grad_one.astype(jnp.bfloat16)
    grad_self_out = reduce_weight(column_sum(attended, grad_attended_out), count, order_y)
    bias_self_out = jnp.sum(grad_attended_out.astype(jnp.float32), 0)
    grad_attended = input_grad(grad_attended_out, full_self_out).astype(jnp.bfloat16)
    grad_attended_heads = sort_rows(to_heads(grad_attended))
    dq_heads, dk_heads, dv_heads = attend_backward(
        (own_heads, 0), self_keys, self_values, grad_attended_heads, log_rows(log_self),
        delta_rows(grad_attended_heads, exact_self), self_low, self_high, key_order, self_flags,
        block, self_chunk,
    )
    pair_heads = scatter_sequence(jnp.concatenate([dk_heads, dv_heads], 1), count)
    grad_qkv = from_heads(unsort_rows(jnp.concatenate([dq_heads, pair_heads], 1)), 3)
    grad_self_in = reduce_weight(column_sum(tokens_in, grad_qkv), count, order_x)
    bias_qkv = jnp.sum(grad_qkv.astype(jnp.float32), 0)
    grad_rows = (
        residual_scale * grad_one + input_grad(grad_qkv, full_self_in)
    ).astype(jnp.bfloat16)
    grad_tokens = from_packs(grad_rows[:half], grad_rows[half:]).astype(jnp.float32)

    blocks = T_SIZE * count * 8
    grad_vec = jnp.stack(
        [
            gain_one, gain_two, gain_three, offset_one, offset_two, offset_three, bias_qkv[:D],
            bias_qkv[2 * D :], bias_cross_q, bias_cross_value, bias_cross_out, bias_down,
        ],
        1,
    )
    small_grads = jnp.concatenate(
        [
            grad_vec.reshape(blocks, -1),
            bias_up.reshape(blocks, -1),
            bias_self_out.reshape(blocks, -1),
        ],
        1,
    )
    small_sum = reduce_blocks(small_grads, count, order_y)
    vec_end = 12 * D // blocks
    up_end = vec_end + 4 * D // blocks
    return (
        layer_out,
        grad_tokens,
        grad_encoder,
        grad_self_in,
        grad_self_out,
        grad_cross_q,
        grad_cross_pair,
        grad_cross_out,
        grad_up,
        grad_down,
        small_sum[:vec_end].reshape(D // blocks, 12),
        small_sum[vec_end:up_end],
        small_sum[up_end:],
    )


def solution(mesh):
    contexts = mesh.shape["ctx"]
    count = contexts // (T_SIZE * PAIR)
    fine = Mesh(
        mesh.devices.reshape(T_SIZE, count, PAIR, PAIR, PAIR), ("t", "s", "y", "x", "core")
    )
    fsdp, ctx = ("x", "core"), ("t", "s", "y")
    in_specs = (
        P(None, ROWS, None),
        P(None, ROWS, None),
        P(fsdp, None, None),
        P(fsdp, None, ctx),
        P(fsdp, None, None),
        P(None, ROWS, None),
        P(fsdp, None),
        P(fsdp, None),
        P(fsdp, None),
        P(fsdp, None),
        P(fsdp, None),
        P(fsdp, None),
        P(fsdp, None),
        P(fsdp, None),
        P(fsdp),
        P(fsdp),
    )
    out_specs = (P(None, ROWS, None),) * 3 + (P(BLOCKS, None),) * 8 + (P(BLOCKS),) * 2
    return jax.shard_map(
        functools.partial(on_device, count),
        mesh=fine,
        in_specs=in_specs,
        out_specs=out_specs,
        check_vma=False,
    )
```

```python
import functools

import jax
import jax.numpy as jnp
from jax import lax
from jax.experimental import pallas as pl
from jax.experimental.pallas import tpu as pltpu
from jax.sharding import Mesh
from jax.sharding import PartitionSpec as P

D = 1024
HD = 64
ENC = 1024
NSEQ = 3
MICRO = 2
DEPTH = 6

EPSILON = 1e-05
MASKED = -1e30
SCALE = HD ** (-0.5)
T_SIZE = 4
PAIR = 2
GROUP = ("y", "core")
ROWS = ("x", "core", "t", "s", "y")
BLOCKS = ("t", "s", "y", "x", "core")
MEMBERS = 4
WIDTH = D // MEMBERS
HEADS = WIDTH // HD
VMEM_LIMIT = 56 * 1024 * 1024
RESIDUAL = (3.0 * DEPTH) ** 0.25
COST = pl.CostEstimate(flops=0, bytes_accessed=0, transcendentals=0)


def norm_forward(resid, gain, offset):
    average = jnp.mean(resid, -1, keepdims=True)
    centered = resid - average
    inverse = lax.rsqrt(jnp.mean(centered * centered, -1, keepdims=True) + EPSILON)
    normed = centered * inverse
    return (normed * gain + offset, normed, inverse)


def norm_backward(grad_out, normed, inverse, gain):
    grad_normed = grad_out * gain
    first_mean = jnp.mean(grad_normed, -1, keepdims=True)
    second_mean = jnp.mean(grad_normed * normed, -1, keepdims=True)
    grad_resid = inverse * (grad_normed - first_mean - normed * second_mean)
    return (grad_resid, jnp.sum(grad_out * normed, 0), jnp.sum(grad_out, 0))


def gelu_slope(values):
    cumulative = 0.5 * (1.0 + lax.erf(values * 0.7071067811865476))
    density = jnp.exp(-0.5 * values * values) * 0.3989422804014327
    return cumulative + values * density


def column_sum(left, right):
    return lax.dot_general(
        left, right, (((0,), (0,)), ((), ())), preferred_element_type=jnp.float32
    )


def input_grad(grad_rows, weight):
    return lax.dot_general(
        grad_rows, weight, (((1,), (1,)), ((), ())), preferred_element_type=jnp.float32
    )


def linear(inputs, weight):
    return jnp.dot(inputs, weight, preferred_element_type=jnp.float32)


def pack_routes():
    straight, crossed = [], []
    for t in range(T_SIZE):
        for core in range(PAIR):
            here = t * PAIR + core
            straight.append((here, (2 * core + (t & 1)) * PAIR + (t >> 1)))
            crossed.append((here, (2 * core + 1 - (t & 1)) * PAIR + (t >> 1)))
    return straight, crossed


def to_packs(parts):
    straight, crossed = pack_routes()
    parity = lax.axis_index("t") & 1
    first = lax.dynamic_index_in_dim(parts, parity, 0, keepdims=False)
    second = lax.dynamic_index_in_dim(parts, 1 - parity, 0, keepdims=False)
    return (
        lax.ppermute(first, ("t", "core"), straight),
        lax.ppermute(second, ("t", "core"), crossed),
    )


def from_packs(first, second):
    straight, crossed = pack_routes()
    first = lax.ppermute(first, ("t", "core"), [(to, source) for source, to in straight])
    second = lax.ppermute(second, ("t", "core"), [(to, source) for source, to in crossed])
    parity = lax.axis_index("t") & 1
    return jnp.stack(
        [jnp.where(parity == 0, first, second), jnp.where(parity == 0, second, first)], 0
    )


def group_route(step):
    return [(member, member ^ step) for member in range(MEMBERS)]


def group_index():
    return lax.axis_index("y") * PAIR + lax.axis_index("core")


def join_kernel(parts, me_ref, *refs):
    matrix_ref = refs[-1]
    for step, block_ref in enumerate(refs[:-1]):
        for part in range(parts):
            start = pl.multiple_of(part * D + (me_ref[0] ^ step) * WIDTH, WIDTH)
            matrix_ref[:, pl.ds(start, WIDTH)] = block_ref[:, part * WIDTH : (part + 1) * WIDTH]


def join_members_kernel(blocks_ref, matrix_ref):
    rows = matrix_ref.shape[0]
    for member in range(MEMBERS):
        for part in range(matrix_ref.shape[1] // D):
            start = part * D + member * WIDTH
            matrix_ref[:, start : start + WIDTH] = blocks_ref[
                member * rows : (member + 1) * rows, part * WIDTH : (part + 1) * WIDTH
            ]


def in_vmem(count):
    return [pl.BlockSpec(memory_space=pltpu.VMEM)] * count


def small_kernel(body, scalars, operands, outs, work=0):
    return pl.pallas_call(
        body,
        in_specs=[pl.BlockSpec(memory_space=pltpu.SMEM)] * len(scalars) + in_vmem(len(operands)),
        out_specs=in_vmem(len(outs)),
        out_shape=outs,
        compiler_params=pltpu.CompilerParams(vmem_limit_bytes=VMEM_LIMIT),
        cost_estimate=COST,
    )(*scalars, *operands)


def gelu(values):
    return 0.5 * values * (1.0 + lax.erf(values * 0.7071067811865476))


def fetch(weight):
    return lax.all_gather(weight, ("x", "core"), axis=0, tiled=True)


SWAP = [(0, 1), (1, 0)]


def stack_feed(up, down):
    return jnp.concatenate([down] + [up[:, part * D : (part + 1) * D] for part in range(4)], 0)


def up_specs(column):
    def block(i, p):
        place = column(i, p)
        return (MEMBERS + place // 2, place % 2)

    return [pl.BlockSpec((D // MEMBERS, FEED_TILE), block)] * MEMBERS


def shard_index():
    return (lax.axis_index("x") * PAIR + lax.axis_index("core"))[None]


def product(rows_ref, weight_ref, start=0, width=None):
    columns = slice(start, weight_ref.shape[1] if width is None else start + width)
    if len(rows_ref.shape) == 2:
        return linear(rows_ref[...], weight_ref[:, columns])
    total = None
    for member in range(MEMBERS):
        lines = slice(member * WIDTH, (member + 1) * WIDTH)
        term = linear(rows_ref[member], weight_ref[lines, columns])
        total = term if total is None else total + term
    return total


def back_product(grads_ref, weight_ref, lines=slice(None), offset=0):
    if len(grads_ref.shape) == 2:
        return input_grad(
            grads_ref[...], weight_ref[lines, offset : offset + grads_ref.shape[1]]
        )
    total = None
    for member in range(MEMBERS):
        columns = slice(offset + member * WIDTH, offset + (member + 1) * WIDTH)
        term = input_grad(grads_ref[member], weight_ref[lines, columns])
        total = term if total is None else total + term
    return total


def put_heads(rows_ref, weight_ref, bias_ref, out_ref, offset=0):
    count = out_ref.shape[0] // MEMBERS
    for member in range(MEMBERS):
        for part in range(out_ref.shape[1] // WIDTH):
            start = part * D + member * WIDTH
            value = product(rows_ref, weight_ref, offset + start, WIDTH)
            value = value + bias_ref[:, start : start + WIDTH]
            out_ref[
                member * count : (member + 1) * count, part * WIDTH : (part + 1) * WIDTH
            ] = value.astype(jnp.bfloat16)


def put_back_heads(grads_ref, weight_ref, out_ref):
    count = out_ref.shape[0] // MEMBERS
    for member in range(MEMBERS):
        value = back_product(grads_ref, weight_ref, slice(member * WIDTH, (member + 1) * WIDTH))
        out_ref[member * count : (member + 1) * count, :] = value.astype(jnp.bfloat16)


def heads_kernel(rows_ref, weight_ref, bias_ref, out_ref):
    put_heads(rows_ref, weight_ref, bias_ref, out_ref)


def project_heads(rows, weight, bias):
    shape = jax.ShapeDtypeStruct((rows.shape[0] * MEMBERS, weight.shape[1] // MEMBERS), jnp.bfloat16)
    work = 2 * rows.shape[0] * weight.size
    return small_kernel(heads_kernel, [], [rows, weight, bias[None, :]], [shape], work)[0]


def own_heads_kernel(me_ref, rows_ref, weight_ref, bias_ref, *outs):
    for step, out_ref in reversed(list(enumerate(outs))):
        for part in range(out_ref.shape[1] // WIDTH):
            start = pl.multiple_of(part * D + (me_ref[0] ^ step) * WIDTH, WIDTH)
            value = linear(rows_ref[...], weight_ref[:, pl.ds(start, WIDTH)])
            value = value + bias_ref[:, pl.ds(start, WIDTH)]
            out_ref[:, part * WIDTH : (part + 1) * WIDTH] = value.astype(jnp.bfloat16)


def project_blocks(rows, weight, bias):
    shape = jax.ShapeDtypeStruct((rows.shape[0], weight.shape[1] // MEMBERS), jnp.bfloat16)
    work = 2 * rows.shape[0] * weight.size
    return small_kernel(
        own_heads_kernel, [group_index()[None]], [rows, weight, bias[None, :]], [shape] * MEMBERS,
        work,
    )


def norm_kernel(
    rows_ref, weight_ref, bias_ref, base_ref, gain_ref, offset_ref, *refs
):
    outs = refs if len(refs) == 4 else refs[1:]
    resid = (
        RESIDUAL * base_ref[...].astype(jnp.float32)
        + product(rows_ref, weight_ref, 0, D)
        + bias_ref[...]
    )
    normed, unit, inverse = norm_forward(resid, gain_ref[...], offset_ref[...])
    outs[0][...] = normed
    outs[1][...] = normed.astype(jnp.bfloat16)
    outs[2][...] = unit
    outs[3][...] = inverse
    if len(refs) > 4:
        put_heads(outs[1], weight_ref, refs[0], outs[4], D)


def project_norm(rows, weight, bias, base, gain, offset, after=()):
    count = base.shape[0]
    outs = [
        jax.ShapeDtypeStruct((count, D), jnp.float32),
        jax.ShapeDtypeStruct((count, D), jnp.bfloat16),
        jax.ShapeDtypeStruct((count, D), jnp.float32),
        jax.ShapeDtypeStruct((count, 1), jnp.float32),
    ]
    if after:
        outs.append(jax.ShapeDtypeStruct((count * MEMBERS, WIDTH), jnp.bfloat16))
    return small_kernel(
        norm_kernel, [],
        [rows, weight, bias[None, :], base, gain[None, :], offset[None, :]]
        + [row[None, :] for row in after],
        outs,
    )


FEED_TILE = 512


def feed_column(step, me, tiles):
    return (me ^ (step // tiles)) * tiles + step % tiles


def up_kernel(me_ref, rows_ref, *refs):
    shards, (bias_ref, active_ref, hidden_ref) = refs[:MEMBERS], refs[MEMBERS:]
    depth = shards[0].shape[0]
    active = bias_ref[...]
    for index, shard in enumerate(shards):
        start = pl.multiple_of((me_ref[0] ^ index) * depth, depth)
        active = active + linear(rows_ref[:, pl.ds(start, depth)], shard[...])
    active_ref[...] = active
    hidden_ref[...] = gelu(active).astype(jnp.bfloat16)


def feed_up_gelu(rows, shards, bias):
    count, width = rows.shape[0], 4 * D
    column = lambda i, p: (0, i)
    return pl.pallas_call(
        up_kernel,
        grid_spec=pltpu.PrefetchScalarGridSpec(
            num_scalar_prefetch=1,
            grid=(width // FEED_TILE,),
            in_specs=[pl.BlockSpec((count, D), lambda i, p: (0, 0))]
            + up_specs(lambda i, p: i)
            + [pl.BlockSpec((1, FEED_TILE), column)],
            out_specs=[pl.BlockSpec((count, FEED_TILE), column)] * 2,
        ),
        out_shape=[
            jax.ShapeDtypeStruct((count, width), jnp.float32),
            jax.ShapeDtypeStruct((count, width), jnp.bfloat16),
        ],
        compiler_params=pltpu.CompilerParams(vmem_limit_bytes=VMEM_LIMIT),
        cost_estimate=COST,
    )(shard_index(), rows, *shards, bias[None, :])


def put_norm_back(grads, unit, inverse, gain, resid_ref, low_ref, sums_ref):
    resid, gain_sum, offset_sum = norm_backward(grads, unit, inverse, gain)
    low = resid.astype(jnp.bfloat16)
    resid_ref[...] = resid
    low_ref[...] = low
    sums_ref[0:1, :] = gain_sum[None, :]
    sums_ref[1:2, :] = offset_sum[None, :]
    sums_ref[2:3, :] = jnp.sum(low.astype(jnp.float32), 0)[None, :]
    sums_ref[3:8, :] = jnp.zeros((5, D), jnp.float32)


def down_kernel(tiles, me_ref, hidden_ref, *refs):
    shards = refs[:MEMBERS]
    bias_ref, base_ref, gain_ref, offset_ref, grads_ref = refs[MEMBERS : MEMBERS + 5]
    layer_ref, resid_ref, low_ref, sums_ref, total_ref = refs[MEMBERS + 5 :]
    step = pl.program_id(0)

    @pl.when(step == 0)
    def _():
        total_ref[...] = RESIDUAL * base_ref[...] + bias_ref[...]

    for index, shard in enumerate(shards):

        @pl.when(step // tiles == index)
        def _(shard=shard):
            total_ref[...] += linear(hidden_ref[...], shard[...])

    @pl.when(step == pl.num_programs(0) - 1)
    def _():
        layer, unit, inverse = norm_forward(total_ref[...], gain_ref[...], offset_ref[...])
        layer_ref[...] = layer.astype(jnp.bfloat16)
        put_norm_back(
            grads_ref[...].astype(jnp.float32), unit, inverse, gain_ref[...], resid_ref, low_ref,
            sums_ref,
        )


def one_block(array):
    return pl.BlockSpec(array.shape, lambda i, p: (0,) * len(array.shape))


def down_specs(tiles):
    return [
        pl.BlockSpec((FEED_TILE, D), lambda i, p, s=s: (jnp.clip(i - s * tiles, 0, tiles - 1), 0))
        for s in range(MEMBERS)
    ]


def feed_down_norm(hidden, shards, bias, base, gain, offset, grads):
    count = base.shape[0]
    tiles = D // FEED_TILE
    fixed = [bias[None, :], base, gain[None, :], offset[None, :], grads]
    outs = [
        jax.ShapeDtypeStruct((count, D), jnp.bfloat16),
        jax.ShapeDtypeStruct((count, D), jnp.float32),
        jax.ShapeDtypeStruct((count, D), jnp.bfloat16),
        jax.ShapeDtypeStruct((8, D), jnp.float32),
    ]
    return pl.pallas_call(
        functools.partial(down_kernel, tiles),
        grid_spec=pltpu.PrefetchScalarGridSpec(
            num_scalar_prefetch=1,
            grid=(MEMBERS * tiles,),
            in_specs=[
                pl.BlockSpec((count, FEED_TILE), lambda i, p: (0, feed_column(i, p[0], tiles)))
            ]
            + down_specs(tiles)
            + [one_block(array) for array in fixed],
            out_specs=[one_block(out) for out in outs],
            scratch_shapes=[pltpu.VMEM((count, D), jnp.float32)],
        ),
        out_shape=outs,
        compiler_params=pltpu.CompilerParams(vmem_limit_bytes=VMEM_LIMIT),
        cost_estimate=COST,
    )(shard_index(), hidden, *shards, *fixed)


def feed_back_kernel(tiles, me_ref, active_ref, *refs):
    downs, ups, refs = refs[:MEMBERS], refs[MEMBERS : 2 * MEMBERS], refs[2 * MEMBERS :]
    grads_ref, resid_ref, unit_ref, inverse_ref, gain_ref, out_ref = refs[:6]
    du_ref, bias_ref, next_resid_ref, next_low_ref, sums_ref, heads_ref, total_ref = refs[6:]
    step = pl.program_id(0)
    depth = ups[0].shape[0]

    @pl.when(step == 0)
    def _():
        total_ref[...] = RESIDUAL * resid_ref[...]

    slope = gelu_slope(active_ref[...])
    for index, shard in enumerate(downs):

        @pl.when(step // tiles == index)
        def _(shard=shard):
            du_ref[...] = (back_product(grads_ref, shard) * slope).astype(jnp.bfloat16)

    du = du_ref[...]
    bias_ref[...] = jnp.sum(du.astype(jnp.float32), 0, keepdims=True)
    for index, shard in enumerate(ups):
        start = pl.multiple_of((me_ref[0] ^ index) * depth, depth)
        total_ref[:, pl.ds(start, depth)] += input_grad(du, shard[...])

    @pl.when(step == pl.num_programs(0) - 1)
    def _():
        put_norm_back(
            total_ref[...], unit_ref[...], inverse_ref[...], gain_ref[...], next_resid_ref,
            next_low_ref, sums_ref,
        )
        put_back_heads(next_low_ref, out_ref, heads_ref)


def feed_back(active, shards, grads, resid, unit, inverse, gain, out_weight):
    count, width = active.shape
    tiles = D // FEED_TILE
    fixed = [grads, resid, unit, inverse, gain[None, :], out_weight]
    column = lambda i, p: (0, feed_column(i, p[0], tiles))
    outs = [
        jax.ShapeDtypeStruct((count, width), jnp.bfloat16),
        jax.ShapeDtypeStruct((1, width), jnp.float32),
        jax.ShapeDtypeStruct((count, D), jnp.float32),
        jax.ShapeDtypeStruct((count, D), jnp.bfloat16),
        jax.ShapeDtypeStruct((8, D), jnp.float32),
        jax.ShapeDtypeStruct((count * MEMBERS, WIDTH), jnp.bfloat16),
    ]
    return pl.pallas_call(
        functools.partial(feed_back_kernel, tiles),
        grid_spec=pltpu.PrefetchScalarGridSpec(
            num_scalar_prefetch=1,
            grid=(MEMBERS * tiles,),
            in_specs=[pl.BlockSpec((count, FEED_TILE), column)]
            + down_specs(tiles)
            + up_specs(lambda i, p: feed_column(i, p[0], tiles))
            + [one_block(array) for array in fixed],
            out_specs=[
                pl.BlockSpec((count, FEED_TILE), column), pl.BlockSpec((1, FEED_TILE), column)
            ]
            + [one_block(out) for out in outs[2:]],
            scratch_shapes=[pltpu.VMEM((count, D), jnp.float32)],
        ),
        out_shape=outs,
        compiler_params=pltpu.CompilerParams(vmem_limit_bytes=VMEM_LIMIT),
        cost_estimate=COST,
    )(shard_index(), active, *shards, *shards, *fixed)


def norm_back_kernel(
    grads_ref, weight_ref, resid_ref, unit_ref, inverse_ref, gain_ref,
    next_resid_ref, next_low_ref, sums_ref, heads_ref,
):
    total = RESIDUAL * resid_ref[...] + back_product(grads_ref, weight_ref, offset=D)
    put_norm_back(
        total, unit_ref[...], inverse_ref[...], gain_ref[...], next_resid_ref, next_low_ref, sums_ref
    )
    put_back_heads(next_low_ref, weight_ref, heads_ref)


def back_norm(grads, weight, resid, unit, inverse, gain):
    count = resid.shape[0]
    outs = [
        jax.ShapeDtypeStruct((count, D), jnp.float32),
        jax.ShapeDtypeStruct((count, D), jnp.bfloat16),
        jax.ShapeDtypeStruct((8, D), jnp.float32),
        jax.ShapeDtypeStruct((count * MEMBERS, WIDTH), jnp.bfloat16),
    ]
    return small_kernel(
        norm_back_kernel, [], [grads, weight, resid, unit, inverse, gain[None, :]], outs
    )


def back_kernel(grads_ref, weight_ref, out_ref):
    out_ref[...] = back_product(grads_ref, weight_ref).astype(out_ref.dtype)


def back_project(grads, weight, dtype=jnp.bfloat16):
    count, width = grads.shape
    rows = 256
    return pl.pallas_call(
        back_kernel,
        grid=(weight.shape[0] // rows,),
        in_specs=[
            pl.BlockSpec((count, width), lambda i: (0, 0)),
            pl.BlockSpec((rows, width), lambda i: (i, 0)),
        ],
        out_specs=pl.BlockSpec((count, rows), lambda i: (0, i)),
        out_shape=jax.ShapeDtypeStruct((count, weight.shape[0]), dtype),
        compiler_params=pltpu.CompilerParams(vmem_limit_bytes=VMEM_LIMIT),
        cost_estimate=COST,
    )(grads, weight)


def to_members(blocks):
    return lax.all_to_all(blocks, GROUP, 0, 0, tiled=True)


def by_member(blocks):
    return blocks.reshape(MEMBERS, blocks.shape[0] // MEMBERS, blocks.shape[1])


def as_columns(blocks):
    shape = (blocks.shape[0] // MEMBERS, blocks.shape[1] * MEMBERS)
    return small_kernel(
        join_members_kernel, [], [blocks], [jax.ShapeDtypeStruct(shape, blocks.dtype)]
    )[0]


def chain(first, second):
    return lax.optimization_barrier((first, second))


def exchange(blocks):
    return [
        block if step == 0 else lax.ppermute(block, GROUP, group_route(step))
        for step, block in enumerate(blocks)
    ]


def during(blocks, work, inputs):
    own, inputs = chain(blocks[0], inputs)
    results, received = chain(work(*inputs), exchange(blocks)[1:])
    return [own, *received], results


def during_members(blocks, work, inputs):
    blocks, inputs = chain(blocks, inputs)
    results, received = chain(work(*inputs), to_members(blocks))
    return received, results


def join_heads(blocks, me):
    rows, parts = blocks[0].shape[0], blocks[0].shape[1] // WIDTH
    shape = jax.ShapeDtypeStruct((rows, parts * D), blocks[0].dtype)
    return small_kernel(
        functools.partial(join_kernel, parts), [me], blocks, [shape]
    )[0]


def cut(matrix):
    rows = matrix.shape[0] // MEMBERS
    return [matrix[step * rows : (step + 1) * rows] for step in range(MEMBERS)]


def sort_kernel(rank_ref, blocks_ref, sorted_ref):
    rows = blocks_ref.shape[0] // MEMBERS
    for place in range(MEMBERS):
        wanted = lax.broadcasted_iota(jnp.int32, (rows, rows * MEMBERS), 0) + place * rows
        pick = (rank_ref[...] == wanted).astype(jnp.bfloat16)
        sorted_ref[place * rows : (place + 1) * rows, :] = linear(pick, blocks_ref[...]).astype(
            jnp.bfloat16
        )


def put_unsorted(ranks, parts, block_ref, lines):
    rows = ranks.shape[0]
    wanted = lax.broadcasted_iota(jnp.int32, (rows, rows * MEMBERS), 1)
    pick = (ranks == wanted).astype(jnp.bfloat16)
    start = 0
    for sorted_ref in parts:
        end = start + sorted_ref.shape[1]
        block_ref[lines, start:end] = linear(pick, sorted_ref[...]).astype(jnp.bfloat16)
        start = end


def unsort_kernel(rank_ref, *refs):
    blocks_ref = refs[-1]
    rows = blocks_ref.shape[0] // MEMBERS
    for member in range(MEMBERS):
        lines = slice(member * rows, (member + 1) * rows)
        put_unsorted(rank_ref[lines, :], refs[:-1], blocks_ref, lines)


def sort_rows(blocks, rank):
    shape = jax.ShapeDtypeStruct(blocks.shape, jnp.bfloat16)
    work = 2 * blocks.size * blocks.shape[0]
    return small_kernel(sort_kernel, [], [rank[None, :], blocks], [shape], work)[0]


def unsort_rows(parts, rank):
    width = sum(part.shape[1] for part in parts)
    shape = jax.ShapeDtypeStruct((parts[0].shape[0], width), jnp.bfloat16)
    work = 2 * shape.size * shape.shape[0]
    return small_kernel(unsort_kernel, [], [rank[:, None], *parts], [shape], work)[0]


def gather_sequence(matrix, count):
    if count == 1:
        return matrix
    return lax.all_gather(matrix, "s", axis=0, tiled=True)


def scatter_sequence(matrix, count):
    if count == 1:
        return matrix
    return lax.psum_scatter(matrix, "s", scatter_dimension=0, tiled=True)


def own_bits():
    t_index = lax.axis_index("t")
    return {
        "t1": t_index >> 1,
        "t0": t_index & 1,
        "y": lax.axis_index("y"),
        "x": lax.axis_index("x"),
        "core": lax.axis_index("core"),
    }


def flip(block, name):
    if name in ("t1", "t0"):
        step = 2 if name == "t1" else 1
        return lax.ppermute(block, "t", [(i, i ^ step) for i in range(T_SIZE)])
    return lax.ppermute(block, name, [(i, i ^ 1) for i in range(PAIR)])


def relative_index(total, count, order):
    rows = total // (32 * count)
    place = jnp.arange(total, dtype=jnp.int32)
    bits, mine = {"r": place % rows, "s": place // rows % count}, own_bits()
    for index, name in enumerate(order):
        bits[name] = (place // (rows * count) >> (len(order) - 1 - index) & 1) ^ mine[name]
    row = (bits["t1"] * PAIR + bits["t0"]) * count + bits["s"]
    for name in ("y", "x", "core"):
        row = row * PAIR + bits[name]
    return row * rows + bits["r"]


def relative_columns(matrix, count, order):
    index = relative_index(matrix.shape[1], count, order)
    pick = jnp.arange(matrix.shape[1], dtype=jnp.int32)[:, None] == index[None, :]
    return linear(matrix, pick.astype(jnp.bfloat16)).astype(jnp.bfloat16)


def put_grads(pairs, outs):
    half, start = outs[0].shape[0], 0
    for left_ref, right in pairs:
        end = start + right.shape[1]
        for out_ref, lines in zip(outs, (slice(half, 2 * half), slice(0, half))):
            value = column_sum(left_ref[:, lines], right)
            out_ref[:, start:end] = value.astype(jnp.bfloat16)
        start = end
    return start


def grads_kernel(count, *refs):
    put_grads([(refs[i], refs[count + i][...]) for i in range(count)], refs[-2:])


def weight_grads(lefts, rights):
    half = lefts[0].shape[1] // 2
    shape = jax.ShapeDtypeStruct((half, sum(right.shape[1] for right in rights)), jnp.bfloat16)
    return small_kernel(
        functools.partial(grads_kernel, len(lefts)), [], [*lefts, *rights], [shape] * 2
    )


def self_in_kernel(
    left_ref, right_ref, grads_ref, pick_ref, one_ref, two_ref, three_ref, up_ref, query_ref,
    pair_ref, left_sent, left_kept, right_sent, right_kept, small_ref,
):
    middle = grads_ref.shape[1] // 2
    put_grads([(left_ref, grads_ref[:, :middle])], [left_sent, left_kept])
    start = put_grads([(right_ref, grads_ref[:, middle:])], [right_sent, right_kept])

    def total(rows):
        return jnp.sum(rows.astype(jnp.float32), 0, keepdims=True)

    small_ref[...] = jnp.zeros_like(small_ref)
    rows = [one_ref[0:1, :], two_ref[0:1, :], three_ref[0:1, :]]
    rows += [one_ref[1:2, :], two_ref[1:2, :], three_ref[1:2, :]]
    rows += [total(grads_ref[:, :D]), total(grads_ref[:, 2 * D :]), total(query_ref[...])]
    rows += [total(pair_ref[:, D:]), two_ref[2:3, :], three_ref[2:3, :], one_ref[2:3, :]]
    for place, row in enumerate(rows):
        small_ref[place : place + 1, :] = row
    small_ref[13:17, :] = up_ref[...]
    half = right_sent.shape[0]
    low = small_ref[...].astype(jnp.bfloat16)
    for out_ref, lines in ((right_sent, slice(half, 2 * half)), (right_kept, slice(0, half))):
        out_ref[:, start:] = input_grad(pick_ref[lines, :], low).astype(jnp.bfloat16)


def self_in_grads(left, right, grads, pick, one, two, three, up, query, pair):
    half, middle = D // 2, grads.shape[1] // 2
    outs = [jax.ShapeDtypeStruct((half, middle), jnp.bfloat16)] * 2
    outs += [jax.ShapeDtypeStruct((half, middle + 128), jnp.bfloat16)] * 2
    operands = [left, right, grads, pick, one, two, three, up.reshape(D, 4).T, query, pair]
    results = pl.pallas_call(
        self_in_kernel,
        in_specs=in_vmem(len(operands)),
        out_specs=in_vmem(len(outs)),
        out_shape=outs,
        scratch_shapes=[pltpu.VMEM((128, D), jnp.float32)],
        compiler_params=pltpu.CompilerParams(vmem_limit_bytes=VMEM_LIMIT),
        cost_estimate=COST,
    )(*operands)
    return results[:2], results[2:]


class Halving:
    def __init__(self, parts, count, order):
        sent, self.value = parts
        self.count, self.order = count, list(order)
        self.send(sent)

    def send(self, block):
        self.sent = block.astype(jnp.bfloat16)
        self.pending = flip(self.sent, self.order.pop(0))

    def step(self):
        total = self.value.astype(jnp.float32) + self.pending.astype(jnp.float32)
        half = total.shape[0] // 2
        self.value = total[:half]
        self.send(total[half:])

    def finish(self):
        total = self.value + self.pending.astype(jnp.float32)
        if self.count > 1:
            total = lax.psum_scatter(
                total.astype(jnp.bfloat16), "s", scatter_dimension=0, tiled=True
            ).astype(jnp.float32)
        return total


def feed_grads_kernel(hidden_ref, grads_ref, rows_ref, active_grads_ref, out_ref):
    others, _, _, rows, _ = out_ref.shape

    @pl.when(pl.program_id(0) == 0)
    def _():
        value = column_sum(hidden_ref[...], grads_ref[...]).astype(jnp.bfloat16)
        value = value.reshape(PAIR, others, 4, rows, D)
        for y_index in range(PAIR):
            out_ref[:, y_index] = value[y_index]

    @pl.when(pl.program_id(0) == 1)
    def _():
        for part in range(4):
            value = column_sum(rows_ref[...], active_grads_ref[:, part * D : (part + 1) * D])
            value = value.astype(jnp.bfloat16).reshape(PAIR, others, rows, D)
            for y_index in range(PAIR):
                out_ref[:, y_index, part] = value[y_index]


def feed_grads(hidden, grads, rows, active_grads, count):
    blocks = 32 * count
    lines = D // blocks
    size = rows.shape[0]
    if count > 1:
        parts = [column_sum(hidden, grads).astype(jnp.bfloat16).reshape(-1, PAIR, 4, 4, lines, D)]
        for part in range(4):
            up = column_sum(rows, active_grads[:, part * D : (part + 1) * D])
            parts.append(up.astype(jnp.bfloat16).reshape(-1, PAIR, 4, 1, lines, D))
        return jnp.swapaxes(jnp.concatenate(parts, 3), 1, 2).reshape(-1, PAIR, 8, lines, D)
    return pl.pallas_call(
        feed_grads_kernel,
        grid=(2, T_SIZE),
        in_specs=[
            pl.BlockSpec((size, D), lambda p, i: (0, jnp.where(p == 0, i, T_SIZE - 1))),
            pl.BlockSpec((size, D), lambda p, i: (0, 0)),
            pl.BlockSpec((size, D // T_SIZE), lambda p, i: (0, jnp.where(p == 0, 0, i))),
            pl.BlockSpec((size, 4 * D), lambda p, i: (0, 0)),
        ],
        out_specs=pl.BlockSpec((4, PAIR, 4, lines, D), lambda p, i: (i, 0, p, 0, 0)),
        out_shape=jax.ShapeDtypeStruct((blocks // PAIR, PAIR, 8, lines, D), jnp.bfloat16),
        compiler_params=pltpu.CompilerParams(vmem_limit_bytes=VMEM_LIMIT),
        cost_estimate=COST,
    )(hidden, grads, rows, active_grads)


def reduce_feed(parts):
    return lax.psum_scatter(parts, ("t", "s", "x", "core"), scatter_dimension=0, tiled=True)[0]


def split_feed(halves):
    mine = lax.axis_index("y")
    keep = lax.dynamic_index_in_dim(halves, mine, 0, keepdims=False)
    sent = lax.dynamic_index_in_dim(halves, 1 - mine, 0, keepdims=False)
    total = keep.astype(jnp.float32) + flip(sent, "y").astype(jnp.float32)
    return jnp.concatenate([total[4 + part] for part in range(4)], 1), total[:4].reshape(-1, D)


def forward_kernel(
    chunk, flags_ref, q_ref, k_ref, v_ref, low_ref, high_ref, key_ref, out_ref, exact_ref, log_ref,
    masked_ref, turned_ref, top_ref, sum_ref, total_ref,
):
    step = pl.program_id(0)
    chunks = k_ref.shape[0] // chunk
    rows = q_ref.shape[0]
    lane = lax.broadcasted_iota(jnp.int32, (rows, 128), 1)

    @pl.when(step == 0)
    def _():
        def turn(index, carry):
            start = pl.multiple_of(index * chunk, chunk)
            turned_ref[:, pl.ds(start, chunk)] = v_ref[pl.ds(start, chunk), :].T
            return carry

        lax.fori_loop(0, chunks, turn, 0)

    for head in range(HEADS):
        pair = q_ref[:, (head // 2) * 128 : (head // 2 + 1) * 128] * SCALE
        masked_ref[head] = jnp.where((lane >= HD) == (head % 2 == 1), pair, 0).astype(jnp.bfloat16)
    top_ref[...] = jnp.full_like(top_ref, MASKED)
    sum_ref[...] = jnp.zeros_like(sum_ref)
    total_ref[...] = jnp.zeros_like(total_ref)

    def one_chunk(index, carry):
        @pl.when(flags_ref[step * chunks + index] != 0)
        def _():
            start = pl.multiple_of(index * chunk, chunk)
            here = pl.ds(start, chunk)
            keys = key_ref[here, :]
            allow = (keys >= low_ref[...]) & (keys <= high_ref[...])
            bias = jnp.where(allow, 0.0, MASKED)
            for head in range(HEADS):
                columns = slice((head // 2) * 128, (head // 2 + 1) * 128)
                lines = slice(head * HD, (head + 1) * HD)
                scores = lax.dot_general(
                    k_ref[here, columns],
                    masked_ref[head],
                    (((1,), (1,)), ((), ())),
                    preferred_element_type=jnp.float32,
                ) + bias
                before = top_ref[head : head + 1, :]
                after = jnp.maximum(before, jnp.max(scores, 0, keepdims=True))
                exponent = jnp.exp(scores - after)
                fade = jnp.exp(before - after)
                top_ref[head : head + 1, :] = after
                sum_ref[head : head + 1, :] = sum_ref[head : head + 1, :] * fade + jnp.sum(
                    exponent, 0, keepdims=True
                )
                total_ref[lines, :] = total_ref[lines, :] * fade + jnp.dot(
                    turned_ref[lines, here],
                    exponent.astype(jnp.bfloat16),
                    preferred_element_type=jnp.float32,
                )

        return carry

    lax.fori_loop(0, chunks, one_chunk, 0)
    for head in range(HEADS):
        lines = slice(head * HD, (head + 1) * HD)
        total_ref[lines, :] = total_ref[lines, :] / sum_ref[head : head + 1, :]
    exact = total_ref[...].T
    exact_ref[...] = exact
    out_ref[...] = exact.astype(jnp.bfloat16)
    log_ref[:HEADS, :] = top_ref[:HEADS, :] + jnp.log(sum_ref[:HEADS, :])
    log_ref[HEADS:, :] = jnp.zeros((8 - HEADS, rows), jnp.float32)


def attend_forward(queries, keys, values, low, high, key_ids, flags, block, chunk):
    count, depth = queries[0].shape[0], keys[0].shape[0]
    whole = functools.partial(pl.BlockSpec, pipeline_mode=pl.Buffered(1))
    return pl.pallas_call(
        functools.partial(forward_kernel, chunk),
        grid_spec=pltpu.PrefetchScalarGridSpec(
            num_scalar_prefetch=1,
            grid=(count // block,),
            in_specs=[
                pl.BlockSpec((block, WIDTH), lambda i, f, c=queries[1]: (i, c)),
                whole((depth, WIDTH), lambda i, f, c=keys[1]: (0, c)),
                whole((depth, WIDTH), lambda i, f, c=values[1]: (0, c)),
                pl.BlockSpec((1, block), lambda i, f: (0, i)),
                pl.BlockSpec((1, block), lambda i, f: (0, i)),
                whole((depth, 1), lambda i, f: (0, 0)),
            ],
            out_specs=[
                pl.BlockSpec((block, WIDTH), lambda i, f: (i, 0)),
                pl.BlockSpec((block, WIDTH), lambda i, f: (i, 0)),
                pl.BlockSpec((8, block), lambda i, f: (0, i)),
            ],
            scratch_shapes=[
                pltpu.VMEM((HEADS, block, 128), jnp.bfloat16),
                pltpu.VMEM((WIDTH, depth), jnp.bfloat16),
                pltpu.VMEM((8, block), jnp.float32),
                pltpu.VMEM((8, block), jnp.float32),
                pltpu.VMEM((WIDTH, block), jnp.float32),
            ],
        ),
        out_shape=[
            jax.ShapeDtypeStruct((count, WIDTH), jnp.bfloat16),
            jax.ShapeDtypeStruct((count, WIDTH), jnp.float32),
            jax.ShapeDtypeStruct((8, count), jnp.float32),
        ],
        compiler_params=pltpu.CompilerParams(vmem_limit_bytes=VMEM_LIMIT),
        cost_estimate=COST,
    )(
        flags.reshape(-1), queries[0], keys[0], values[0], low[None, :], high[None, :],
        key_ids[:, None],
    )


def backward_kernel(
    chunk, flags_ref, q_ref, k_ref, v_ref, g_ref, log_ref, exact_ref, low_ref, high_ref, key_ref,
    dq_ref, *refs,
):
    pair_refs, (q_masked, g_masked, delta_ref, turned_ref, dq_sum, dk_sum, dv_sum) = (
        refs[:-7], refs[-7:]
    )
    step = pl.program_id(0)
    chunks = k_ref.shape[0] // chunk
    rows = q_ref.shape[0]
    lane = lax.broadcasted_iota(jnp.int32, (rows, 128), 1)

    @pl.when(step == 0)
    def _():
        dk_sum[...] = jnp.zeros_like(dk_sum)
        dv_sum[...] = jnp.zeros_like(dv_sum)

        def turn(index, carry):
            start = pl.multiple_of(index * chunk, chunk)
            turned_ref[:, pl.ds(start, chunk)] = k_ref[pl.ds(start, chunk), :].T
            return carry

        lax.fori_loop(0, chunks, turn, 0)

    for head in range(HEADS):
        columns = slice((head // 2) * 128, (head // 2 + 1) * 128)
        chosen = (lane >= HD) == (head % 2 == 1)
        q_masked[head] = jnp.where(chosen, q_ref[:, columns] * SCALE, 0).astype(jnp.bfloat16)
        g_masked[head] = jnp.where(chosen, g_ref[:, columns], 0).astype(jnp.bfloat16)
    dq_sum[...] = jnp.zeros_like(dq_sum)
    members = lax.broadcasted_iota(jnp.int32, (8, WIDTH), 1) // HD
    members = (members == lax.broadcasted_iota(jnp.int32, (8, WIDTH), 0)).astype(jnp.float32)
    delta_ref[...] = lax.dot_general(
        members,
        g_ref[...].astype(jnp.float32) * exact_ref[...],
        (((1,), (1,)), ((), ())),
        precision=lax.Precision.HIGHEST,
        preferred_element_type=jnp.float32,
    )

    def one_chunk(index, carry):
        @pl.when(flags_ref[step * chunks + index] != 0)
        def _():
            start = pl.multiple_of(index * chunk, chunk)
            here = pl.ds(start, chunk)
            keys = key_ref[here, :]
            allow = (keys >= low_ref[...]) & (keys <= high_ref[...])
            bias = jnp.where(allow, 0.0, MASKED)
            for head in range(HEADS):
                columns = slice((head // 2) * 128, (head // 2 + 1) * 128)
                scores = lax.dot_general(
                    k_ref[here, columns],
                    q_masked[head],
                    (((1,), (1,)), ((), ())),
                    preferred_element_type=jnp.float32,
                )
                chances = jnp.exp(scores + bias - log_ref[head : head + 1, :])
                grads = lax.dot_general(
                    v_ref[here, columns],
                    g_masked[head],
                    (((1,), (1,)), ((), ())),
                    preferred_element_type=jnp.float32,
                )
                slopes = (chances * (grads - delta_ref[head : head + 1, :])).astype(jnp.bfloat16)
                dk_sum[here, columns] += jnp.dot(
                    slopes, q_masked[head], preferred_element_type=jnp.float32
                )
                dv_sum[here, columns] += jnp.dot(
                    chances.astype(jnp.bfloat16), g_masked[head], preferred_element_type=jnp.float32
                )
                dq_sum[head * HD : (head + 1) * HD, :] += jnp.dot(
                    turned_ref[head * HD : (head + 1) * HD, here],
                    slopes,
                    preferred_element_type=jnp.float32,
                )

        return carry

    lax.fori_loop(0, chunks, one_chunk, 0)
    dq_ref[...] = (dq_sum[...] * SCALE).T.astype(jnp.bfloat16)

    @pl.when(step == pl.num_programs(0) - 1)
    def _():
        for place, pair_ref in enumerate(pair_refs):
            size = pair_ref.shape[0]
            lines = slice(place * size, (place + 1) * size)
            pair_ref[:, :WIDTH] = dk_sum[lines, :].astype(jnp.bfloat16)
            pair_ref[:, WIDTH:] = dv_sum[lines, :].astype(jnp.bfloat16)


def attend_backward(
    queries, keys, values, grads, logs, exact, low, high, key_ids, flags, block, chunk, splits
):
    count, depth = queries[0].shape[0], keys[0].shape[0]
    whole = functools.partial(pl.BlockSpec, pipeline_mode=pl.Buffered(1))
    return pl.pallas_call(
        functools.partial(backward_kernel, chunk),
        grid_spec=pltpu.PrefetchScalarGridSpec(
            num_scalar_prefetch=1,
            grid=(count // block,),
            in_specs=[
                pl.BlockSpec((block, WIDTH), lambda i, f, c=queries[1]: (i, c)),
                whole((depth, WIDTH), lambda i, f, c=keys[1]: (0, c)),
                whole((depth, WIDTH), lambda i, f, c=values[1]: (0, c)),
                pl.BlockSpec((block, WIDTH), lambda i, f: (i, 0)),
                pl.BlockSpec((8, block), lambda i, f: (0, i)),
                pl.BlockSpec((block, WIDTH), lambda i, f: (i, 0)),
                pl.BlockSpec((1, block), lambda i, f: (0, i)),
                pl.BlockSpec((1, block), lambda i, f: (0, i)),
                whole((depth, 1), lambda i, f: (0, 0)),
            ],
            out_specs=[
                pl.BlockSpec((block, WIDTH), lambda i, f: (i, 0)),
            ]
            + [whole((depth // splits, 2 * WIDTH), lambda i, f: (0, 0))] * splits,
            scratch_shapes=[
                pltpu.VMEM((HEADS, block, 128), jnp.bfloat16),
                pltpu.VMEM((HEADS, block, 128), jnp.bfloat16),
                pltpu.VMEM((8, block), jnp.float32),
                pltpu.VMEM((WIDTH, depth), jnp.bfloat16),
                pltpu.VMEM((WIDTH, block), jnp.float32),
                pltpu.VMEM((depth, WIDTH), jnp.float32),
                pltpu.VMEM((depth, WIDTH), jnp.float32),
            ],
        ),
        out_shape=[
            jax.ShapeDtypeStruct((count, WIDTH), jnp.bfloat16),
        ]
        + [jax.ShapeDtypeStruct((depth // splits, 2 * WIDTH), jnp.bfloat16)] * splits,
        compiler_params=pltpu.CompilerParams(vmem_limit_bytes=VMEM_LIMIT),
        cost_estimate=COST,
    )(
        flags.reshape(-1), queries[0], keys[0], values[0], grads, logs, exact, low[None, :],
        high[None, :], key_ids[:, None],
    )


def needed_chunks(low, high, key_ids, block, chunk):
    first = jnp.min(low.reshape(-1, block), 1)[:, None]
    last = jnp.max(high.reshape(-1, block), 1)[:, None]
    smallest = jnp.min(key_ids.reshape(-1, chunk), 1)[None, :]
    largest = jnp.max(key_ids.reshape(-1, chunk), 1)[None, :]
    return ((largest >= first) & (smallest <= last)).astype(jnp.int32)


def on_device(
    count,
    tokens,
    encoder,
    seq_lengths,
    slot_ids,
    enc_lengths,
    cotangent,
    self_in,
    self_out,
    cross_query,
    cross_pair,
    cross_out,
    feed_up,
    feed_down,
    vectors,
    feed_bias,
    self_bias,
):

    full_self_in = fetch(self_in)
    facts = jnp.concatenate([slot_ids[0], seq_lengths[0], enc_lengths[0]], 1)
    slots = slot_ids.shape[2]
    facts_one, facts_two = to_packs(facts)
    tokens_in = jnp.concatenate(to_packs(tokens), 0)
    small = jnp.concatenate([vectors.T, feed_bias.reshape(D // 4, 4).T, self_bias[None, :]], 0)
    full_small = lax.all_gather(small, ("x", "core"), axis=1, tiled=True)
    vec = full_small[:12].astype(jnp.float32)
    bias_row = full_small[12:16].T.reshape(4 * D).astype(jnp.float32)
    self_bias_row = full_small[16].astype(jnp.float32)
    zero_row = jnp.zeros((D,), jnp.float32)
    facts_one, (self_out, cross_query) = chain(facts_one, (self_out, cross_query))
    full_out_query = fetch(jnp.concatenate([self_out, cross_query], 1))
    encoder_in = jnp.concatenate(to_packs(encoder), 0)
    tokens_in, (cross_pair, cross_out) = chain(tokens_in, (cross_pair, cross_out))
    full_cross_pair = fetch(cross_pair)
    full_cross_out = fetch(cross_out)

    lengths = facts_one[slots : slots + NSEQ]
    limits = facts_one[slots + NSEQ : slots + 2 * NSEQ]
    own_ids = jnp.concatenate([facts_one[:slots], facts_two[:slots]])
    ids = lax.all_gather(own_ids, GROUP, axis=0, tiled=True)
    ends = jnp.cumsum(lengths)
    key_ids = gather_sequence(ids, count)
    rank = jnp.sum((ids[None, :] < ids[:, None]).astype(jnp.int32), 1)
    places = jnp.arange(ids.shape[0], dtype=jnp.int32)
    sorted_ids = jnp.sum(jnp.where(places[:, None] == rank[None, :], ids[None, :], 0), 1)
    key_order = gather_sequence(sorted_ids, count)
    seq_of = jnp.sum((sorted_ids[:, None] >= ends[None, :]).astype(jnp.int32), 1)
    starts = jnp.concatenate([jnp.zeros((1,), jnp.int32), ends[:-1]])
    picked = seq_of[:, None] == jnp.arange(NSEQ, dtype=jnp.int32)[None, :]
    self_low = jnp.sum(jnp.where(picked, starts[None, :], 0), 1)
    self_high = sorted_ids
    cross_low = seq_of * ENC
    cross_high = cross_low + jnp.sum(jnp.where(picked, limits[None, :], 0), 1) - 1
    enc_rows = encoder.shape[1]
    micro = lax.axis_index("t") & 1
    enc_ids = []
    for place in range(count):
        index_s = place if count > 1 else 0
        for step in range(MEMBERS):
            core = lax.axis_index("core") ^ (step & 1)
            y_index = lax.axis_index("y") ^ (step >> 1)
            for part in range(2):
                t_index = 2 * core + (micro ^ part)
                row = ((t_index * count + index_s) * PAIR + y_index) * enc_rows
                enc_ids.append(row + jnp.arange(enc_rows, dtype=jnp.int32))
    enc_ids = jnp.concatenate(enc_ids)
    block = 256
    self_chunk, cross_chunk = 256, 384
    self_flags = needed_chunks(self_low, self_high, key_order, block, self_chunk)
    cross_flags = needed_chunks(cross_low, cross_high, enc_ids, block, cross_chunk)

    orders = {
        "x": ("core", "x", "y", "t0", "t1"),
        "y": ("core", "y", "x", "t0", "t1"),
    }

    def relative(matrix, name):
        return relative_columns(matrix, count, orders[name])

    facts_known = (rank, self_flags, cross_flags, key_order, enc_ids, self_low, cross_low, cross_high)
    tokens_in, facts_known = chain(tokens_in, facts_known)
    rank, self_flags, cross_flags, key_order, enc_ids, self_low, cross_low, cross_high = facts_known
    qkv = project_heads(tokens_in, full_self_in, jnp.concatenate([vec[6], zero_row, vec[7]]))
    feed_own = stack_feed(feed_up, feed_down)
    own_heads = sort_rows(to_members(qkv), rank)
    if count > 1:
        pairs = gather_sequence(own_heads[:, WIDTH:], count)
        self_keys, self_values = (pairs, 0), (pairs, 1)
    else:
        self_keys, self_values = (own_heads, 1), (own_heads, 2)
    tokens_x, tokens_y = relative(tokens_in, "x"), relative(tokens_in, "y")
    encoder_x = relative(encoder_in, "x")
    index = relative_index(D, count, orders["y"])
    pick_y = (index[:, None] == jnp.arange(D, dtype=jnp.int32)[None, :]).astype(jnp.bfloat16)
    (tokens_x, tokens_y, encoder_x, pick_y, own_heads), (encoder_in, cotangent) = chain(
        (tokens_x, tokens_y, encoder_x, pick_y, own_heads), (encoder_in, cotangent)
    )
    grad_in = jnp.concatenate(to_packs(cotangent), 0)
    attended_heads, exact_self, log_self = attend_forward(
        (own_heads, 0), self_keys, self_values, self_low, self_high, key_order, self_flags,
        block, self_chunk,
    )
    attended_heads, feed_own = chain(attended_heads, feed_own)
    feed_far = lax.ppermute(feed_own, "x", SWAP)
    enc_pairs = project_blocks(
        encoder_in, full_cross_pair, jnp.concatenate([zero_row, vec[9]])
    )
    attended = to_members(unsort_rows([attended_heads], rank))
    attended, enc_pairs = chain(attended, enc_pairs)
    enc_heads = gather_sequence(jnp.concatenate(exchange(enc_pairs), 0), count)
    normed_one, normed_one_low, unit_one, inverse_one, cross_queries = project_norm(
        by_member(attended), full_out_query, self_bias_row, tokens_in, vec[0], vec[3],
        after=(vec[8],),
    )
    cross_heads = sort_rows(to_members(cross_queries), rank)
    attended_x = relative(as_columns(attended), "x")
    normed_one_x = relative(normed_one_low, "x")
    (attended_x, normed_one_x), cross_heads = chain((attended_x, normed_one_x), cross_heads)
    crossed_heads, exact_cross, log_cross = attend_forward(
        (cross_heads, 0), (enc_heads, 0), (enc_heads, 1), cross_low, cross_high, enc_ids,
        cross_flags, block, cross_chunk,
    )
    cross_heads, feed_own = chain(cross_heads, feed_own)
    feed_near = lax.ppermute(feed_own, "core", SWAP)
    crossed_heads, feed_far = chain(crossed_heads, feed_far)
    feed_shards = [feed_own, feed_near, feed_far, lax.ppermute(feed_far, "core", SWAP)]
    crossed = to_members(unsort_rows([crossed_heads], rank))
    normed_two, normed_two_low, unit_two, inverse_two = project_norm(
        by_member(crossed), full_cross_out, vec[10], normed_one, vec[1], vec[4]
    )
    crossed_x = relative(as_columns(crossed), "x")
    crossed_x, normed_two_low = chain(crossed_x, normed_two_low)
    pre_active, hidden = feed_up_gelu(normed_two_low, feed_shards, bias_row)
    layer_low, grad_three, grad_branch, sums_three = feed_down_norm(
        hidden, feed_shards, vec[11], normed_two, vec[2], vec[5], grad_in
    )
    half = tokens_in.shape[0] // 2

    grad_pre, bias_up, grad_two, grad_crossed_out, sums_two, grad_crossed = feed_back(
        pre_active, feed_shards, grad_branch, grad_three, unit_two, inverse_two, vec[1],
        full_cross_out,
    )
    received, (feed_parts, layer_low) = during_members(
        grad_crossed, lambda layer, *rows: (feed_grads(*rows, count), layer),
        (layer_low, hidden, grad_branch, normed_two_low, grad_pre),
    )
    layer_out = from_packs(layer_low[:half], layer_low[half:])
    feed_sum = reduce_feed(feed_parts)
    grad_crossed_heads = sort_rows(received, rank)
    dq_heads, *enc_pair_grads = attend_backward(
        (cross_heads, 0), (enc_heads, 0), (enc_heads, 1), grad_crossed_heads, log_cross,
        exact_cross, cross_low, cross_high, enc_ids, cross_flags, block, cross_chunk,
        MEMBERS if count == 1 else 1,
    )
    layer_out, dq_heads = chain(layer_out, dq_heads)
    if count > 1:
        enc_pair_grads = cut(scatter_sequence(enc_pair_grads[0], count))
    dq_blocks, (enc_pair_grads,) = during_members(
        unsort_rows([dq_heads], rank), lambda *rest: rest, (enc_pair_grads,)
    )
    enc_blocks = exchange(enc_pair_grads)
    grad_one, grad_attended_out, sums_one, grad_attended = back_norm(
        by_member(dq_blocks), full_out_query, grad_two, unit_one, inverse_one, vec[0]
    )

    def three_side(dq_blocks, *lefts):
        grads = as_columns(dq_blocks)
        return grads, weight_grads(lefts, [grad_attended_out, grads, grad_crossed_out])

    received, (grad_cross_queries, three_parts) = during_members(
        grad_attended, three_side, (dq_blocks, attended_x, normed_one_x, crossed_x)
    )
    three_sum = Halving(three_parts, count, orders["x"])
    grad_attended_heads = sort_rows(received, rank)
    dq_heads, pair_heads = attend_backward(
        (own_heads, 0), self_keys, self_values, grad_attended_heads, log_self, exact_self,
        self_low, self_high, key_order, self_flags, block, self_chunk, 1,
    )
    pair_heads = scatter_sequence(pair_heads, count)
    half_enc = encoder_in.shape[0] // 2

    dq_heads, enc_blocks = chain(dq_heads, enc_blocks)

    def encoder_side(pending, me):
        three_sum.pending = pending
        three_sum.step()
        grads = join_heads(enc_blocks, me)
        parts = weight_grads([encoder_x], [grads])
        return grads, back_project(grads, full_cross_pair), parts, three_sum.sent, three_sum.value

    received, (grad_enc_pairs, grad_enc, pair_parts, three_sum.sent, three_sum.value) = (
        during_members(
            unsort_rows([dq_heads, pair_heads], rank), encoder_side,
            (three_sum.pending, group_index()[None]),
        )
    )
    pair_sum = Halving(pair_parts, count, orders["x"])
    grad_encoder = from_packs(grad_enc[:half_enc], grad_enc[half_enc:])
    grad_qkv = as_columns(received)
    left_parts, right_parts = self_in_grads(
        tokens_x, tokens_y, grad_qkv, pick_y, sums_one, sums_two, sums_three, bias_up,
        grad_cross_queries, grad_enc_pairs,
    )
    left_sum = Halving(left_parts, count, orders["x"])
    right_sum = Halving(right_parts, count, orders["y"])
    (left_sum.sent, right_sum.sent), grad_qkv = chain((left_sum.sent, right_sum.sent), grad_qkv)
    grad_rows = (RESIDUAL * grad_one + back_project(grad_qkv, full_self_in, jnp.float32)).astype(
        jnp.bfloat16
    )
    turn, grad_encoder = chain(right_sum.sent, grad_encoder)
    grad_tokens = from_packs(grad_rows[:half], grad_rows[half:]).astype(jnp.float32)
    for halving in [pair_sum, left_sum, right_sum, three_sum] * 5:
        if halving.order:
            turn, halving.pending = chain(turn, halving.pending)
            halving.step()
            turn = halving.sent
    three, pair = three_sum.finish(), pair_sum.finish()
    left, right = left_sum.finish(), right_sum.finish()
    up_sum, down_sum = split_feed(feed_sum)
    small = right[:, 3 * D // 2 :]
    return (
        layer_out,
        grad_tokens,
        grad_encoder.astype(jnp.float32),
        jnp.concatenate([left, right[:, : 3 * D // 2]], 1),
        three[:, :D],
        three[:, D : 2 * D],
        pair,
        three[:, 2 * D :],
        up_sum,
        down_sum,
        small[:, :12],
        small[:, 13:17].reshape(-1),
        small[:, 12],
    )


def solution(mesh):
    contexts = mesh.shape["ctx"]
    count = contexts // (T_SIZE * PAIR)
    fine = Mesh(
        mesh.devices.reshape(T_SIZE, count, PAIR, PAIR, PAIR), ("t", "s", "y", "x", "core")
    )
    fsdp, ctx = ("x", "core"), ("t", "s", "y")
    in_specs = (
        P(None, ROWS, None),
        P(None, ROWS, None),
        P(fsdp, None, None),
        P(fsdp, None, ctx),
        P(fsdp, None, None),
        P(None, ROWS, None),
        P(fsdp, None),
        P(fsdp, None),
        P(fsdp, None),
        P(fsdp, None),
        P(fsdp, None),
        P(fsdp, None),
        P(fsdp, None),
        P(fsdp, None),
        P(fsdp),
        P(fsdp),
    )
    out_specs = (P(None, ROWS, None),) * 3 + (P(BLOCKS, None),) * 8 + (P(BLOCKS),) * 2
    return jax.shard_map(
        functools.partial(on_device, count),
        mesh=fine,
        in_specs=in_specs,
        out_specs=out_specs,
        check_vma=False,
    )
```

```python
import functools

import jax
import jax.numpy as jnp
from jax import lax
from jax.experimental import pallas as pl
from jax.experimental.pallas import tpu as pltpu
from jax.sharding import Mesh
from jax.sharding import PartitionSpec as P

D = 1024
HD = 64
ENC = 1024
NSEQ = 3
MICRO = 2
DEPTH = 6

EPSILON = 1e-05
MASKED = -1e30
SCALE = HD ** (-0.5)
T_SIZE = 4
PAIR = 2
GROUP = ("y", "core")
ROWS = ("x", "core", "t", "s", "y")
BLOCKS = ("t", "s", "y", "x", "core")
MEMBERS = 4
WIDTH = D // MEMBERS
HEADS = WIDTH // HD
VMEM_LIMIT = 56 * 1024 * 1024
RESIDUAL = (3.0 * DEPTH) ** 0.25
COST = pl.CostEstimate(flops=0, bytes_accessed=0, transcendentals=0)


def norm_forward(resid, gain, offset):
    average = jnp.mean(resid, -1, keepdims=True)
    centered = resid - average
    inverse = lax.rsqrt(jnp.mean(centered * centered, -1, keepdims=True) + EPSILON)
    normed = centered * inverse
    return (normed * gain + offset, normed, inverse)


def norm_backward(grad_out, normed, inverse, gain):
    grad_normed = grad_out * gain
    first_mean = jnp.mean(grad_normed, -1, keepdims=True)
    second_mean = jnp.mean(grad_normed * normed, -1, keepdims=True)
    grad_resid = inverse * (grad_normed - first_mean - normed * second_mean)
    return (grad_resid, jnp.sum(grad_out * normed, 0), jnp.sum(grad_out, 0))


def column_sum(left, right):
    return lax.dot_general(
        left, right, (((0,), (0,)), ((), ())), preferred_element_type=jnp.float32
    )


def input_grad(grad_rows, weight):
    return lax.dot_general(
        grad_rows, weight, (((1,), (1,)), ((), ())), preferred_element_type=jnp.float32
    )


def linear(inputs, weight):
    return jnp.dot(inputs, weight, preferred_element_type=jnp.float32)


def pack_routes():
    straight, crossed = [], []
    for t in range(T_SIZE):
        for core in range(PAIR):
            here = t * PAIR + core
            straight.append((here, (2 * core + (t & 1)) * PAIR + (t >> 1)))
            crossed.append((here, (2 * core + 1 - (t & 1)) * PAIR + (t >> 1)))
    return straight, crossed


def to_packs(parts):
    straight, crossed = pack_routes()
    parity = lax.axis_index("t") & 1
    first = lax.dynamic_index_in_dim(parts, parity, 0, keepdims=False)
    second = lax.dynamic_index_in_dim(parts, 1 - parity, 0, keepdims=False)
    return (
        lax.ppermute(first, ("t", "core"), straight),
        lax.ppermute(second, ("t", "core"), crossed),
    )


def send_back(part, place):
    route = pack_routes()[place]
    return lax.ppermute(part, ("t", "core"), [(to, source) for source, to in route])


def order_back(first, second):
    parity = lax.axis_index("t") & 1
    return jnp.stack(
        [jnp.where(parity == 0, first, second), jnp.where(parity == 0, second, first)], 0
    )


def from_packs(first, second):
    return order_back(send_back(first, 0), send_back(second, 1))


def group_route(step):
    return [(member, member ^ step) for member in range(MEMBERS)]


def group_index():
    return lax.axis_index("y") * PAIR + lax.axis_index("core")


def join_kernel(parts, me_ref, *refs):
    matrix_ref = refs[-1]
    for step, block_ref in enumerate(refs[:-1]):
        for part in range(parts):
            start = pl.multiple_of(part * D + (me_ref[0] ^ step) * WIDTH, WIDTH)
            matrix_ref[:, pl.ds(start, WIDTH)] = block_ref[:, part * WIDTH : (part + 1) * WIDTH]


def join_members_kernel(blocks_ref, matrix_ref):
    rows = matrix_ref.shape[0]
    for member in range(MEMBERS):
        for part in range(matrix_ref.shape[1] // D):
            start = part * D + member * WIDTH
            matrix_ref[:, start : start + WIDTH] = blocks_ref[
                member * rows : (member + 1) * rows, part * WIDTH : (part + 1) * WIDTH
            ]


def in_vmem(count):
    return [pl.BlockSpec(memory_space=pltpu.VMEM)] * count


def small_kernel(body, scalars, operands, outs, work=0):
    return pl.pallas_call(
        body,
        in_specs=[pl.BlockSpec(memory_space=pltpu.SMEM)] * len(scalars) + in_vmem(len(operands)),
        out_specs=in_vmem(len(outs)),
        out_shape=outs,
        compiler_params=pltpu.CompilerParams(vmem_limit_bytes=VMEM_LIMIT),
        cost_estimate=COST,
    )(*scalars, *operands)


def fetch(weight):
    return lax.all_gather(weight, ("x", "core"), axis=0, tiled=True)


SWAP = [(0, 1), (1, 0)]


def stack_feed(up, down):
    return jnp.concatenate([down] + [up[:, part * D : (part + 1) * D] for part in range(4)], 0)


def up_specs(column):
    def block(i, p):
        place = column(i, p)
        return (MEMBERS + place // 2, place % 2)

    return [pl.BlockSpec((D // MEMBERS, FEED_TILE), block)] * MEMBERS


def shard_index():
    return (lax.axis_index("x") * PAIR + lax.axis_index("core"))[None]


def product(rows_ref, weight_ref, start=0, width=None):
    columns = slice(start, weight_ref.shape[1] if width is None else start + width)
    if len(rows_ref.shape) == 2:
        return linear(rows_ref[...], weight_ref[:, columns])
    total = None
    for member in range(MEMBERS):
        lines = slice(member * WIDTH, (member + 1) * WIDTH)
        term = linear(rows_ref[member], weight_ref[lines, columns])
        total = term if total is None else total + term
    return total


def back_product(grads_ref, weight_ref, lines=slice(None), offset=0):
    if len(grads_ref.shape) == 2:
        return input_grad(
            grads_ref[...], weight_ref[lines, offset : offset + grads_ref.shape[1]]
        )
    total = None
    for member in range(MEMBERS):
        columns = slice(offset + member * WIDTH, offset + (member + 1) * WIDTH)
        term = input_grad(grads_ref[member], weight_ref[lines, columns])
        total = term if total is None else total + term
    return total


def put_heads(rows_ref, weight_ref, bias_ref, out_ref, offset=0):
    count = out_ref.shape[0] // MEMBERS
    for member in range(MEMBERS):
        for part in range(out_ref.shape[1] // WIDTH):
            start = part * D + member * WIDTH
            value = product(rows_ref, weight_ref, offset + start, WIDTH)
            value = value + bias_ref[:, start : start + WIDTH]
            out_ref[
                member * count : (member + 1) * count, part * WIDTH : (part + 1) * WIDTH
            ] = value.astype(jnp.bfloat16)


def put_back_heads(grads_ref, weight_ref, out_ref):
    count = out_ref.shape[0] // MEMBERS
    for member in range(MEMBERS):
        value = back_product(grads_ref, weight_ref, slice(member * WIDTH, (member + 1) * WIDTH))
        out_ref[member * count : (member + 1) * count, :] = value.astype(jnp.bfloat16)


def heads_kernel(rows_ref, weight_ref, bias_ref, out_ref):
    put_heads(rows_ref, weight_ref, bias_ref, out_ref)


def project_heads(rows, weight, bias):
    shape = jax.ShapeDtypeStruct((rows.shape[0] * MEMBERS, weight.shape[1] // MEMBERS), jnp.bfloat16)
    return small_kernel(heads_kernel, [], [rows, weight, bias[None, :]], [shape])[0]


def own_heads_kernel(me_ref, rows_ref, weight_ref, bias_ref, *outs):
    for step, out_ref in reversed(list(enumerate(outs))):
        for part in range(out_ref.shape[1] // WIDTH):
            start = pl.multiple_of(part * D + (me_ref[0] ^ step) * WIDTH, WIDTH)
            value = linear(rows_ref[...], weight_ref[:, pl.ds(start, WIDTH)])
            value = value + bias_ref[:, pl.ds(start, WIDTH)]
            out_ref[:, part * WIDTH : (part + 1) * WIDTH] = value.astype(jnp.bfloat16)


def project_blocks(rows, weight, bias):
    shape = jax.ShapeDtypeStruct((rows.shape[0], weight.shape[1] // MEMBERS), jnp.bfloat16)
    work = 2 * rows.shape[0] * weight.size
    return small_kernel(
        own_heads_kernel, [group_index()[None]], [rows, weight, bias[None, :]], [shape] * MEMBERS,
        work,
    )


def norm_kernel(
    rows_ref, weight_ref, bias_ref, base_ref, gain_ref, offset_ref, *refs
):
    outs = refs if len(refs) == 4 else refs[1:]
    resid = (
        RESIDUAL * base_ref[...].astype(jnp.float32)
        + product(rows_ref, weight_ref, 0, D)
        + bias_ref[...]
    )
    normed, unit, inverse = norm_forward(resid, gain_ref[...], offset_ref[...])
    outs[0][...] = normed
    outs[1][...] = normed.astype(jnp.bfloat16)
    outs[2][...] = unit
    outs[3][...] = inverse
    if len(refs) > 4:
        put_heads(outs[1], weight_ref, refs[0], outs[4], D)


def project_norm(rows, weight, bias, base, gain, offset, after=()):
    count = base.shape[0]
    outs = [
        jax.ShapeDtypeStruct((count, D), jnp.float32),
        jax.ShapeDtypeStruct((count, D), jnp.bfloat16),
        jax.ShapeDtypeStruct((count, D), jnp.float32),
        jax.ShapeDtypeStruct((count, 1), jnp.float32),
    ]
    if after:
        outs.append(jax.ShapeDtypeStruct((count * MEMBERS, WIDTH), jnp.bfloat16))
    return small_kernel(
        norm_kernel, [],
        [rows, weight, bias[None, :], base, gain[None, :], offset[None, :]]
        + [row[None, :] for row in after],
        outs,
    )


FEED_TILE = 512


def feed_column(step, me, tiles):
    return (me ^ (step // tiles)) * tiles + step % tiles


def up_kernel(me_ref, rows_ref, *refs):
    shards, (bias_ref, slope_ref, hidden_ref) = refs[:MEMBERS], refs[MEMBERS:]
    depth = shards[0].shape[0]
    active = bias_ref[...]
    for index, shard in enumerate(shards):
        start = pl.multiple_of((me_ref[0] ^ index) * depth, depth)
        active = active + linear(rows_ref[:, pl.ds(start, depth)], shard[...])
    cumulative = 0.5 * (1.0 + lax.erf(active * 0.7071067811865476))
    density = jnp.exp(-0.5 * active * active) * 0.3989422804014327
    slope_ref[...] = cumulative + active * density
    hidden_ref[...] = (active * cumulative).astype(jnp.bfloat16)


def feed_up_gelu(rows, shards, bias):
    count, width = rows.shape[0], 4 * D
    column = lambda i, p: (0, i)
    return pl.pallas_call(
        up_kernel,
        grid_spec=pltpu.PrefetchScalarGridSpec(
            num_scalar_prefetch=1,
            grid=(width // FEED_TILE,),
            in_specs=[pl.BlockSpec((count, D), lambda i, p: (0, 0))]
            + up_specs(lambda i, p: i)
            + [pl.BlockSpec((1, FEED_TILE), column)],
            out_specs=[pl.BlockSpec((count, FEED_TILE), column)] * 2,
        ),
        out_shape=[
            jax.ShapeDtypeStruct((count, width), jnp.float32),
            jax.ShapeDtypeStruct((count, width), jnp.bfloat16),
        ],
        compiler_params=pltpu.CompilerParams(vmem_limit_bytes=VMEM_LIMIT),
        cost_estimate=COST,
    )(shard_index(), rows, *shards, bias[None, :])


def put_norm_back(grads, unit, inverse, gain, resid_ref, low_ref, sums_ref):
    resid, gain_sum, offset_sum = norm_backward(grads, unit, inverse, gain)
    low = resid.astype(jnp.bfloat16)
    resid_ref[...] = resid
    low_ref[...] = low
    sums_ref[0:1, :] = gain_sum[None, :]
    sums_ref[1:2, :] = offset_sum[None, :]
    sums_ref[2:3, :] = jnp.sum(low.astype(jnp.float32), 0)[None, :]
    sums_ref[3:8, :] = jnp.zeros((5, D), jnp.float32)


def down_kernel(tiles, me_ref, hidden_ref, *refs):
    shards = refs[:MEMBERS]
    bias_ref, base_ref, gain_ref, offset_ref, grads_ref = refs[MEMBERS : MEMBERS + 5]
    layer_ref, resid_ref, low_ref, sums_ref, total_ref = refs[MEMBERS + 5 :]
    step = pl.program_id(0)

    @pl.when(step == 0)
    def _():
        total_ref[...] = RESIDUAL * base_ref[...] + bias_ref[...]

    for index, shard in enumerate(shards):

        @pl.when(step // tiles == index)
        def _(shard=shard):
            total_ref[...] += linear(hidden_ref[...], shard[...])

    @pl.when(step == pl.num_programs(0) - 1)
    def _():
        layer, unit, inverse = norm_forward(total_ref[...], gain_ref[...], offset_ref[...])
        layer_ref[...] = layer.astype(jnp.bfloat16)
        put_norm_back(
            grads_ref[...].astype(jnp.float32), unit, inverse, gain_ref[...], resid_ref, low_ref,
            sums_ref,
        )


def one_block(array):
    return pl.BlockSpec(array.shape, lambda i, p: (0,) * len(array.shape))


def down_specs(tiles):
    return [
        pl.BlockSpec((FEED_TILE, D), lambda i, p, s=s: (jnp.clip(i - s * tiles, 0, tiles - 1), 0))
        for s in range(MEMBERS)
    ]


def feed_down_norm(hidden, shards, bias, base, gain, offset, grads):
    count = base.shape[0]
    tiles = D // FEED_TILE
    fixed = [bias[None, :], base, gain[None, :], offset[None, :], grads]
    outs = [
        jax.ShapeDtypeStruct((count, D), jnp.bfloat16),
        jax.ShapeDtypeStruct((count, D), jnp.float32),
        jax.ShapeDtypeStruct((count, D), jnp.bfloat16),
        jax.ShapeDtypeStruct((8, D), jnp.float32),
    ]
    return pl.pallas_call(
        functools.partial(down_kernel, tiles),
        grid_spec=pltpu.PrefetchScalarGridSpec(
            num_scalar_prefetch=1,
            grid=(MEMBERS * tiles,),
            in_specs=[
                pl.BlockSpec((count, FEED_TILE), lambda i, p: (0, feed_column(i, p[0], tiles)))
            ]
            + down_specs(tiles)
            + [one_block(array) for array in fixed],
            out_specs=[one_block(out) for out in outs],
            scratch_shapes=[pltpu.VMEM((count, D), jnp.float32)],
        ),
        out_shape=outs,
        compiler_params=pltpu.CompilerParams(vmem_limit_bytes=VMEM_LIMIT),
        cost_estimate=COST,
    )(shard_index(), hidden, *shards, *fixed)


def feed_back_kernel(tiles, me_ref, slope_ref, *refs):
    downs, ups, refs = refs[:MEMBERS], refs[MEMBERS : 2 * MEMBERS], refs[2 * MEMBERS :]
    grads_ref, resid_ref, unit_ref, inverse_ref, gain_ref, out_ref = refs[:6]
    du_ref, bias_ref, next_resid_ref, next_low_ref, sums_ref, heads_ref, total_ref = refs[6:]
    step = pl.program_id(0)
    depth = ups[0].shape[0]

    @pl.when(step == 0)
    def _():
        total_ref[...] = RESIDUAL * resid_ref[...]

    slope = slope_ref[...]
    for index, shard in enumerate(downs):

        @pl.when(step // tiles == index)
        def _(shard=shard):
            du_ref[...] = (back_product(grads_ref, shard) * slope).astype(jnp.bfloat16)

    du = du_ref[...]
    bias_ref[...] = jnp.sum(du.astype(jnp.float32), 0, keepdims=True)
    for index, shard in enumerate(ups):
        start = pl.multiple_of((me_ref[0] ^ index) * depth, depth)
        total_ref[:, pl.ds(start, depth)] += input_grad(du, shard[...])

    @pl.when(step == pl.num_programs(0) - 1)
    def _():
        put_norm_back(
            total_ref[...], unit_ref[...], inverse_ref[...], gain_ref[...], next_resid_ref,
            next_low_ref, sums_ref,
        )
        put_back_heads(next_low_ref, out_ref, heads_ref)


def feed_back(slope, shards, grads, resid, unit, inverse, gain, out_weight):
    count, width = slope.shape
    tiles = D // FEED_TILE
    fixed = [grads, resid, unit, inverse, gain[None, :], out_weight]
    column = lambda i, p: (0, feed_column(i, p[0], tiles))
    outs = [
        jax.ShapeDtypeStruct((count, width), jnp.bfloat16),
        jax.ShapeDtypeStruct((1, width), jnp.float32),
        jax.ShapeDtypeStruct((count, D), jnp.float32),
        jax.ShapeDtypeStruct((count, D), jnp.bfloat16),
        jax.ShapeDtypeStruct((8, D), jnp.float32),
        jax.ShapeDtypeStruct((count * MEMBERS, WIDTH), jnp.bfloat16),
    ]
    return pl.pallas_call(
        functools.partial(feed_back_kernel, tiles),
        grid_spec=pltpu.PrefetchScalarGridSpec(
            num_scalar_prefetch=1,
            grid=(MEMBERS * tiles,),
            in_specs=[pl.BlockSpec((count, FEED_TILE), column)]
            + down_specs(tiles)
            + up_specs(lambda i, p: feed_column(i, p[0], tiles))
            + [one_block(array) for array in fixed],
            out_specs=[
                pl.BlockSpec((count, FEED_TILE), column), pl.BlockSpec((1, FEED_TILE), column)
            ]
            + [one_block(out) for out in outs[2:]],
            scratch_shapes=[pltpu.VMEM((count, D), jnp.float32)],
        ),
        out_shape=outs,
        compiler_params=pltpu.CompilerParams(vmem_limit_bytes=VMEM_LIMIT),
        cost_estimate=COST,
    )(shard_index(), slope, *shards, *shards, *fixed)


def norm_back_kernel(
    grads_ref, weight_ref, resid_ref, unit_ref, inverse_ref, gain_ref,
    next_resid_ref, next_low_ref, sums_ref, heads_ref,
):
    total = RESIDUAL * resid_ref[...] + back_product(grads_ref, weight_ref, offset=D)
    put_norm_back(
        total, unit_ref[...], inverse_ref[...], gain_ref[...], next_resid_ref, next_low_ref, sums_ref
    )
    put_back_heads(next_low_ref, weight_ref, heads_ref)


def back_norm(grads, weight, resid, unit, inverse, gain):
    count = resid.shape[0]
    outs = [
        jax.ShapeDtypeStruct((count, D), jnp.float32),
        jax.ShapeDtypeStruct((count, D), jnp.bfloat16),
        jax.ShapeDtypeStruct((8, D), jnp.float32),
        jax.ShapeDtypeStruct((count * MEMBERS, WIDTH), jnp.bfloat16),
    ]
    return small_kernel(
        norm_back_kernel, [], [grads, weight, resid, unit, inverse, gain[None, :]], outs
    )


def back_kernel(grads_ref, weight_ref, resid_ref, out_ref):
    value = RESIDUAL * resid_ref[...] + back_product(grads_ref, weight_ref)
    out_ref[...] = value.astype(out_ref.dtype)


def back_project(grads, weight, resid):
    count, width = grads.shape
    rows = 256
    return pl.pallas_call(
        back_kernel,
        grid=(weight.shape[0] // rows,),
        in_specs=[
            pl.BlockSpec((count, width), lambda i: (0, 0)),
            pl.BlockSpec((rows, width), lambda i: (i, 0)),
            pl.BlockSpec((count, rows), lambda i: (0, i)),
        ],
        out_specs=pl.BlockSpec((count, rows), lambda i: (0, i)),
        out_shape=jax.ShapeDtypeStruct((count, weight.shape[0]), jnp.bfloat16),
        compiler_params=pltpu.CompilerParams(vmem_limit_bytes=VMEM_LIMIT),
        cost_estimate=COST,
    )(grads, weight, resid)


def to_members(blocks):
    return lax.all_to_all(blocks, GROUP, 0, 0, tiled=True)


def by_member(blocks):
    return blocks.reshape(MEMBERS, blocks.shape[0] // MEMBERS, blocks.shape[1])


def as_columns(blocks):
    shape = (blocks.shape[0] // MEMBERS, blocks.shape[1] * MEMBERS)
    return small_kernel(
        join_members_kernel, [], [blocks], [jax.ShapeDtypeStruct(shape, blocks.dtype)]
    )[0]


def chain(first, second):
    return lax.optimization_barrier((first, second))


def exchange(blocks):
    return [
        block if step == 0 else lax.ppermute(block, GROUP, group_route(step))
        for step, block in enumerate(blocks)
    ]


def during(blocks, work, inputs):
    own, inputs = chain(blocks[0], inputs)
    results, received = chain(work(*inputs), exchange(blocks)[1:])
    return [own, *received], results


def during_members(blocks, work, inputs):
    blocks, inputs = chain(blocks, inputs)
    results, received = chain(work(*inputs), to_members(blocks))
    return received, results


def cut(matrix):
    rows = matrix.shape[0] // MEMBERS
    return [matrix[step * rows : (step + 1) * rows] for step in range(MEMBERS)]


def sort_kernel(rank_ref, blocks_ref, sorted_ref):
    rows = blocks_ref.shape[0] // MEMBERS
    for place in range(MEMBERS):
        wanted = lax.broadcasted_iota(jnp.int32, (rows, rows * MEMBERS), 0) + place * rows
        pick = (rank_ref[...] == wanted).astype(jnp.bfloat16)
        sorted_ref[place * rows : (place + 1) * rows, :] = linear(pick, blocks_ref[...]).astype(
            jnp.bfloat16
        )


def put_unsorted(ranks, parts, block_ref, lines):
    rows = ranks.shape[0]
    wanted = lax.broadcasted_iota(jnp.int32, (rows, rows * MEMBERS), 1)
    pick = (ranks == wanted).astype(jnp.bfloat16)
    start = 0
    for sorted_ref in parts:
        end = start + sorted_ref.shape[1]
        block_ref[lines, start:end] = linear(pick, sorted_ref[...]).astype(jnp.bfloat16)
        start = end


def unsort_kernel(rank_ref, *refs):
    blocks_ref = refs[-1]
    rows = blocks_ref.shape[0] // MEMBERS
    for member in range(MEMBERS):
        lines = slice(member * rows, (member + 1) * rows)
        put_unsorted(rank_ref[lines, :], refs[:-1], blocks_ref, lines)


def unsort_blocks_kernel(me_ref, rank_ref, *refs):
    for step, block_ref in enumerate(refs[-MEMBERS:]):
        rows = block_ref.shape[0]
        start = pl.multiple_of((me_ref[0] ^ step) * rows, rows)
        put_unsorted(rank_ref[pl.ds(start, rows), :], refs[:-MEMBERS], block_ref, slice(None))


def unsort_blocks(parts, rank):
    rows, width = parts[0].shape[0] // MEMBERS, sum(part.shape[1] for part in parts)
    shape = jax.ShapeDtypeStruct((rows, width), jnp.bfloat16)
    return small_kernel(
        unsort_blocks_kernel, [group_index()[None]], [rank[:, None], *parts], [shape] * MEMBERS
    )


def sort_rows(blocks, rank):
    shape = jax.ShapeDtypeStruct(blocks.shape, jnp.bfloat16)
    work = 2 * blocks.size * blocks.shape[0]
    return small_kernel(sort_kernel, [], [rank[None, :], blocks], [shape], work)[0]


def unsort_rows(parts, rank):
    width = sum(part.shape[1] for part in parts)
    shape = jax.ShapeDtypeStruct((parts[0].shape[0], width), jnp.bfloat16)
    work = 2 * shape.size * shape.shape[0]
    return small_kernel(unsort_kernel, [], [rank[:, None], *parts], [shape], work)[0]


def assemble_kernel(places_ref, *refs):
    blocks, whole_ref = refs[:-1], refs[-1]
    for place, block_ref in enumerate(blocks):
        size = block_ref.shape[0] // 2
        for half in range(2):
            start = pl.multiple_of(places_ref[2 * place + half], 128)
            whole_ref[pl.ds(start, size), :] = block_ref[half * size : (half + 1) * size, :]


def assemble(blocks, places):
    shape = jax.ShapeDtypeStruct((len(blocks) * blocks[0].shape[0], blocks[0].shape[1]), jnp.bfloat16)
    return small_kernel(assemble_kernel, [places], blocks, [shape])[0]


def gather_sequence(matrix, count):
    if count == 1:
        return matrix
    return lax.all_gather(matrix, "s", axis=0, tiled=True)


def scatter_sequence(matrix, count):
    if count == 1:
        return matrix
    return lax.psum_scatter(matrix, "s", scatter_dimension=0, tiled=True)


def own_bits():
    t_index = lax.axis_index("t")
    return {
        "t1": t_index >> 1,
        "t0": t_index & 1,
        "y": lax.axis_index("y"),
        "x": lax.axis_index("x"),
        "core": lax.axis_index("core"),
    }


def flip(block, name):
    if name in ("t1", "t0"):
        step = 2 if name == "t1" else 1
        return lax.ppermute(block, "t", [(i, i ^ step) for i in range(T_SIZE)])
    return lax.ppermute(block, name, [(i, i ^ 1) for i in range(PAIR)])


def relative_index(total, count, order):
    rows = total // (32 * count)
    place = jnp.arange(total, dtype=jnp.int32)
    bits, mine = {"r": place % rows, "s": place // rows % count}, own_bits()
    for index, name in enumerate(order):
        bits[name] = (place // (rows * count) >> (len(order) - 1 - index) & 1) ^ mine[name]
    row = (bits["t1"] * PAIR + bits["t0"]) * count + bits["s"]
    for name in ("y", "x", "core"):
        row = row * PAIR + bits[name]
    return row * rows + bits["r"]


def relative_columns(matrix, count, order):
    index = relative_index(matrix.shape[1], count, order)
    pick = jnp.arange(matrix.shape[1], dtype=jnp.int32)[:, None] == index[None, :]
    return linear(matrix, pick.astype(jnp.bfloat16)).astype(jnp.bfloat16)


def put_grads(pairs, outs):
    half, start = outs[0].shape[0], 0
    for left_ref, right in pairs:
        end = start + right.shape[1]
        for out_ref, lines in zip(outs, (slice(half, 2 * half), slice(0, half))):
            value = column_sum(left_ref[:, lines], right)
            out_ref[:, start:end] = value.astype(jnp.bfloat16)
        start = end
    return start


def total_rows(rows):
    return jnp.sum(rows.astype(jnp.float32), 0, keepdims=True)


def three_kernel(
    out_left, query_left, cross_left, out_grads, query_blocks, cross_grads,
    sent_ref, kept_ref, sums_ref, columns_ref,
):
    rows = columns_ref.shape[0]
    for member in range(MEMBERS):
        columns_ref[:, member * WIDTH : (member + 1) * WIDTH] = query_blocks[
            member * rows : (member + 1) * rows, :
        ]
    pairs = [(out_left, out_grads), (query_left, columns_ref), (cross_left, cross_grads)]
    put_grads([(left, right[...]) for left, right in pairs], [sent_ref, kept_ref])
    sums_ref[...] = total_rows(columns_ref[...])


def three_grads(out_left, query_left, cross_left, out_grads, query_blocks, cross_grads):
    operands = [out_left, query_left, cross_left, out_grads, query_blocks, cross_grads]
    return pl.pallas_call(
        three_kernel,
        in_specs=in_vmem(6),
        out_specs=in_vmem(3),
        out_shape=[jax.ShapeDtypeStruct((D // 2, 3 * D), jnp.bfloat16)] * 2
        + [jax.ShapeDtypeStruct((1, D), jnp.float32)],
        scratch_shapes=[pltpu.VMEM(out_grads.shape, jnp.bfloat16)],
        compiler_params=pltpu.CompilerParams(vmem_limit_bytes=VMEM_LIMIT),
        cost_estimate=COST,
    )(*operands)


def encoder_kernel(
    me_ref, left_ref, weight_ref, *refs
):
    blocks, refs = refs[:MEMBERS], refs[MEMBERS:]
    sent_ref, kept_ref, first_ref, second_ref, sums_ref, grads_ref = refs
    join_kernel(2, me_ref, *blocks, grads_ref)
    put_grads([(left_ref, grads_ref[...])], [sent_ref, kept_ref])
    half = first_ref.shape[0]
    first_ref[...] = input_grad(grads_ref[:half, :], weight_ref[...]).astype(jnp.bfloat16)
    second_ref[...] = input_grad(grads_ref[half:, :], weight_ref[...]).astype(jnp.bfloat16)
    sums_ref[...] = total_rows(grads_ref[:, D:])


def encoder_grads(me, left, weight, blocks):
    rows = left.shape[0]
    return pl.pallas_call(
        encoder_kernel,
        in_specs=[pl.BlockSpec(memory_space=pltpu.SMEM)] + in_vmem(2 + MEMBERS),
        out_specs=in_vmem(5),
        out_shape=[jax.ShapeDtypeStruct((D // 2, 2 * D), jnp.bfloat16)] * 2
        + [jax.ShapeDtypeStruct((rows // 2, D), jnp.bfloat16)] * 2
        + [jax.ShapeDtypeStruct((1, D), jnp.float32)],
        scratch_shapes=[pltpu.VMEM((rows, 2 * D), jnp.bfloat16)],
        compiler_params=pltpu.CompilerParams(vmem_limit_bytes=VMEM_LIMIT),
        cost_estimate=COST,
    )(me, left, weight, *blocks)


def self_in_kernel(
    me_ref, left_ref, right_ref, pick_ref, one_ref, two_ref, three_ref, up_ref, query_ref,
    value_ref, *refs
):
    blocks, refs = refs[:MEMBERS], refs[MEMBERS:]
    left_sent, left_kept, right_sent, right_kept, grads_ref, small_ref = refs
    join_kernel(3, me_ref, *blocks, grads_ref)
    middle = grads_ref.shape[1] // 2
    put_grads([(left_ref, grads_ref[:, :middle])], [left_sent, left_kept])
    start = put_grads([(right_ref, grads_ref[:, middle:])], [right_sent, right_kept])

    small_ref[...] = jnp.zeros_like(small_ref)
    rows = [one_ref[0:1, :], two_ref[0:1, :], three_ref[0:1, :]]
    rows += [one_ref[1:2, :], two_ref[1:2, :], three_ref[1:2, :]]
    rows += [total_rows(grads_ref[:, :D]), total_rows(grads_ref[:, 2 * D :]), query_ref[...]]
    rows += [value_ref[...], two_ref[2:3, :], three_ref[2:3, :], one_ref[2:3, :]]
    for place, row in enumerate(rows):
        small_ref[place : place + 1, :] = row
    small_ref[13:17, :] = up_ref[...]
    half = right_sent.shape[0]
    low = small_ref[...].astype(jnp.bfloat16)
    for out_ref, lines in ((right_sent, slice(half, 2 * half)), (right_kept, slice(0, half))):
        out_ref[:, start:] = input_grad(pick_ref[lines, :], low).astype(jnp.bfloat16)


def self_in_grads(me, left, right, pick, one, two, three, up, query, value, blocks):
    rows = left.shape[0]
    half, middle = D // 2, 3 * D // 2
    outs = [jax.ShapeDtypeStruct((half, middle), jnp.bfloat16)] * 2
    outs += [jax.ShapeDtypeStruct((half, middle + 128), jnp.bfloat16)] * 2
    outs += [jax.ShapeDtypeStruct((rows, 3 * D), jnp.bfloat16)]
    operands = [left, right, pick, one, two, three, up.reshape(D, 4).T, query, value, *blocks]
    results = pl.pallas_call(
        self_in_kernel,
        in_specs=[pl.BlockSpec(memory_space=pltpu.SMEM)] + in_vmem(len(operands)),
        out_specs=in_vmem(len(outs)),
        out_shape=outs,
        scratch_shapes=[pltpu.VMEM((128, D), jnp.float32)],
        compiler_params=pltpu.CompilerParams(vmem_limit_bytes=VMEM_LIMIT),
        cost_estimate=COST,
    )(me, *operands)
    return results[:2], results[2:4], results[4]


class Halving:
    def __init__(self, parts, count, order):
        sent, self.value = parts
        self.count, self.order = count, list(order)
        self.send(sent)

    def send(self, block):
        self.sent = block.astype(jnp.bfloat16)
        self.pending = flip(self.sent, self.order.pop(0))

    def step(self):
        total = self.value.astype(jnp.float32) + self.pending.astype(jnp.float32)
        half = total.shape[0] // 2
        self.value = total[:half]
        self.send(total[half:])

    def finish(self):
        total = self.value + self.pending.astype(jnp.float32)
        if self.count > 1:
            total = lax.psum_scatter(
                total.astype(jnp.bfloat16), "s", scatter_dimension=0, tiled=True
            ).astype(jnp.float32)
        return total


def feed_grads_kernel(hidden_ref, grads_ref, rows_ref, active_grads_ref, out_ref):
    others, _, _, rows, _ = out_ref.shape

    @pl.when(pl.program_id(0) == 0)
    def _():
        value = column_sum(hidden_ref[...], grads_ref[...]).astype(jnp.bfloat16)
        value = value.reshape(PAIR, others, 4, rows, D)
        for y_index in range(PAIR):
            out_ref[:, y_index] = value[y_index]

    @pl.when(pl.program_id(0) == 1)
    def _():
        for part in range(4):
            value = column_sum(rows_ref[...], active_grads_ref[:, part * D : (part + 1) * D])
            value = value.astype(jnp.bfloat16).reshape(PAIR, others, rows, D)
            for y_index in range(PAIR):
                out_ref[:, y_index, part] = value[y_index]


def feed_grads(hidden, grads, rows, active_grads, count):
    blocks = 32 * count
    lines = D // blocks
    size = rows.shape[0]
    if count > 1:
        parts = [column_sum(hidden, grads).astype(jnp.bfloat16).reshape(-1, PAIR, 4, 4, lines, D)]
        for part in range(4):
            up = column_sum(rows, active_grads[:, part * D : (part + 1) * D])
            parts.append(up.astype(jnp.bfloat16).reshape(-1, PAIR, 4, 1, lines, D))
        return jnp.swapaxes(jnp.concatenate(parts, 3), 1, 2).reshape(-1, PAIR, 8, lines, D)
    return pl.pallas_call(
        feed_grads_kernel,
        grid=(2, T_SIZE),
        in_specs=[
            pl.BlockSpec((size, D), lambda p, i: (0, jnp.where(p == 0, i, T_SIZE - 1))),
            pl.BlockSpec((size, D), lambda p, i: (0, 0)),
            pl.BlockSpec((size, D // T_SIZE), lambda p, i: (0, jnp.where(p == 0, 0, i))),
            pl.BlockSpec((size, 4 * D), lambda p, i: (0, 0)),
        ],
        out_specs=pl.BlockSpec((4, PAIR, 4, lines, D), lambda p, i: (i, 0, p, 0, 0)),
        out_shape=jax.ShapeDtypeStruct((blocks // PAIR, PAIR, 8, lines, D), jnp.bfloat16),
        compiler_params=pltpu.CompilerParams(vmem_limit_bytes=VMEM_LIMIT),
        cost_estimate=COST,
    )(hidden, grads, rows, active_grads)


def reduce_feed(parts):
    return lax.psum_scatter(parts, ("t", "s", "x", "core"), scatter_dimension=0, tiled=True)[0]


def split_feed(halves):
    mine = lax.axis_index("y")
    return [
        lax.dynamic_index_in_dim(halves, place, 0, keepdims=False) for place in (mine, 1 - mine)
    ]


def merge_feed(kept, arrived):
    total = kept.astype(jnp.float32) + arrived.astype(jnp.float32)
    return jnp.concatenate([total[4 + part] for part in range(4)], 1), total[:4].reshape(-1, D)


def forward_kernel(
    chunk, flags_ref, q_ref, k_ref, v_ref, low_ref, high_ref, key_ref, out_ref, exact_ref, log_ref,
    masked_ref, top_ref, sum_ref, fade_ref, total_ref,
):
    step = pl.program_id(0)
    chunks = k_ref.shape[0] // chunk
    rows = q_ref.shape[0]
    lane = lax.broadcasted_iota(jnp.int32, (rows, 128), 1)
    for head in range(HEADS):
        pair = q_ref[:, (head // 2) * 128 : (head // 2 + 1) * 128] * SCALE
        masked_ref[head] = jnp.where((lane >= HD) == (head % 2 == 1), pair, 0).astype(jnp.bfloat16)
    top_ref[...] = jnp.full_like(top_ref, MASKED)
    sum_ref[...] = jnp.ones_like(sum_ref)
    sum_ref[:HEADS, :] = jnp.zeros((HEADS, rows), jnp.float32)
    fade_ref[...] = jnp.zeros_like(fade_ref)
    total_ref[...] = jnp.zeros_like(total_ref)

    def one_chunk(index, carry):
        @pl.when(flags_ref[step * chunks + index] != 0)
        def _():
            start = pl.multiple_of(index * chunk, chunk)
            here = pl.ds(start, chunk)
            keys = key_ref[here, :]
            allow = (keys >= low_ref[...]) & (keys <= high_ref[...])
            bias = jnp.where(allow, 0.0, MASKED)
            def pair_of(head):
                return slice((head // 2) * 128, (head // 2 + 1) * 128)

            scores = [
                lax.dot_general(
                    k_ref[here, pair_of(head)],
                    masked_ref[head],
                    (((1,), (1,)), ((), ())),
                    preferred_element_type=jnp.float32,
                ) + bias
                for head in range(HEADS)
            ]
            befores = [top_ref[head : head + 1, :] for head in range(HEADS)]
            afters = [
                jnp.maximum(before, jnp.max(score, 0, keepdims=True))
                for before, score in zip(befores, scores)
            ]
            exponents = [jnp.exp(score - after) for score, after in zip(scores, afters)]
            chances = [exponent.astype(jnp.bfloat16) for exponent in exponents]
            for head in range(HEADS):
                fade = jnp.exp(befores[head] - afters[head])
                top_ref[head : head + 1, :] = afters[head]
                fade_ref[head : head + 1, :] = fade
                sum_ref[head : head + 1, :] = sum_ref[head : head + 1, :] * fade + jnp.sum(
                    exponents[head], 0, keepdims=True
                )
            fades = fade_ref[...].T
            for head in range(HEADS):
                columns = slice((head // 2) * 128, (head // 2 + 1) * 128)
                total_ref[head] = total_ref[head] * fades[:, head : head + 1] + column_sum(
                    chances[head], v_ref[here, columns]
                )

        return carry

    lax.fori_loop(0, chunks, one_chunk, 0)
    shares = (1.0 / sum_ref[...]).T
    for head in range(0, HEADS, 2):
        columns = slice((head // 2) * 128, (head // 2 + 1) * 128)
        exact = jnp.where(
            lane < HD,
            total_ref[head] * shares[:, head : head + 1],
            total_ref[head + 1] * shares[:, head + 1 : head + 2],
        )
        exact_ref[:, columns] = exact
        out_ref[:, columns] = exact.astype(jnp.bfloat16)
    log_ref[:HEADS, :] = top_ref[:HEADS, :] + jnp.log(sum_ref[:HEADS, :])
    log_ref[HEADS:, :] = jnp.zeros((8 - HEADS, rows), jnp.float32)


def attend_forward(queries, keys, values, low, high, key_ids, flags, block, chunk):
    count, depth = queries[0].shape[0], keys[0].shape[0]
    whole = functools.partial(pl.BlockSpec, pipeline_mode=pl.Buffered(1))
    return pl.pallas_call(
        functools.partial(forward_kernel, chunk),
        grid_spec=pltpu.PrefetchScalarGridSpec(
            num_scalar_prefetch=1,
            grid=(count // block,),
            in_specs=[
                pl.BlockSpec((block, WIDTH), lambda i, f, c=queries[1]: (i, c)),
                whole((depth, WIDTH), lambda i, f, c=keys[1]: (0, c)),
                whole((depth, WIDTH), lambda i, f, c=values[1]: (0, c)),
                pl.BlockSpec((1, block), lambda i, f: (0, i)),
                pl.BlockSpec((1, block), lambda i, f: (0, i)),
                whole((depth, 1), lambda i, f: (0, 0)),
            ],
            out_specs=[
                pl.BlockSpec((block, WIDTH), lambda i, f: (i, 0)),
                pl.BlockSpec((block, WIDTH), lambda i, f: (i, 0)),
                pl.BlockSpec((8, block), lambda i, f: (0, i)),
            ],
            scratch_shapes=[
                pltpu.VMEM((HEADS, block, 128), jnp.bfloat16),
                pltpu.VMEM((8, block), jnp.float32),
                pltpu.VMEM((8, block), jnp.float32),
                pltpu.VMEM((8, block), jnp.float32),
                pltpu.VMEM((HEADS, block, 128), jnp.float32),
            ],
        ),
        out_shape=[
            jax.ShapeDtypeStruct((count, WIDTH), jnp.bfloat16),
            jax.ShapeDtypeStruct((count, WIDTH), jnp.float32),
            jax.ShapeDtypeStruct((8, count), jnp.float32),
        ],
        compiler_params=pltpu.CompilerParams(vmem_limit_bytes=VMEM_LIMIT),
        cost_estimate=COST,
    )(
        flags.reshape(-1), queries[0], keys[0], values[0], low[None, :], high[None, :],
        key_ids[:, None],
    )


def backward_kernel(
    chunk, flags_ref, places_ref, q_ref, k_ref, v_ref, g_ref, log_ref, exact_ref, low_ref, high_ref, key_ref,
    dq_ref, *refs,
):
    pair_refs, (q_masked, g_masked, delta_ref, turned_ref, dq_sum, dk_sum, dv_sum) = (
        refs[:-7], refs[-7:]
    )
    step = pl.program_id(0)
    chunks = k_ref.shape[0] // chunk
    rows = q_ref.shape[0]
    lane = lax.broadcasted_iota(jnp.int32, (rows, 128), 1)

    @pl.when(step == 0)
    def _():
        dk_sum[...] = jnp.zeros_like(dk_sum)
        dv_sum[...] = jnp.zeros_like(dv_sum)

        def turn(index, carry):
            start = pl.multiple_of(index * chunk, chunk)
            turned_ref[:, pl.ds(start, chunk)] = k_ref[pl.ds(start, chunk), :].T
            return carry

        lax.fori_loop(0, chunks, turn, 0)

    for head in range(HEADS):
        columns = slice((head // 2) * 128, (head // 2 + 1) * 128)
        chosen = (lane >= HD) == (head % 2 == 1)
        q_masked[head] = jnp.where(chosen, q_ref[:, columns] * SCALE, 0).astype(jnp.bfloat16)
        g_masked[head] = jnp.where(chosen, g_ref[:, columns], 0).astype(jnp.bfloat16)
    dq_sum[...] = jnp.zeros_like(dq_sum)
    members = lax.broadcasted_iota(jnp.int32, (8, WIDTH), 1) // HD
    members = (members == lax.broadcasted_iota(jnp.int32, (8, WIDTH), 0)).astype(jnp.float32)
    delta_ref[...] = lax.dot_general(
        members,
        g_ref[...].astype(jnp.float32) * exact_ref[...],
        (((1,), (1,)), ((), ())),
        precision=lax.Precision.HIGHEST,
        preferred_element_type=jnp.float32,
    )

    def one_chunk(index, carry):
        @pl.when(flags_ref[step * chunks + index] != 0)
        def _():
            start = pl.multiple_of(index * chunk, chunk)
            here = pl.ds(start, chunk)
            keys = key_ref[here, :]
            allow = (keys >= low_ref[...]) & (keys <= high_ref[...])
            bias = jnp.where(allow, 0.0, MASKED)

            def pair_of(head):
                return slice((head // 2) * 128, (head // 2 + 1) * 128)

            def against(keys_ref, head, masked):
                return lax.dot_general(
                    keys_ref[here, pair_of(head)],
                    masked[head],
                    (((1,), (1,)), ((), ())),
                    preferred_element_type=jnp.float32,
                )

            heads = range(HEADS)
            scores = [against(k_ref, head, q_masked) for head in heads]
            grads = [against(v_ref, head, g_masked) for head in heads]
            chances = [
                jnp.exp(scores[head] + bias - log_ref[head : head + 1, :]) for head in heads
            ]
            slopes = [
                (chances[head] * (grads[head] - delta_ref[head : head + 1, :])).astype(jnp.bfloat16)
                for head in heads
            ]
            chances = [chance.astype(jnp.bfloat16) for chance in chances]
            for head in heads:
                dv_sum[here, pair_of(head)] += linear(chances[head], g_masked[head])
            for head in heads:
                dk_sum[here, pair_of(head)] += linear(slopes[head], q_masked[head])
            for head in heads:
                lines = slice(head * HD, (head + 1) * HD)
                dq_sum[lines, :] += linear(turned_ref[lines, here], slopes[head])

        return carry

    lax.fori_loop(0, chunks, one_chunk, 0)
    dq_ref[...] = (dq_sum[...] * SCALE).T.astype(jnp.bfloat16)

    @pl.when(step == pl.num_programs(0) - 1)
    def _():
        for place, pair_ref in enumerate(pair_refs):
            size = pair_ref.shape[0] // 2
            for half in range(2):
                start = pl.multiple_of(places_ref[2 * place + half], 128)
                lines = slice(half * size, (half + 1) * size)
                pair_ref[lines, :WIDTH] = dk_sum[pl.ds(start, size), :].astype(jnp.bfloat16)
                pair_ref[lines, WIDTH:] = dv_sum[pl.ds(start, size), :].astype(jnp.bfloat16)


def attend_backward(
    queries, keys, values, grads, logs, exact, low, high, key_ids, flags, block, chunk, places
):
    splits = places.shape[0] // 2
    count, depth = queries[0].shape[0], keys[0].shape[0]
    whole = functools.partial(pl.BlockSpec, pipeline_mode=pl.Buffered(1))
    return pl.pallas_call(
        functools.partial(backward_kernel, chunk),
        grid_spec=pltpu.PrefetchScalarGridSpec(
            num_scalar_prefetch=2,
            grid=(count // block,),
            in_specs=[
                pl.BlockSpec((block, WIDTH), lambda i, f, p, c=queries[1]: (i, c)),
                whole((depth, WIDTH), lambda i, f, p, c=keys[1]: (0, c)),
                whole((depth, WIDTH), lambda i, f, p, c=values[1]: (0, c)),
                pl.BlockSpec((block, WIDTH), lambda i, f, p: (i, 0)),
                pl.BlockSpec((8, block), lambda i, f, p: (0, i)),
                pl.BlockSpec((block, WIDTH), lambda i, f, p: (i, 0)),
                pl.BlockSpec((1, block), lambda i, f, p: (0, i)),
                pl.BlockSpec((1, block), lambda i, f, p: (0, i)),
                whole((depth, 1), lambda i, f, p: (0, 0)),
            ],
            out_specs=[
                pl.BlockSpec((block, WIDTH), lambda i, f, p: (i, 0)),
            ]
            + [whole((depth // splits, 2 * WIDTH), lambda i, f, p: (0, 0))] * splits,
            scratch_shapes=[
                pltpu.VMEM((HEADS, block, 128), jnp.bfloat16),
                pltpu.VMEM((HEADS, block, 128), jnp.bfloat16),
                pltpu.VMEM((8, block), jnp.float32),
                pltpu.VMEM((WIDTH, depth), jnp.bfloat16),
                pltpu.VMEM((WIDTH, block), jnp.float32),
                pltpu.VMEM((depth, WIDTH), jnp.float32),
                pltpu.VMEM((depth, WIDTH), jnp.float32),
            ],
        ),
        out_shape=[
            jax.ShapeDtypeStruct((count, WIDTH), jnp.bfloat16),
        ]
        + [jax.ShapeDtypeStruct((depth // splits, 2 * WIDTH), jnp.bfloat16)] * splits,
        compiler_params=pltpu.CompilerParams(vmem_limit_bytes=VMEM_LIMIT),
        cost_estimate=COST,
    )(
        flags.reshape(-1), places, queries[0], keys[0], values[0], grads, logs, exact, low[None, :],
        high[None, :], key_ids[:, None],
    )


def needed_chunks(low, high, key_ids, block, chunk):
    first = jnp.min(low.reshape(-1, block), 1)[:, None]
    last = jnp.max(high.reshape(-1, block), 1)[:, None]
    smallest = jnp.min(key_ids.reshape(-1, chunk), 1)[None, :]
    largest = jnp.max(key_ids.reshape(-1, chunk), 1)[None, :]
    return ((largest >= first) & (smallest <= last)).astype(jnp.int32)


def on_device(
    count,
    tokens,
    encoder,
    seq_lengths,
    slot_ids,
    enc_lengths,
    cotangent,
    self_in,
    self_out,
    cross_query,
    cross_pair,
    cross_out,
    feed_up,
    feed_down,
    vectors,
    feed_bias,
    self_bias,
):

    full_self_in = fetch(self_in)
    facts = jnp.concatenate([slot_ids[0], seq_lengths[0], enc_lengths[0]], 1)
    slots = slot_ids.shape[2]
    facts_one, facts_two = to_packs(facts)
    tokens_in = jnp.concatenate(to_packs(tokens), 0)
    small = jnp.concatenate([vectors.T, feed_bias.reshape(D // 4, 4).T, self_bias[None, :]], 0)
    full_small = lax.all_gather(small, ("x", "core"), axis=1, tiled=True)
    vec = full_small[:12].astype(jnp.float32)
    bias_row = full_small[12:16].T.reshape(4 * D).astype(jnp.float32)
    self_bias_row = full_small[16].astype(jnp.float32)
    zero_row = jnp.zeros((D,), jnp.float32)
    facts_one, (self_out, cross_query) = chain(facts_one, (self_out, cross_query))
    full_out_query = fetch(jnp.concatenate([self_out, cross_query], 1))
    encoder_in = jnp.concatenate(to_packs(encoder), 0)
    tokens_in, (cross_pair, cross_out) = chain(tokens_in, (cross_pair, cross_out))
    full_cross_pair = fetch(cross_pair)
    full_cross_out = fetch(cross_out)

    lengths = facts_one[slots : slots + NSEQ]
    limits = facts_one[slots + NSEQ : slots + 2 * NSEQ]
    own_ids = jnp.concatenate([facts_one[:slots], facts_two[:slots]])
    ids = lax.all_gather(own_ids, GROUP, axis=0, tiled=True)
    ends = jnp.cumsum(lengths)
    key_ids = gather_sequence(ids, count)
    rank = jnp.sum((ids[None, :] < ids[:, None]).astype(jnp.int32), 1)
    places = jnp.arange(ids.shape[0], dtype=jnp.int32)
    sorted_ids = jnp.sum(jnp.where(places[:, None] == rank[None, :], ids[None, :], 0), 1)
    key_order = gather_sequence(sorted_ids, count)
    seq_of = jnp.sum((sorted_ids[:, None] >= ends[None, :]).astype(jnp.int32), 1)
    starts = jnp.concatenate([jnp.zeros((1,), jnp.int32), ends[:-1]])
    picked = seq_of[:, None] == jnp.arange(NSEQ, dtype=jnp.int32)[None, :]
    self_low = jnp.sum(jnp.where(picked, starts[None, :], 0), 1)
    self_high = sorted_ids
    cross_low = seq_of * ENC
    cross_high = cross_low + jnp.sum(jnp.where(picked, limits[None, :], 0), 1) - 1
    enc_rows = encoder.shape[1]
    micro = lax.axis_index("t") & 1
    starts_of = []
    for index_s in range(count):
        for step in range(MEMBERS):
            core = lax.axis_index("core") ^ (step & 1)
            y_index = lax.axis_index("y") ^ (step >> 1)
            for part in range(2):
                t_index = 2 * core + (micro ^ part)
                starts_of.append(((t_index * count + index_s) * PAIR + y_index) * enc_rows)
    enc_places = jnp.stack(starts_of)
    enc_ids = jnp.arange(NSEQ * ENC, dtype=jnp.int32)
    if count > 1:
        enc_ids = (enc_places[:, None] + jnp.arange(enc_rows, dtype=jnp.int32)[None, :]).reshape(-1)
        enc_places = jnp.array([0, NSEQ * ENC // 2], jnp.int32)
    self_places = jnp.array([0, key_order.shape[0] // 2], jnp.int32)
    block = 256
    self_chunk, cross_chunk = 256, 512 if count == 1 else 384
    self_flags = needed_chunks(self_low, self_high, key_order, block, self_chunk)
    cross_flags = needed_chunks(cross_low, cross_high, enc_ids, block, cross_chunk)

    orders = {
        "x": ("core", "x", "y", "t0", "t1"),
        "y": ("core", "y", "x", "t0", "t1"),
    }

    def relative(matrix, name):
        return relative_columns(matrix, count, orders[name])

    facts_known = (rank, self_flags, cross_flags, key_order, enc_places, self_low, cross_low, cross_high)
    tokens_in, facts_known = chain(tokens_in, facts_known)
    rank, self_flags, cross_flags, key_order, enc_places, self_low, cross_low, cross_high = facts_known
    qkv = project_heads(tokens_in, full_self_in, jnp.concatenate([vec[6], zero_row, vec[7]]))
    feed_own = stack_feed(feed_up, feed_down)
    own_heads = sort_rows(to_members(qkv), rank)
    if count > 1:
        pairs = gather_sequence(own_heads[:, WIDTH:], count)
        self_keys, self_values = (pairs, 0), (pairs, 1)
    else:
        self_keys, self_values = (own_heads, 1), (own_heads, 2)
    tokens_x, tokens_y = relative(tokens_in, "x"), relative(tokens_in, "y")
    encoder_y = relative(encoder_in, "y")
    index = relative_index(D, count, orders["y"])
    pick_y = (index[:, None] == jnp.arange(D, dtype=jnp.int32)[None, :]).astype(jnp.bfloat16)
    (tokens_x, tokens_y, encoder_y, pick_y, own_heads), (encoder_in, cotangent) = chain(
        (tokens_x, tokens_y, encoder_y, pick_y, own_heads), (encoder_in, cotangent)
    )
    grad_in = jnp.concatenate(to_packs(cotangent), 0)
    attended_heads, exact_self, log_self = attend_forward(
        (own_heads, 0), self_keys, self_values, self_low, self_high, key_order, self_flags,
        block, self_chunk,
    )
    attended_heads, feed_own = chain(attended_heads, feed_own)
    feed_far = lax.ppermute(feed_own, "x", SWAP)
    enc_pairs = project_blocks(
        encoder_in, full_cross_pair, jnp.concatenate([zero_row, vec[9]])
    )
    attended = to_members(unsort_rows([attended_heads], rank))
    attended, enc_pairs = chain(attended, enc_pairs)
    if count == 1:
        enc_heads = assemble(exchange(enc_pairs), enc_places)
    else:
        enc_heads = gather_sequence(jnp.concatenate(exchange(enc_pairs), 0), count)
    normed_one, normed_one_low, unit_one, inverse_one, cross_queries = project_norm(
        by_member(attended), full_out_query, self_bias_row, tokens_in, vec[0], vec[3],
        after=(vec[8],),
    )
    cross_heads = sort_rows(to_members(cross_queries), rank)
    attended_y = relative(as_columns(attended), "y")
    normed_one_y = relative(normed_one_low, "y")
    (attended_y, normed_one_y), cross_heads = chain((attended_y, normed_one_y), cross_heads)
    crossed_heads, exact_cross, log_cross = attend_forward(
        (cross_heads, 0), (enc_heads, 0), (enc_heads, 1), cross_low, cross_high, enc_ids,
        cross_flags, block, cross_chunk,
    )
    cross_heads, (feed_own, full_cross_out) = chain(cross_heads, (feed_own, full_cross_out))
    feed_near = lax.ppermute(feed_own, "core", SWAP)
    crossed_heads, grad_in = chain(crossed_heads, grad_in)
    crossed = to_members(unsort_rows([crossed_heads], rank))
    crossed, feed_far = chain(crossed, feed_far)
    feed_shards = [feed_own, feed_near, feed_far, lax.ppermute(feed_far, "core", SWAP)]
    normed_two, normed_two_low, unit_two, inverse_two = project_norm(
        by_member(crossed), full_cross_out, vec[10], normed_one, vec[1], vec[4]
    )
    crossed_y = relative(as_columns(crossed), "y")
    crossed_y, normed_two_low = chain(crossed_y, normed_two_low)
    slope, hidden = feed_up_gelu(normed_two_low, feed_shards, bias_row)
    layer_low, grad_three, grad_branch, sums_three = feed_down_norm(
        hidden, feed_shards, vec[11], normed_two, vec[2], vec[5], grad_in
    )
    half = tokens_in.shape[0] // 2

    grad_pre, bias_up, grad_two, grad_crossed_out, sums_two, grad_crossed = feed_back(
        slope, feed_shards, grad_branch, grad_three, unit_two, inverse_two, vec[1],
        full_cross_out,
    )
    received, (feed_parts, layer_low) = during_members(
        grad_crossed, lambda layer, *rows: (feed_grads(*rows, count), layer),
        (layer_low, hidden, grad_branch, normed_two_low, grad_pre),
    )
    layer_out = from_packs(layer_low[:half], layer_low[half:])
    feed_sum = reduce_feed(feed_parts)
    grad_crossed_heads = sort_rows(received, rank)
    dq_heads, *enc_pair_grads = attend_backward(
        (cross_heads, 0), (enc_heads, 0), (enc_heads, 1), grad_crossed_heads, log_cross,
        exact_cross, cross_low, cross_high, enc_ids, cross_flags, block, cross_chunk, enc_places,
    )
    layer_out, dq_heads = chain(layer_out, dq_heads)
    if count > 1:
        enc_pair_grads = cut(scatter_sequence(enc_pair_grads[0], count))
    dq_blocks, (enc_pair_grads,) = during_members(
        unsort_rows([dq_heads], rank), lambda *rest: rest, (enc_pair_grads,)
    )
    enc_blocks = exchange(enc_pair_grads)
    grad_one, grad_attended_out, sums_one, grad_attended = back_norm(
        by_member(dq_blocks), full_out_query, grad_two, unit_one, inverse_one, vec[0]
    )

    received, (*three_parts, query_sums) = during_members(
        grad_attended,
        lambda blocks: three_grads(
            attended_y, normed_one_y, crossed_y, grad_attended_out, blocks, grad_crossed_out
        ),
        (dq_blocks,),
    )
    three_sum = Halving(three_parts, count, orders["y"])
    grad_attended_heads = sort_rows(received, rank)
    dq_heads, pair_heads = attend_backward(
        (own_heads, 0), self_keys, self_values, grad_attended_heads, log_self, exact_self,
        self_low, self_high, key_order, self_flags, block, self_chunk, self_places,
    )
    pair_heads = scatter_sequence(pair_heads, count)

    dq_heads, three_sum.pending = chain(dq_heads, three_sum.pending)
    three_sum.step()
    (dq_heads, three_sum.sent, three_sum.value), enc_blocks = chain(
        (dq_heads, three_sum.sent, three_sum.value), enc_blocks
    )

    blocks, me = chain(unsort_blocks([dq_heads, pair_heads], rank), group_index()[None])
    received = exchange(blocks)
    *pair_parts, enc_first, enc_rest, value_sums = encoder_grads(
        me, encoder_y, full_cross_pair, enc_blocks
    )
    (pair_parts, enc_first, enc_rest), received = chain((pair_parts, enc_first, enc_rest), received)
    pair_sum = Halving(pair_parts, count, orders["y"])
    enc_first = send_back(enc_first, 0)
    left_parts, right_parts, grad_qkv = self_in_grads(
        group_index()[None], tokens_x, tokens_y, pick_y, sums_one, sums_two, sums_three, bias_up,
        query_sums, value_sums, received,
    )
    left_sum = Halving(left_parts, count, orders["x"])
    right_sum = Halving(right_parts, count, orders["y"])
    def steps(last, *halvings):
        for halving in halvings:
            last.value, halving.pending = chain(last.value, halving.pending)
            halving.step()
            last = halving
        return last

    last = right_sum
    last.value, grad_qkv = chain(last.value, grad_qkv)
    grad_rows = back_project(grad_qkv, full_self_in, grad_one)
    last.value, grad_rows = chain(last.value, grad_rows)
    last = steps(last, left_sum, right_sum, pair_sum, three_sum)
    last.value, (enc_first, enc_rest) = chain(last.value, (enc_first, enc_rest))
    enc_second = send_back(enc_rest, 1)
    last = steps(last, right_sum, left_sum, pair_sum)
    last.value, feed_sum = chain(last.value, feed_sum)
    feed_kept, feed_sent = split_feed(feed_sum)
    feed_arrived = flip(feed_sent, "y")
    last = steps(last, three_sum)
    last.value, enc_second = chain(last.value, enc_second)
    last = steps(last, right_sum)
    last.value, rows_first = chain(last.value, grad_rows[:half])
    rows_first = send_back(rows_first, 0)
    last = steps(last, left_sum, three_sum)
    last.value, (rows_first, rows_second) = chain(last.value, (rows_first, grad_rows[half:]))
    rows_second = send_back(rows_second, 1)
    last = steps(last, pair_sum)
    last.value, feed_arrived = chain(last.value, feed_arrived)
    last = steps(last, right_sum, left_sum, pair_sum)
    grad_encoder = order_back(enc_first, enc_second)
    grad_tokens = order_back(rows_first, rows_second).astype(jnp.float32)
    three, pair = three_sum.finish(), pair_sum.finish()
    left, right = left_sum.finish(), right_sum.finish()
    up_sum, down_sum = merge_feed(feed_kept, feed_arrived)
    small = right[:, 3 * D // 2 :]
    return (
        layer_out,
        grad_tokens,
        grad_encoder.astype(jnp.float32),
        jnp.concatenate([left, right[:, : 3 * D // 2]], 1),
        three[:, :D],
        three[:, D : 2 * D],
        pair,
        three[:, 2 * D :],
        up_sum,
        down_sum,
        small[:, :12],
        small[:, 13:17].reshape(-1),
        small[:, 12],
    )


def solution(mesh):
    contexts = mesh.shape["ctx"]
    count = contexts // (T_SIZE * PAIR)
    fine = Mesh(
        mesh.devices.reshape(T_SIZE, count, PAIR, PAIR, PAIR), ("t", "s", "y", "x", "core")
    )
    fsdp, ctx = ("x", "core"), ("t", "s", "y")
    in_specs = (
        P(None, ROWS, None),
        P(None, ROWS, None),
        P(fsdp, None, None),
        P(fsdp, None, ctx),
        P(fsdp, None, None),
        P(None, ROWS, None),
        P(fsdp, None),
        P(fsdp, None),
        P(fsdp, None),
        P(fsdp, None),
        P(fsdp, None),
        P(fsdp, None),
        P(fsdp, None),
        P(fsdp, None),
        P(fsdp),
        P(fsdp),
    )
    out_specs = (P(None, ROWS, None),) * 3 + (P(BLOCKS, None),) * 8 + (P(BLOCKS),) * 2
    return jax.shard_map(
        functools.partial(on_device, count),
        mesh=fine,
        in_specs=in_specs,
        out_specs=out_specs,
        check_vma=False,
    )
```

```python
import functools

import jax
import jax.numpy as jnp
from jax import lax
from jax.experimental import pallas as pl
from jax.experimental.pallas import tpu as pltpu
from jax.sharding import Mesh
from jax.sharding import PartitionSpec as P

D = 1024
HD = 64
ENC = 1024
NSEQ = 3
MICRO = 2
DEPTH = 6

EPSILON = 1e-05
MASKED = -1e30
SCALE = HD ** (-0.5)
T_SIZE = 4
PAIR = 2
GROUP = ("y", "core")
ROWS = ("x", "core", "t", "s", "y")
BLOCKS = ("t", "s", "y", "x", "core")
MEMBERS = 4
WIDTH = D // MEMBERS
HEADS = WIDTH // HD
VMEM_LIMIT = 56 * 1024 * 1024
RESIDUAL = (3.0 * DEPTH) ** 0.25
COST = pl.CostEstimate(flops=0, bytes_accessed=0, transcendentals=0)


def norm_forward(resid, gain, offset):
    average = jnp.mean(resid, -1, keepdims=True)
    centered = resid - average
    inverse = lax.rsqrt(jnp.mean(centered * centered, -1, keepdims=True) + EPSILON)
    normed = centered * inverse
    return (normed * gain + offset, normed, inverse)


def norm_backward(grad_out, normed, inverse, gain):
    grad_normed = grad_out * gain
    first_mean = jnp.mean(grad_normed, -1, keepdims=True)
    second_mean = jnp.mean(grad_normed * normed, -1, keepdims=True)
    grad_resid = inverse * (grad_normed - first_mean - normed * second_mean)
    return (grad_resid, jnp.sum(grad_out * normed, 0), jnp.sum(grad_out, 0))


def column_sum(left, right):
    return lax.dot_general(
        left, right, (((0,), (0,)), ((), ())), preferred_element_type=jnp.float32
    )


def input_grad(grad_rows, weight):
    return lax.dot_general(
        grad_rows, weight, (((1,), (1,)), ((), ())), preferred_element_type=jnp.float32
    )


def linear(inputs, weight):
    return jnp.dot(inputs, weight, preferred_element_type=jnp.float32)


def pack_routes():
    straight, crossed = [], []
    for t in range(T_SIZE):
        for core in range(PAIR):
            here = t * PAIR + core
            straight.append((here, (2 * core + (t & 1)) * PAIR + (t >> 1)))
            crossed.append((here, (2 * core + 1 - (t & 1)) * PAIR + (t >> 1)))
    return straight, crossed


def to_packs(parts):
    straight, crossed = pack_routes()
    parity = lax.axis_index("t") & 1
    first = lax.dynamic_index_in_dim(parts, parity, 0, keepdims=False)
    second = lax.dynamic_index_in_dim(parts, 1 - parity, 0, keepdims=False)
    return (
        lax.ppermute(first, ("t", "core"), straight),
        lax.ppermute(second, ("t", "core"), crossed),
    )


def send_back(part, place):
    route = pack_routes()[place]
    return lax.ppermute(part, ("t", "core"), [(to, source) for source, to in route])


def order_back(first, second):
    parity = lax.axis_index("t") & 1
    return jnp.stack(
        [jnp.where(parity == 0, first, second), jnp.where(parity == 0, second, first)], 0
    )


def from_packs(first, second):
    return order_back(send_back(first, 0), send_back(second, 1))


def group_route(step):
    return [(member, member ^ step) for member in range(MEMBERS)]


def group_index():
    return lax.axis_index("y") * PAIR + lax.axis_index("core")


def join_kernel(parts, me_ref, *refs):
    matrix_ref = refs[-1]
    for step, block_ref in enumerate(refs[:-1]):
        for part in range(parts):
            start = pl.multiple_of(part * D + (me_ref[0] ^ step) * WIDTH, WIDTH)
            matrix_ref[:, pl.ds(start, WIDTH)] = block_ref[:, part * WIDTH : (part + 1) * WIDTH]


def join_members_kernel(blocks_ref, matrix_ref):
    rows = matrix_ref.shape[0]
    for member in range(MEMBERS):
        for part in range(matrix_ref.shape[1] // D):
            start = part * D + member * WIDTH
            matrix_ref[:, start : start + WIDTH] = blocks_ref[
                member * rows : (member + 1) * rows, part * WIDTH : (part + 1) * WIDTH
            ]


def in_vmem(count):
    return [pl.BlockSpec(memory_space=pltpu.VMEM)] * count


def small_kernel(body, scalars, operands, outs, work=0):
    return pl.pallas_call(
        body,
        in_specs=[pl.BlockSpec(memory_space=pltpu.SMEM)] * len(scalars) + in_vmem(len(operands)),
        out_specs=in_vmem(len(outs)),
        out_shape=outs,
        compiler_params=pltpu.CompilerParams(vmem_limit_bytes=VMEM_LIMIT),
        cost_estimate=COST,
    )(*scalars, *operands)


def fetch(weight):
    return lax.all_gather(weight, ("x", "core"), axis=0, tiled=True)


SWAP = [(0, 1), (1, 0)]


def stack_feed(up, down):
    return jnp.concatenate([down] + [up[:, part * D : (part + 1) * D] for part in range(4)], 0)


def up_specs(column):
    def block(i, p):
        place = column(i, p)
        return (MEMBERS + place // 2, place % 2)

    return [pl.BlockSpec((D // MEMBERS, FEED_TILE), block)] * MEMBERS


def shard_index():
    return (lax.axis_index("x") * PAIR + lax.axis_index("core"))[None]


def product(rows_ref, weight_ref, start=0, width=None):
    columns = slice(start, weight_ref.shape[1] if width is None else start + width)
    if len(rows_ref.shape) == 2:
        return linear(rows_ref[...], weight_ref[:, columns])
    total = None
    for member in range(MEMBERS):
        lines = slice(member * WIDTH, (member + 1) * WIDTH)
        term = linear(rows_ref[member], weight_ref[lines, columns])
        total = term if total is None else total + term
    return total


def back_product(grads_ref, weight_ref, lines=slice(None), offset=0):
    if len(grads_ref.shape) == 2:
        return input_grad(
            grads_ref[...], weight_ref[lines, offset : offset + grads_ref.shape[1]]
        )
    total = None
    for member in range(MEMBERS):
        columns = slice(offset + member * WIDTH, offset + (member + 1) * WIDTH)
        term = input_grad(grads_ref[member], weight_ref[lines, columns])
        total = term if total is None else total + term
    return total


def put_heads(rows_ref, weight_ref, bias_ref, out_ref, offset=0):
    count = out_ref.shape[0] // MEMBERS
    for member in range(MEMBERS):
        for part in range(out_ref.shape[1] // WIDTH):
            start = part * D + member * WIDTH
            value = product(rows_ref, weight_ref, offset + start, WIDTH)
            value = value + bias_ref[:, start : start + WIDTH]
            out_ref[
                member * count : (member + 1) * count, part * WIDTH : (part + 1) * WIDTH
            ] = value.astype(jnp.bfloat16)


def put_back_heads(grads_ref, weight_ref, out_ref):
    count = out_ref.shape[0] // MEMBERS
    for member in range(MEMBERS):
        value = back_product(grads_ref, weight_ref, slice(member * WIDTH, (member + 1) * WIDTH))
        out_ref[member * count : (member + 1) * count, :] = value.astype(jnp.bfloat16)


def heads_kernel(rows_ref, weight_ref, bias_ref, out_ref):
    put_heads(rows_ref, weight_ref, bias_ref, out_ref)


def project_heads(rows, weight, bias):
    shape = jax.ShapeDtypeStruct((rows.shape[0] * MEMBERS, weight.shape[1] // MEMBERS), jnp.bfloat16)
    return small_kernel(heads_kernel, [], [rows, weight, bias[None, :]], [shape])[0]


def own_heads_kernel(me_ref, rows_ref, weight_ref, bias_ref, *outs):
    for step, out_ref in reversed(list(enumerate(outs))):
        for part in range(out_ref.shape[1] // WIDTH):
            start = pl.multiple_of(part * D + (me_ref[0] ^ step) * WIDTH, WIDTH)
            value = linear(rows_ref[...], weight_ref[:, pl.ds(start, WIDTH)])
            value = value + bias_ref[:, pl.ds(start, WIDTH)]
            out_ref[:, part * WIDTH : (part + 1) * WIDTH] = value.astype(jnp.bfloat16)


def project_blocks(rows, weight, bias):
    shape = jax.ShapeDtypeStruct((rows.shape[0], weight.shape[1] // MEMBERS), jnp.bfloat16)
    work = 2 * rows.shape[0] * weight.size
    return small_kernel(
        own_heads_kernel, [group_index()[None]], [rows, weight, bias[None, :]], [shape] * MEMBERS,
        work,
    )


def norm_kernel(
    rows_ref, weight_ref, bias_ref, base_ref, gain_ref, offset_ref, *refs
):
    outs = refs if len(refs) == 4 else refs[1:]
    resid = (
        RESIDUAL * base_ref[...].astype(jnp.float32)
        + product(rows_ref, weight_ref, 0, D)
        + bias_ref[...]
    )
    normed, unit, inverse = norm_forward(resid, gain_ref[...], offset_ref[...])
    outs[0][...] = normed
    outs[1][...] = normed.astype(jnp.bfloat16)
    outs[2][...] = unit
    outs[3][...] = inverse
    if len(refs) > 4:
        put_heads(outs[1], weight_ref, refs[0], outs[4], D)


def project_norm(rows, weight, bias, base, gain, offset, after=()):
    count = base.shape[0]
    outs = [
        jax.ShapeDtypeStruct((count, D), jnp.float32),
        jax.ShapeDtypeStruct((count, D), jnp.bfloat16),
        jax.ShapeDtypeStruct((count, D), jnp.float32),
        jax.ShapeDtypeStruct((count, 1), jnp.float32),
    ]
    if after:
        outs.append(jax.ShapeDtypeStruct((count * MEMBERS, WIDTH), jnp.bfloat16))
    return small_kernel(
        norm_kernel, [],
        [rows, weight, bias[None, :], base, gain[None, :], offset[None, :]]
        + [row[None, :] for row in after],
        outs,
    )


FEED_TILE = 512


def feed_column(step, me, tiles):
    return (me ^ (step // tiles)) * tiles + step % tiles


def up_kernel(me_ref, rows_ref, *refs):
    shards, (bias_ref, slope_ref, hidden_ref) = refs[:MEMBERS], refs[MEMBERS:]
    depth = shards[0].shape[0]
    active = bias_ref[...]
    for index, shard in enumerate(shards):
        start = pl.multiple_of((me_ref[0] ^ index) * depth, depth)
        active = active + linear(rows_ref[:, pl.ds(start, depth)], shard[...])
    cumulative = 0.5 * (1.0 + lax.erf(active * 0.7071067811865476))
    density = jnp.exp(-0.5 * active * active) * 0.3989422804014327
    slope_ref[...] = cumulative + active * density
    hidden_ref[...] = (active * cumulative).astype(jnp.bfloat16)


def feed_up_gelu(rows, shards, bias):
    count, width = rows.shape[0], 4 * D
    column = lambda i, p: (0, i)
    return pl.pallas_call(
        up_kernel,
        grid_spec=pltpu.PrefetchScalarGridSpec(
            num_scalar_prefetch=1,
            grid=(width // FEED_TILE,),
            in_specs=[pl.BlockSpec((count, D), lambda i, p: (0, 0))]
            + up_specs(lambda i, p: i)
            + [pl.BlockSpec((1, FEED_TILE), column)],
            out_specs=[pl.BlockSpec((count, FEED_TILE), column)] * 2,
        ),
        out_shape=[
            jax.ShapeDtypeStruct((count, width), jnp.float32),
            jax.ShapeDtypeStruct((count, width), jnp.bfloat16),
        ],
        compiler_params=pltpu.CompilerParams(vmem_limit_bytes=VMEM_LIMIT),
        cost_estimate=COST,
    )(shard_index(), rows, *shards, bias[None, :])


def put_norm_back(grads, unit, inverse, gain, resid_ref, low_ref, sums_ref):
    resid, gain_sum, offset_sum = norm_backward(grads, unit, inverse, gain)
    low = resid.astype(jnp.bfloat16)
    resid_ref[...] = resid
    low_ref[...] = low
    sums_ref[0:1, :] = gain_sum[None, :]
    sums_ref[1:2, :] = offset_sum[None, :]
    sums_ref[2:3, :] = jnp.sum(low.astype(jnp.float32), 0)[None, :]
    sums_ref[3:8, :] = jnp.zeros((5, D), jnp.float32)


def down_kernel(tiles, me_ref, hidden_ref, *refs):
    shards = refs[:MEMBERS]
    bias_ref, base_ref, gain_ref, offset_ref, grads_ref = refs[MEMBERS : MEMBERS + 5]
    layer_ref, resid_ref, low_ref, sums_ref, total_ref = refs[MEMBERS + 5 :]
    step = pl.program_id(0)

    @pl.when(step == 0)
    def _():
        total_ref[...] = RESIDUAL * base_ref[...] + bias_ref[...]

    for index, shard in enumerate(shards):

        @pl.when(step // tiles == index)
        def _(shard=shard):
            total_ref[...] += linear(hidden_ref[...], shard[...])

    @pl.when(step == pl.num_programs(0) - 1)
    def _():
        layer, unit, inverse = norm_forward(total_ref[...], gain_ref[...], offset_ref[...])
        layer_ref[...] = layer.astype(jnp.bfloat16)
        put_norm_back(
            grads_ref[...].astype(jnp.float32), unit, inverse, gain_ref[...], resid_ref, low_ref,
            sums_ref,
        )


def one_block(array):
    return pl.BlockSpec(array.shape, lambda i, p: (0,) * len(array.shape))


def down_specs(tiles):
    return [
        pl.BlockSpec((FEED_TILE, D), lambda i, p, s=s: (jnp.clip(i - s * tiles, 0, tiles - 1), 0))
        for s in range(MEMBERS)
    ]


def feed_down_norm(hidden, shards, bias, base, gain, offset, grads):
    count = base.shape[0]
    tiles = D // FEED_TILE
    fixed = [bias[None, :], base, gain[None, :], offset[None, :], grads]
    outs = [
        jax.ShapeDtypeStruct((count, D), jnp.bfloat16),
        jax.ShapeDtypeStruct((count, D), jnp.float32),
        jax.ShapeDtypeStruct((count, D), jnp.bfloat16),
        jax.ShapeDtypeStruct((8, D), jnp.float32),
    ]
    return pl.pallas_call(
        functools.partial(down_kernel, tiles),
        grid_spec=pltpu.PrefetchScalarGridSpec(
            num_scalar_prefetch=1,
            grid=(MEMBERS * tiles,),
            in_specs=[
                pl.BlockSpec((count, FEED_TILE), lambda i, p: (0, feed_column(i, p[0], tiles)))
            ]
            + down_specs(tiles)
            + [one_block(array) for array in fixed],
            out_specs=[one_block(out) for out in outs],
            scratch_shapes=[pltpu.VMEM((count, D), jnp.float32)],
        ),
        out_shape=outs,
        compiler_params=pltpu.CompilerParams(vmem_limit_bytes=VMEM_LIMIT),
        cost_estimate=COST,
    )(shard_index(), hidden, *shards, *fixed)


def feed_back_kernel(tiles, me_ref, slope_ref, *refs):
    downs, ups, refs = refs[:MEMBERS], refs[MEMBERS : 2 * MEMBERS], refs[2 * MEMBERS :]
    grads_ref, resid_ref, unit_ref, inverse_ref, gain_ref, out_ref = refs[:6]
    du_ref, bias_ref, next_resid_ref, next_low_ref, sums_ref, heads_ref, total_ref = refs[6:]
    step = pl.program_id(0)
    depth = ups[0].shape[0]

    @pl.when(step == 0)
    def _():
        total_ref[...] = RESIDUAL * resid_ref[...]

    slope = slope_ref[...]
    for index, shard in enumerate(downs):

        @pl.when(step // tiles == index)
        def _(shard=shard):
            du_ref[...] = (back_product(grads_ref, shard) * slope).astype(jnp.bfloat16)

    du = du_ref[...]
    bias_ref[...] = jnp.sum(du.astype(jnp.float32), 0, keepdims=True)
    for index, shard in enumerate(ups):
        start = pl.multiple_of((me_ref[0] ^ index) * depth, depth)
        total_ref[:, pl.ds(start, depth)] += input_grad(du, shard[...])

    @pl.when(step == pl.num_programs(0) - 1)
    def _():
        put_norm_back(
            total_ref[...], unit_ref[...], inverse_ref[...], gain_ref[...], next_resid_ref,
            next_low_ref, sums_ref,
        )
        put_back_heads(next_low_ref, out_ref, heads_ref)


def feed_back(slope, shards, grads, resid, unit, inverse, gain, out_weight):
    count, width = slope.shape
    tiles = D // FEED_TILE
    fixed = [grads, resid, unit, inverse, gain[None, :], out_weight]
    column = lambda i, p: (0, feed_column(i, p[0], tiles))
    outs = [
        jax.ShapeDtypeStruct((count, width), jnp.bfloat16),
        jax.ShapeDtypeStruct((1, width), jnp.float32),
        jax.ShapeDtypeStruct((count, D), jnp.float32),
        jax.ShapeDtypeStruct((count, D), jnp.bfloat16),
        jax.ShapeDtypeStruct((8, D), jnp.float32),
        jax.ShapeDtypeStruct((count * MEMBERS, WIDTH), jnp.bfloat16),
    ]
    return pl.pallas_call(
        functools.partial(feed_back_kernel, tiles),
        grid_spec=pltpu.PrefetchScalarGridSpec(
            num_scalar_prefetch=1,
            grid=(MEMBERS * tiles,),
            in_specs=[pl.BlockSpec((count, FEED_TILE), column)]
            + down_specs(tiles)
            + up_specs(lambda i, p: feed_column(i, p[0], tiles))
            + [one_block(array) for array in fixed],
            out_specs=[
                pl.BlockSpec((count, FEED_TILE), column), pl.BlockSpec((1, FEED_TILE), column)
            ]
            + [one_block(out) for out in outs[2:]],
            scratch_shapes=[pltpu.VMEM((count, D), jnp.float32)],
        ),
        out_shape=outs,
        compiler_params=pltpu.CompilerParams(vmem_limit_bytes=VMEM_LIMIT),
        cost_estimate=COST,
    )(shard_index(), slope, *shards, *shards, *fixed)


def norm_back_kernel(
    grads_ref, weight_ref, resid_ref, unit_ref, inverse_ref, gain_ref,
    next_resid_ref, next_low_ref, sums_ref, heads_ref,
):
    total = RESIDUAL * resid_ref[...] + back_product(grads_ref, weight_ref, offset=D)
    put_norm_back(
        total, unit_ref[...], inverse_ref[...], gain_ref[...], next_resid_ref, next_low_ref, sums_ref
    )
    put_back_heads(next_low_ref, weight_ref, heads_ref)


def back_norm(grads, weight, resid, unit, inverse, gain):
    count = resid.shape[0]
    outs = [
        jax.ShapeDtypeStruct((count, D), jnp.float32),
        jax.ShapeDtypeStruct((count, D), jnp.bfloat16),
        jax.ShapeDtypeStruct((8, D), jnp.float32),
        jax.ShapeDtypeStruct((count * MEMBERS, WIDTH), jnp.bfloat16),
    ]
    return small_kernel(
        norm_back_kernel, [], [grads, weight, resid, unit, inverse, gain[None, :]], outs
    )


def back_kernel(grads_ref, weight_ref, resid_ref, out_ref):
    value = RESIDUAL * resid_ref[...] + back_product(grads_ref, weight_ref)
    out_ref[...] = value.astype(out_ref.dtype)


def back_project(grads, weight, resid):
    count, width = grads.shape
    rows = 256
    return pl.pallas_call(
        back_kernel,
        grid=(weight.shape[0] // rows,),
        in_specs=[
            pl.BlockSpec((count, width), lambda i: (0, 0)),
            pl.BlockSpec((rows, width), lambda i: (i, 0)),
            pl.BlockSpec((count, rows), lambda i: (0, i)),
        ],
        out_specs=pl.BlockSpec((count, rows), lambda i: (0, i)),
        out_shape=jax.ShapeDtypeStruct((count, weight.shape[0]), jnp.bfloat16),
        compiler_params=pltpu.CompilerParams(vmem_limit_bytes=VMEM_LIMIT),
        cost_estimate=COST,
    )(grads, weight, resid)


def to_members(blocks):
    return lax.all_to_all(blocks, GROUP, 0, 0, tiled=True)


def by_member(blocks):
    return blocks.reshape(MEMBERS, blocks.shape[0] // MEMBERS, blocks.shape[1])


def as_columns(blocks):
    shape = (blocks.shape[0] // MEMBERS, blocks.shape[1] * MEMBERS)
    return small_kernel(
        join_members_kernel, [], [blocks], [jax.ShapeDtypeStruct(shape, blocks.dtype)]
    )[0]


def chain(first, second):
    return lax.optimization_barrier((first, second))


def exchange(blocks):
    return [
        block if step == 0 else lax.ppermute(block, GROUP, group_route(step))
        for step, block in enumerate(blocks)
    ]


def during_members(blocks, work, inputs):
    blocks, inputs = chain(blocks, inputs)
    results, received = chain(work(*inputs), to_members(blocks))
    return received, results


def cut(matrix):
    rows = matrix.shape[0] // MEMBERS
    return [matrix[step * rows : (step + 1) * rows] for step in range(MEMBERS)]


def sort_kernel(rank_ref, blocks_ref, sorted_ref):
    rows = blocks_ref.shape[0] // MEMBERS
    for place in range(MEMBERS):
        wanted = lax.broadcasted_iota(jnp.int32, (rows, rows * MEMBERS), 0) + place * rows
        pick = (rank_ref[...] == wanted).astype(jnp.bfloat16)
        sorted_ref[place * rows : (place + 1) * rows, :] = linear(pick, blocks_ref[...]).astype(
            jnp.bfloat16
        )


def put_unsorted(ranks, parts, block_ref, lines):
    rows = ranks.shape[0]
    wanted = lax.broadcasted_iota(jnp.int32, (rows, rows * MEMBERS), 1)
    pick = (ranks == wanted).astype(jnp.bfloat16)
    start = 0
    for sorted_ref in parts:
        end = start + sorted_ref.shape[1]
        block_ref[lines, start:end] = linear(pick, sorted_ref[...]).astype(jnp.bfloat16)
        start = end


def unsort_kernel(rank_ref, *refs):
    blocks_ref = refs[-1]
    rows = blocks_ref.shape[0] // MEMBERS
    for member in range(MEMBERS):
        lines = slice(member * rows, (member + 1) * rows)
        put_unsorted(rank_ref[lines, :], refs[:-1], blocks_ref, lines)


def unsort_blocks_kernel(me_ref, rank_ref, *refs):
    for step, block_ref in enumerate(refs[-MEMBERS:]):
        rows = block_ref.shape[0]
        start = pl.multiple_of((me_ref[0] ^ step) * rows, rows)
        put_unsorted(rank_ref[pl.ds(start, rows), :], refs[:-MEMBERS], block_ref, slice(None))


def unsort_blocks(parts, rank):
    rows, width = parts[0].shape[0] // MEMBERS, sum(part.shape[1] for part in parts)
    shape = jax.ShapeDtypeStruct((rows, width), jnp.bfloat16)
    return small_kernel(
        unsort_blocks_kernel, [group_index()[None]], [rank[:, None], *parts], [shape] * MEMBERS
    )


def sort_rows(blocks, rank):
    shape = jax.ShapeDtypeStruct(blocks.shape, jnp.bfloat16)
    work = 2 * blocks.size * blocks.shape[0]
    return small_kernel(sort_kernel, [], [rank[None, :], blocks], [shape], work)[0]


def unsort_rows(parts, rank):
    width = sum(part.shape[1] for part in parts)
    shape = jax.ShapeDtypeStruct((parts[0].shape[0], width), jnp.bfloat16)
    work = 2 * shape.size * shape.shape[0]
    return small_kernel(unsort_kernel, [], [rank[:, None], *parts], [shape], work)[0]


def assemble_kernel(places_ref, *refs):
    blocks, whole_ref = refs[:-1], refs[-1]
    for place, block_ref in enumerate(blocks):
        size = block_ref.shape[0] // 2
        for half in range(2):
            start = pl.multiple_of(places_ref[2 * place + half], 128)
            whole_ref[pl.ds(start, size), :] = block_ref[half * size : (half + 1) * size, :]


def assemble(blocks, places):
    shape = jax.ShapeDtypeStruct((len(blocks) * blocks[0].shape[0], blocks[0].shape[1]), jnp.bfloat16)
    return small_kernel(assemble_kernel, [places], blocks, [shape])[0]


def gather_sequence(matrix, count):
    if count == 1:
        return matrix
    return lax.all_gather(matrix, "s", axis=0, tiled=True)


def scatter_sequence(matrix, count):
    if count == 1:
        return matrix
    return lax.psum_scatter(matrix, "s", scatter_dimension=0, tiled=True)


def own_bits():
    t_index = lax.axis_index("t")
    return {
        "t1": t_index >> 1,
        "t0": t_index & 1,
        "y": lax.axis_index("y"),
        "x": lax.axis_index("x"),
        "core": lax.axis_index("core"),
    }


def flip(block, name):
    if name in ("t1", "t0"):
        step = 2 if name == "t1" else 1
        return lax.ppermute(block, "t", [(i, i ^ step) for i in range(T_SIZE)])
    return lax.ppermute(block, name, [(i, i ^ 1) for i in range(PAIR)])


def relative_index(total, count, order):
    rows = total // (32 * count)
    place = jnp.arange(total, dtype=jnp.int32)
    bits, mine = {"r": place % rows, "s": place // rows % count}, own_bits()
    for index, name in enumerate(order):
        bits[name] = (place // (rows * count) >> (len(order) - 1 - index) & 1) ^ mine[name]
    row = (bits["t1"] * PAIR + bits["t0"]) * count + bits["s"]
    for name in ("y", "x", "core"):
        row = row * PAIR + bits[name]
    return row * rows + bits["r"]


def relative_columns(matrix, count, order):
    index = relative_index(matrix.shape[1], count, order)
    pick = jnp.arange(matrix.shape[1], dtype=jnp.int32)[:, None] == index[None, :]
    return linear(matrix, pick.astype(jnp.bfloat16)).astype(jnp.bfloat16)


def put_grads(pairs, outs):
    half, start = outs[0].shape[0], 0
    for left_ref, right in pairs:
        end = start + right.shape[1]
        for out_ref, lines in zip(outs, (slice(half, 2 * half), slice(0, half))):
            value = column_sum(left_ref[:, lines], right)
            out_ref[:, start:end] = value.astype(jnp.bfloat16)
        start = end
    return start


def total_rows(rows):
    return jnp.sum(rows.astype(jnp.float32), 0, keepdims=True)


def three_lefts_kernel(*refs):
    for rows_ref, out_ref in zip(refs[:3], refs[4:]):
        out_ref[...] = back_product(rows_ref, refs[3]).astype(jnp.bfloat16)


def three_lefts(attended, normed, crossed, pick):
    shape = jax.ShapeDtypeStruct(normed.shape, jnp.bfloat16)
    return small_kernel(three_lefts_kernel, [], [attended, normed, crossed, pick], [shape] * 3)


def three_kernel(
    out_left, query_left, cross_left, out_grads, query_blocks, cross_grads,
    sent_ref, kept_ref, sums_ref, columns_ref,
):
    rows = columns_ref.shape[0]
    for member in range(MEMBERS):
        columns_ref[:, member * WIDTH : (member + 1) * WIDTH] = query_blocks[
            member * rows : (member + 1) * rows, :
        ]
    pairs = [(out_left, out_grads), (query_left, columns_ref), (cross_left, cross_grads)]
    put_grads([(left, right[...]) for left, right in pairs], [sent_ref, kept_ref])
    sums_ref[...] = total_rows(columns_ref[...])


def three_grads(out_left, query_left, cross_left, out_grads, query_blocks, cross_grads):
    operands = [out_left, query_left, cross_left, out_grads, query_blocks, cross_grads]
    return pl.pallas_call(
        three_kernel,
        in_specs=in_vmem(6),
        out_specs=in_vmem(3),
        out_shape=[jax.ShapeDtypeStruct((D // 2, 3 * D), jnp.bfloat16)] * 2
        + [jax.ShapeDtypeStruct((1, D), jnp.float32)],
        scratch_shapes=[pltpu.VMEM(out_grads.shape, jnp.bfloat16)],
        compiler_params=pltpu.CompilerParams(vmem_limit_bytes=VMEM_LIMIT),
        cost_estimate=COST,
    )(*operands)


def encoder_kernel(
    me_ref, left_ref, weight_ref, *refs
):
    blocks, refs = refs[:MEMBERS], refs[MEMBERS:]
    sent_ref, kept_ref, first_ref, second_ref, sums_ref, grads_ref = refs
    join_kernel(2, me_ref, *blocks, grads_ref)
    put_grads([(left_ref, grads_ref[...])], [sent_ref, kept_ref])
    half = first_ref.shape[0]
    first_ref[...] = input_grad(grads_ref[:half, :], weight_ref[...]).astype(jnp.bfloat16)
    second_ref[...] = input_grad(grads_ref[half:, :], weight_ref[...]).astype(jnp.bfloat16)
    sums_ref[...] = total_rows(grads_ref[:, D:])


def encoder_grads(me, left, weight, blocks):
    rows = left.shape[0]
    return pl.pallas_call(
        encoder_kernel,
        in_specs=[pl.BlockSpec(memory_space=pltpu.SMEM)] + in_vmem(2 + MEMBERS),
        out_specs=in_vmem(5),
        out_shape=[jax.ShapeDtypeStruct((D // 2, 2 * D), jnp.bfloat16)] * 2
        + [jax.ShapeDtypeStruct((rows // 2, D), jnp.bfloat16)] * 2
        + [jax.ShapeDtypeStruct((1, D), jnp.float32)],
        scratch_shapes=[pltpu.VMEM((rows, 2 * D), jnp.bfloat16)],
        compiler_params=pltpu.CompilerParams(vmem_limit_bytes=VMEM_LIMIT),
        cost_estimate=COST,
    )(me, left, weight, *blocks)


def self_in_kernel(
    me_ref, left_ref, right_ref, pick_ref, one_ref, two_ref, three_ref, up_ref, query_ref,
    value_ref, *refs
):
    blocks, refs = refs[:MEMBERS], refs[MEMBERS:]
    left_sent, left_kept, right_sent, right_kept, grads_ref, small_ref = refs
    join_kernel(3, me_ref, *blocks, grads_ref)
    middle = grads_ref.shape[1] // 2
    put_grads([(left_ref, grads_ref[:, :middle])], [left_sent, left_kept])
    start = put_grads([(right_ref, grads_ref[:, middle:])], [right_sent, right_kept])

    small_ref[...] = jnp.zeros_like(small_ref)
    rows = [one_ref[0:1, :], two_ref[0:1, :], three_ref[0:1, :]]
    rows += [one_ref[1:2, :], two_ref[1:2, :], three_ref[1:2, :]]
    rows += [total_rows(grads_ref[:, :D]), total_rows(grads_ref[:, 2 * D :]), query_ref[...]]
    rows += [value_ref[...], two_ref[2:3, :], three_ref[2:3, :], one_ref[2:3, :]]
    for place, row in enumerate(rows):
        small_ref[place : place + 1, :] = row
    small_ref[13:17, :] = up_ref[...]
    half = right_sent.shape[0]
    low = small_ref[...].astype(jnp.bfloat16)
    for out_ref, lines in ((right_sent, slice(half, 2 * half)), (right_kept, slice(0, half))):
        out_ref[:, start:] = input_grad(pick_ref[lines, :], low).astype(jnp.bfloat16)


def self_in_grads(me, left, right, pick, one, two, three, up, query, value, blocks):
    rows = left.shape[0]
    half, middle = D // 2, 3 * D // 2
    outs = [jax.ShapeDtypeStruct((half, middle), jnp.bfloat16)] * 2
    outs += [jax.ShapeDtypeStruct((half, middle + 128), jnp.bfloat16)] * 2
    outs += [jax.ShapeDtypeStruct((rows, 3 * D), jnp.bfloat16)]
    operands = [left, right, pick, one, two, three, up.reshape(D, 4).T, query, value, *blocks]
    results = pl.pallas_call(
        self_in_kernel,
        in_specs=[pl.BlockSpec(memory_space=pltpu.SMEM)] + in_vmem(len(operands)),
        out_specs=in_vmem(len(outs)),
        out_shape=outs,
        scratch_shapes=[pltpu.VMEM((128, D), jnp.float32)],
        compiler_params=pltpu.CompilerParams(vmem_limit_bytes=VMEM_LIMIT),
        cost_estimate=COST,
    )(me, *operands)
    return results[:2], results[2:4], results[4]


class Halving:
    def __init__(self, parts, count, order):
        sent, self.value = parts
        self.count, self.order = count, list(order)
        self.send(sent)

    def send(self, block):
        self.sent = block.astype(jnp.bfloat16)
        self.pending = flip(self.sent, self.order.pop(0))

    def step(self):
        total = self.value.astype(jnp.float32) + self.pending.astype(jnp.float32)
        half = total.shape[0] // 2
        self.value = total[:half].astype(jnp.bfloat16)
        self.send(total[half:])

    def finish(self):
        total = self.value.astype(jnp.float32) + self.pending.astype(jnp.float32)
        if self.count > 1:
            total = lax.psum_scatter(
                total.astype(jnp.bfloat16), "s", scatter_dimension=0, tiled=True
            ).astype(jnp.float32)
        return total


def feed_grads_kernel(hidden_ref, grads_ref, rows_ref, active_grads_ref, out_ref):
    others, _, _, rows, _ = out_ref.shape

    @pl.when(pl.program_id(0) == 0)
    def _():
        value = column_sum(hidden_ref[...], grads_ref[...]).astype(jnp.bfloat16)
        value = value.reshape(PAIR, others, 4, rows, D)
        for y_index in range(PAIR):
            out_ref[:, y_index] = value[y_index]

    @pl.when(pl.program_id(0) == 1)
    def _():
        for part in range(4):
            value = column_sum(rows_ref[...], active_grads_ref[:, part * D : (part + 1) * D])
            value = value.astype(jnp.bfloat16).reshape(PAIR, others, rows, D)
            for y_index in range(PAIR):
                out_ref[:, y_index, part] = value[y_index]


def feed_grads(hidden, grads, rows, active_grads, count):
    blocks = 32 * count
    lines = D // blocks
    size = rows.shape[0]
    if count > 1:
        parts = [column_sum(hidden, grads).astype(jnp.bfloat16).reshape(-1, PAIR, 4, 4, lines, D)]
        for part in range(4):
            up = column_sum(rows, active_grads[:, part * D : (part + 1) * D])
            parts.append(up.astype(jnp.bfloat16).reshape(-1, PAIR, 4, 1, lines, D))
        return jnp.swapaxes(jnp.concatenate(parts, 3), 1, 2).reshape(-1, PAIR, 8, lines, D)
    return pl.pallas_call(
        feed_grads_kernel,
        grid=(2, T_SIZE),
        in_specs=[
            pl.BlockSpec((size, D), lambda p, i: (0, jnp.where(p == 0, i, T_SIZE - 1))),
            pl.BlockSpec((size, D), lambda p, i: (0, 0)),
            pl.BlockSpec((size, D // T_SIZE), lambda p, i: (0, jnp.where(p == 0, 0, i))),
            pl.BlockSpec((size, 4 * D), lambda p, i: (0, 0)),
        ],
        out_specs=pl.BlockSpec((4, PAIR, 4, lines, D), lambda p, i: (i, 0, p, 0, 0)),
        out_shape=jax.ShapeDtypeStruct((blocks // PAIR, PAIR, 8, lines, D), jnp.bfloat16),
        compiler_params=pltpu.CompilerParams(vmem_limit_bytes=VMEM_LIMIT),
        cost_estimate=COST,
    )(hidden, grads, rows, active_grads)


def reduce_feed(parts):
    return lax.psum_scatter(parts, ("t", "s", "x", "core"), scatter_dimension=0, tiled=True)[0]


def split_feed(halves):
    mine = lax.axis_index("y")
    return [
        lax.dynamic_index_in_dim(halves, place, 0, keepdims=False) for place in (mine, 1 - mine)
    ]


def merge_feed(kept, arrived):
    total = kept.astype(jnp.float32) + arrived.astype(jnp.float32)
    return jnp.concatenate([total[4 + part] for part in range(4)], 1), total[:4].reshape(-1, D)


def forward_kernel(
    chunk, flags_ref, q_ref, k_ref, v_ref, low_ref, high_ref, key_ref, out_ref, exact_ref, log_ref,
    masked_ref, top_ref, sum_ref, fade_ref, total_ref,
):
    step = pl.program_id(0)
    chunks = k_ref.shape[0] // chunk
    rows = q_ref.shape[0]
    lane = lax.broadcasted_iota(jnp.int32, (rows, 128), 1)
    for head in range(HEADS):
        pair = q_ref[:, (head // 2) * 128 : (head // 2 + 1) * 128] * SCALE
        masked_ref[head] = jnp.where((lane >= HD) == (head % 2 == 1), pair, 0).astype(jnp.bfloat16)
    top_ref[...] = jnp.full_like(top_ref, MASKED)
    sum_ref[...] = jnp.ones_like(sum_ref)
    sum_ref[:HEADS, :] = jnp.zeros((HEADS, rows), jnp.float32)
    fade_ref[...] = jnp.zeros_like(fade_ref)
    total_ref[...] = jnp.zeros_like(total_ref)

    def one_chunk(index, carry):
        @pl.when(flags_ref[step * chunks + index] != 0)
        def _():
            start = pl.multiple_of(index * chunk, chunk)
            here = pl.ds(start, chunk)
            keys = key_ref[here, :]
            allow = (keys >= low_ref[...]) & (keys <= high_ref[...])
            bias = jnp.where(allow, 0.0, MASKED)
            def pair_of(head):
                return slice((head // 2) * 128, (head // 2 + 1) * 128)

            scores = [
                lax.dot_general(
                    k_ref[here, pair_of(head)],
                    masked_ref[head],
                    (((1,), (1,)), ((), ())),
                    preferred_element_type=jnp.float32,
                ) + bias
                for head in range(HEADS)
            ]
            befores = [top_ref[head : head + 1, :] for head in range(HEADS)]
            afters = [
                jnp.maximum(before, jnp.max(score, 0, keepdims=True))
                for before, score in zip(befores, scores)
            ]
            exponents = [jnp.exp(score - after) for score, after in zip(scores, afters)]
            chances = [exponent.astype(jnp.bfloat16) for exponent in exponents]
            for head in range(HEADS):
                fade = jnp.exp(befores[head] - afters[head])
                top_ref[head : head + 1, :] = afters[head]
                fade_ref[head : head + 1, :] = fade
                sum_ref[head : head + 1, :] = sum_ref[head : head + 1, :] * fade + jnp.sum(
                    exponents[head], 0, keepdims=True
                )
            fades = fade_ref[...].T
            for head in range(HEADS):
                columns = slice((head // 2) * 128, (head // 2 + 1) * 128)
                total_ref[head] = total_ref[head] * fades[:, head : head + 1] + column_sum(
                    chances[head], v_ref[here, columns]
                )

        return carry

    lax.fori_loop(0, chunks, one_chunk, 0)
    shares = (1.0 / sum_ref[...]).T
    for head in range(0, HEADS, 2):
        columns = slice((head // 2) * 128, (head // 2 + 1) * 128)
        exact = jnp.where(
            lane < HD,
            total_ref[head] * shares[:, head : head + 1],
            total_ref[head + 1] * shares[:, head + 1 : head + 2],
        )
        exact_ref[:, columns] = exact
        out_ref[:, columns] = exact.astype(jnp.bfloat16)
    log_ref[:HEADS, :] = top_ref[:HEADS, :] + jnp.log(sum_ref[:HEADS, :])
    log_ref[HEADS:, :] = jnp.zeros((8 - HEADS, rows), jnp.float32)


def attend_forward(queries, keys, values, low, high, key_ids, flags, block, chunk):
    count, depth = queries[0].shape[0], keys[0].shape[0]
    whole = functools.partial(pl.BlockSpec, pipeline_mode=pl.Buffered(1))
    return pl.pallas_call(
        functools.partial(forward_kernel, chunk),
        grid_spec=pltpu.PrefetchScalarGridSpec(
            num_scalar_prefetch=1,
            grid=(count // block,),
            in_specs=[
                pl.BlockSpec((block, WIDTH), lambda i, f, c=queries[1]: (i, c)),
                whole((depth, WIDTH), lambda i, f, c=keys[1]: (0, c)),
                whole((depth, WIDTH), lambda i, f, c=values[1]: (0, c)),
                pl.BlockSpec((1, block), lambda i, f: (0, i)),
                pl.BlockSpec((1, block), lambda i, f: (0, i)),
                whole((depth, 1), lambda i, f: (0, 0)),
            ],
            out_specs=[
                pl.BlockSpec((block, WIDTH), lambda i, f: (i, 0)),
                pl.BlockSpec((block, WIDTH), lambda i, f: (i, 0)),
                pl.BlockSpec((8, block), lambda i, f: (0, i)),
            ],
            scratch_shapes=[
                pltpu.VMEM((HEADS, block, 128), jnp.bfloat16),
                pltpu.VMEM((8, block), jnp.float32),
                pltpu.VMEM((8, block), jnp.float32),
                pltpu.VMEM((8, block), jnp.float32),
                pltpu.VMEM((HEADS, block, 128), jnp.float32),
            ],
        ),
        out_shape=[
            jax.ShapeDtypeStruct((count, WIDTH), jnp.bfloat16),
            jax.ShapeDtypeStruct((count, WIDTH), jnp.float32),
            jax.ShapeDtypeStruct((8, count), jnp.float32),
        ],
        compiler_params=pltpu.CompilerParams(vmem_limit_bytes=VMEM_LIMIT),
        cost_estimate=COST,
    )(
        flags.reshape(-1), queries[0], keys[0], values[0], low[None, :], high[None, :],
        key_ids[:, None],
    )


def backward_kernel(
    chunk, flags_ref, places_ref, q_ref, k_ref, v_ref, g_ref, log_ref, exact_ref, low_ref, high_ref, key_ref,
    dq_ref, *refs,
):
    pair_refs, (q_masked, g_masked, delta_ref, turned_ref, dq_sum, dk_sum, dv_sum) = (
        refs[:-7], refs[-7:]
    )
    step = pl.program_id(0)
    chunks = k_ref.shape[0] // chunk
    rows = q_ref.shape[0]
    lane = lax.broadcasted_iota(jnp.int32, (rows, 128), 1)

    @pl.when(step == 0)
    def _():
        dk_sum[...] = jnp.zeros_like(dk_sum)
        dv_sum[...] = jnp.zeros_like(dv_sum)

        def turn(index, carry):
            start = pl.multiple_of(index * chunk, chunk)
            turned_ref[:, pl.ds(start, chunk)] = k_ref[pl.ds(start, chunk), :].T
            return carry

        lax.fori_loop(0, chunks, turn, 0)

    for head in range(HEADS):
        columns = slice((head // 2) * 128, (head // 2 + 1) * 128)
        chosen = (lane >= HD) == (head % 2 == 1)
        q_masked[head] = jnp.where(chosen, q_ref[:, columns] * SCALE, 0).astype(jnp.bfloat16)
        g_masked[head] = jnp.where(chosen, g_ref[:, columns], 0).astype(jnp.bfloat16)
    dq_sum[...] = jnp.zeros_like(dq_sum)
    members = lax.broadcasted_iota(jnp.int32, (8, WIDTH), 1) // HD
    members = (members == lax.broadcasted_iota(jnp.int32, (8, WIDTH), 0)).astype(jnp.float32)
    delta_ref[...] = lax.dot_general(
        members,
        g_ref[...].astype(jnp.float32) * exact_ref[...],
        (((1,), (1,)), ((), ())),
        precision=lax.Precision.HIGHEST,
        preferred_element_type=jnp.float32,
    )

    def one_chunk(index, carry):
        @pl.when(flags_ref[step * chunks + index] != 0)
        def _():
            start = pl.multiple_of(index * chunk, chunk)
            here = pl.ds(start, chunk)
            keys = key_ref[here, :]
            allow = (keys >= low_ref[...]) & (keys <= high_ref[...])
            bias = jnp.where(allow, 0.0, MASKED)

            def pair_of(head):
                return slice((head // 2) * 128, (head // 2 + 1) * 128)

            def against(keys_ref, head, masked):
                return lax.dot_general(
                    keys_ref[here, pair_of(head)],
                    masked[head],
                    (((1,), (1,)), ((), ())),
                    preferred_element_type=jnp.float32,
                )

            heads = range(HEADS)
            scores = [against(k_ref, head, q_masked) for head in heads]
            grads = [against(v_ref, head, g_masked) for head in heads]
            chances = [
                jnp.exp(scores[head] + bias - log_ref[head : head + 1, :]) for head in heads
            ]
            slopes = [
                (chances[head] * (grads[head] - delta_ref[head : head + 1, :])).astype(jnp.bfloat16)
                for head in heads
            ]
            chances = [chance.astype(jnp.bfloat16) for chance in chances]
            for head in heads:
                dv_sum[here, pair_of(head)] += linear(chances[head], g_masked[head])
            for head in heads:
                dk_sum[here, pair_of(head)] += linear(slopes[head], q_masked[head])
            for head in heads:
                lines = slice(head * HD, (head + 1) * HD)
                dq_sum[lines, :] += linear(turned_ref[lines, here], slopes[head])

        return carry

    lax.fori_loop(0, chunks, one_chunk, 0)
    dq_ref[...] = (dq_sum[...] * SCALE).T.astype(jnp.bfloat16)

    @pl.when(step == pl.num_programs(0) - 1)
    def _():
        for place, pair_ref in enumerate(pair_refs):
            size = pair_ref.shape[0] // 2
            for half in range(2):
                start = pl.multiple_of(places_ref[2 * place + half], 128)
                lines = slice(half * size, (half + 1) * size)
                pair_ref[lines, :WIDTH] = dk_sum[pl.ds(start, size), :].astype(jnp.bfloat16)
                pair_ref[lines, WIDTH:] = dv_sum[pl.ds(start, size), :].astype(jnp.bfloat16)


def attend_backward(
    queries, keys, values, grads, logs, exact, low, high, key_ids, flags, block, chunk, places
):
    splits = places.shape[0] // 2
    count, depth = queries[0].shape[0], keys[0].shape[0]
    whole = functools.partial(pl.BlockSpec, pipeline_mode=pl.Buffered(1))
    return pl.pallas_call(
        functools.partial(backward_kernel, chunk),
        grid_spec=pltpu.PrefetchScalarGridSpec(
            num_scalar_prefetch=2,
            grid=(count // block,),
            in_specs=[
                pl.BlockSpec((block, WIDTH), lambda i, f, p, c=queries[1]: (i, c)),
                whole((depth, WIDTH), lambda i, f, p, c=keys[1]: (0, c)),
                whole((depth, WIDTH), lambda i, f, p, c=values[1]: (0, c)),
                pl.BlockSpec((block, WIDTH), lambda i, f, p: (i, 0)),
                pl.BlockSpec((8, block), lambda i, f, p: (0, i)),
                pl.BlockSpec((block, WIDTH), lambda i, f, p: (i, 0)),
                pl.BlockSpec((1, block), lambda i, f, p: (0, i)),
                pl.BlockSpec((1, block), lambda i, f, p: (0, i)),
                whole((depth, 1), lambda i, f, p: (0, 0)),
            ],
            out_specs=[
                pl.BlockSpec((block, WIDTH), lambda i, f, p: (i, 0)),
            ]
            + [whole((depth // splits, 2 * WIDTH), lambda i, f, p: (0, 0))] * splits,
            scratch_shapes=[
                pltpu.VMEM((HEADS, block, 128), jnp.bfloat16),
                pltpu.VMEM((HEADS, block, 128), jnp.bfloat16),
                pltpu.VMEM((8, block), jnp.float32),
                pltpu.VMEM((WIDTH, depth), jnp.bfloat16),
                pltpu.VMEM((WIDTH, block), jnp.float32),
                pltpu.VMEM((depth, WIDTH), jnp.float32),
                pltpu.VMEM((depth, WIDTH), jnp.float32),
            ],
        ),
        out_shape=[
            jax.ShapeDtypeStruct((count, WIDTH), jnp.bfloat16),
        ]
        + [jax.ShapeDtypeStruct((depth // splits, 2 * WIDTH), jnp.bfloat16)] * splits,
        compiler_params=pltpu.CompilerParams(vmem_limit_bytes=VMEM_LIMIT),
        cost_estimate=COST,
    )(
        flags.reshape(-1), places, queries[0], keys[0], values[0], grads, logs, exact, low[None, :],
        high[None, :], key_ids[:, None],
    )


def needed_chunks(low, high, key_ids, block, chunk):
    first = jnp.min(low.reshape(-1, block), 1)[:, None]
    last = jnp.max(high.reshape(-1, block), 1)[:, None]
    smallest = jnp.min(key_ids.reshape(-1, chunk), 1)[None, :]
    largest = jnp.max(key_ids.reshape(-1, chunk), 1)[None, :]
    return ((largest >= first) & (smallest <= last)).astype(jnp.int32)


def on_device(
    count,
    tokens,
    encoder,
    seq_lengths,
    slot_ids,
    enc_lengths,
    cotangent,
    self_in,
    self_out,
    cross_query,
    cross_pair,
    cross_out,
    feed_up,
    feed_down,
    vectors,
    feed_bias,
    self_bias,
):

    full_self_in = fetch(self_in)
    facts = jnp.concatenate([slot_ids[0], seq_lengths[0], enc_lengths[0]], 1)
    slots = slot_ids.shape[2]
    facts_one, facts_two = to_packs(facts)
    tokens_in = jnp.concatenate(to_packs(tokens), 0)
    small = jnp.concatenate([vectors.T, feed_bias.reshape(D // 4, 4).T, self_bias[None, :]], 0)
    own_ids = jnp.concatenate([facts_one[:slots], facts_two[:slots]])
    ids = lax.all_gather(own_ids, GROUP, axis=0, tiled=True)
    ids, small = chain(ids, small)
    full_small = lax.all_gather(small, ("x", "core"), axis=1, tiled=True)
    vec = full_small[:12].astype(jnp.float32)
    bias_row = full_small[12:16].T.reshape(4 * D).astype(jnp.float32)
    self_bias_row = full_small[16].astype(jnp.float32)
    zero_row = jnp.zeros((D,), jnp.float32)
    facts_one, (self_out, cross_query) = chain(facts_one, (self_out, cross_query))
    full_out_query = fetch(jnp.concatenate([self_out, cross_query], 1))
    encoder_in = jnp.concatenate(to_packs(encoder), 0)
    tokens_in, (cross_pair, cross_out) = chain(tokens_in, (cross_pair, cross_out))
    full_cross_pair = fetch(cross_pair)
    full_cross_out = fetch(cross_out)

    lengths = facts_one[slots : slots + NSEQ]
    limits = facts_one[slots + NSEQ : slots + 2 * NSEQ]
    ends = jnp.cumsum(lengths)
    key_ids = gather_sequence(ids, count)
    rank = jnp.sum((ids[None, :] < ids[:, None]).astype(jnp.int32), 1)
    places = jnp.arange(ids.shape[0], dtype=jnp.int32)
    sorted_ids = jnp.sum(jnp.where(places[:, None] == rank[None, :], ids[None, :], 0), 1)
    key_order = gather_sequence(sorted_ids, count)
    seq_of = jnp.sum((sorted_ids[:, None] >= ends[None, :]).astype(jnp.int32), 1)
    starts = jnp.concatenate([jnp.zeros((1,), jnp.int32), ends[:-1]])
    picked = seq_of[:, None] == jnp.arange(NSEQ, dtype=jnp.int32)[None, :]
    self_low = jnp.sum(jnp.where(picked, starts[None, :], 0), 1)
    self_high = sorted_ids
    cross_low = seq_of * ENC
    cross_high = cross_low + jnp.sum(jnp.where(picked, limits[None, :], 0), 1) - 1
    enc_rows = encoder.shape[1]
    micro = lax.axis_index("t") & 1
    starts_of = []
    for index_s in range(count):
        for step in range(MEMBERS):
            core = lax.axis_index("core") ^ (step & 1)
            y_index = lax.axis_index("y") ^ (step >> 1)
            for part in range(2):
                t_index = 2 * core + (micro ^ part)
                starts_of.append(((t_index * count + index_s) * PAIR + y_index) * enc_rows)
    enc_places = jnp.stack(starts_of)
    enc_ids = jnp.arange(NSEQ * ENC, dtype=jnp.int32)
    if count > 1:
        enc_ids = (enc_places[:, None] + jnp.arange(enc_rows, dtype=jnp.int32)[None, :]).reshape(-1)
        enc_places = jnp.array([0, NSEQ * ENC // 2], jnp.int32)
    self_places = jnp.array([0, key_order.shape[0] // 2], jnp.int32)
    block = 256
    self_chunk, cross_chunk = 256, 512 if count == 1 else 384
    self_flags = needed_chunks(self_low, self_high, key_order, block, self_chunk)
    cross_flags = needed_chunks(cross_low, cross_high, enc_ids, block, cross_chunk)

    orders = {
        "x": ("core", "x", "y", "t0", "t1"),
        "y": ("core", "y", "x", "t0", "t1"),
    }

    def relative(matrix, name):
        return relative_columns(matrix, count, orders[name])

    qkv = project_heads(tokens_in, full_self_in, jnp.concatenate([vec[6], zero_row, vec[7]]))
    feed_own = stack_feed(feed_up, feed_down)
    own_heads = sort_rows(to_members(qkv), rank)
    if count > 1:
        pairs = gather_sequence(own_heads[:, WIDTH:], count)
        self_keys, self_values = (pairs, 0), (pairs, 1)
    else:
        self_keys, self_values = (own_heads, 1), (own_heads, 2)
    tokens_x, tokens_y = relative(tokens_in, "x"), relative(tokens_in, "y")
    encoder_y = relative(encoder_in, "y")
    index = relative_index(D, count, orders["y"])
    pick_y = (index[:, None] == jnp.arange(D, dtype=jnp.int32)[None, :]).astype(jnp.bfloat16)
    (tokens_x, tokens_y, encoder_y, pick_y, own_heads), (encoder_in, cotangent) = chain(
        (tokens_x, tokens_y, encoder_y, pick_y, own_heads), (encoder_in, cotangent)
    )
    grad_in = jnp.concatenate(to_packs(cotangent), 0)
    attended_heads, exact_self, log_self = attend_forward(
        (own_heads, 0), self_keys, self_values, self_low, self_high, key_order, self_flags,
        block, self_chunk,
    )
    attended_heads, feed_own = chain(attended_heads, feed_own)
    feed_far = lax.ppermute(feed_own, "x", SWAP)
    enc_pairs = project_blocks(
        encoder_in, full_cross_pair, jnp.concatenate([zero_row, vec[9]])
    )
    attended = to_members(unsort_rows([attended_heads], rank))
    attended, enc_pairs = chain(attended, enc_pairs)
    if count == 1:
        enc_heads = assemble(exchange(enc_pairs), enc_places)
    else:
        enc_heads = gather_sequence(jnp.concatenate(exchange(enc_pairs), 0), count)
    normed_one, normed_one_low, unit_one, inverse_one, cross_queries = project_norm(
        by_member(attended), full_out_query, self_bias_row, tokens_in, vec[0], vec[3],
        after=(vec[8],),
    )
    cross_heads = sort_rows(to_members(cross_queries), rank)
    crossed_heads, exact_cross, log_cross = attend_forward(
        (cross_heads, 0), (enc_heads, 0), (enc_heads, 1), cross_low, cross_high, enc_ids,
        cross_flags, block, cross_chunk,
    )
    cross_heads, (feed_own, full_cross_out) = chain(cross_heads, (feed_own, full_cross_out))
    feed_near = lax.ppermute(feed_own, "core", SWAP)
    crossed_heads, grad_in = chain(crossed_heads, grad_in)
    crossed = to_members(unsort_rows([crossed_heads], rank))
    crossed, feed_far = chain(crossed, feed_far)
    feed_shards = [feed_own, feed_near, feed_far, lax.ppermute(feed_far, "core", SWAP)]
    normed_two, normed_two_low, unit_two, inverse_two = project_norm(
        by_member(crossed), full_cross_out, vec[10], normed_one, vec[1], vec[4]
    )
    slope, hidden = feed_up_gelu(normed_two_low, feed_shards, bias_row)
    layer_low, grad_three, grad_branch, sums_three = feed_down_norm(
        hidden, feed_shards, vec[11], normed_two, vec[2], vec[5], grad_in
    )
    half = tokens_in.shape[0] // 2

    grad_pre, bias_up, grad_two, grad_crossed_out, sums_two, grad_crossed = feed_back(
        slope, feed_shards, grad_branch, grad_three, unit_two, inverse_two, vec[1],
        full_cross_out,
    )
    received, (feed_parts, layer_low) = during_members(
        grad_crossed, lambda layer, *rows: (feed_grads(*rows, count), layer),
        (layer_low, hidden, grad_branch, normed_two_low, grad_pre),
    )
    layer_out = from_packs(layer_low[:half], layer_low[half:])
    feed_sum = reduce_feed(feed_parts)
    grad_crossed_heads = sort_rows(received, rank)
    dq_heads, *enc_pair_grads = attend_backward(
        (cross_heads, 0), (enc_heads, 0), (enc_heads, 1), grad_crossed_heads, log_cross,
        exact_cross, cross_low, cross_high, enc_ids, cross_flags, block, cross_chunk, enc_places,
    )
    layer_out, dq_heads = chain(layer_out, dq_heads)
    if count > 1:
        enc_pair_grads = cut(scatter_sequence(enc_pair_grads[0], count))
    dq_blocks, (enc_pair_grads, lefts) = during_members(
        unsort_rows([dq_heads], rank),
        lambda pairs, *rows: (pairs, three_lefts(*rows, pick_y)),
        (enc_pair_grads, by_member(attended), normed_one_low, by_member(crossed)),
    )
    enc_blocks = exchange(enc_pair_grads)
    grad_one, grad_attended_out, sums_one, grad_attended = back_norm(
        by_member(dq_blocks), full_out_query, grad_two, unit_one, inverse_one, vec[0]
    )

    received, (*three_parts, query_sums) = during_members(
        grad_attended,
        lambda blocks: three_grads(
            *lefts, grad_attended_out, blocks, grad_crossed_out
        ),
        (dq_blocks,),
    )
    three_sum = Halving(three_parts, count, orders["y"])
    grad_attended_heads = sort_rows(received, rank)
    dq_heads, pair_heads = attend_backward(
        (own_heads, 0), self_keys, self_values, grad_attended_heads, log_self, exact_self,
        self_low, self_high, key_order, self_flags, block, self_chunk, self_places,
    )
    pair_heads = scatter_sequence(pair_heads, count)

    dq_heads, three_sum.pending = chain(dq_heads, three_sum.pending)
    three_sum.step()
    dq_heads, three_sum.value = chain(dq_heads, three_sum.value)

    blocks, (me, enc_blocks) = chain(
        unsort_blocks([dq_heads, pair_heads], rank), (group_index()[None], enc_blocks)
    )
    received = exchange(blocks)
    *pair_parts, enc_first, enc_rest, value_sums = encoder_grads(
        me, encoder_y, full_cross_pair, enc_blocks
    )
    (pair_parts, enc_first, enc_rest), received = chain((pair_parts, enc_first, enc_rest), received)
    pair_sum = Halving(pair_parts, count, orders["y"])
    enc_first = send_back(enc_first, 0)
    left_parts, right_parts, grad_qkv = self_in_grads(
        group_index()[None], tokens_x, tokens_y, pick_y, sums_one, sums_two, sums_three, bias_up,
        query_sums, value_sums, received,
    )
    left_sum = Halving(left_parts, count, orders["x"])
    right_sum = Halving(right_parts, count, orders["y"])
    def steps(last, *halvings):
        for halving in halvings:
            last.value, halving.pending = chain(last.value, halving.pending)
            halving.step()
            last = halving
        return last

    last = right_sum
    last.value, grad_qkv = chain(last.value, grad_qkv)
    grad_rows = back_project(grad_qkv, full_self_in, grad_one)
    last.value, grad_rows = chain(last.value, grad_rows)
    last = steps(last, left_sum, right_sum, pair_sum, three_sum)
    last.value, (enc_first, enc_rest) = chain(last.value, (enc_first, enc_rest))
    enc_second = send_back(enc_rest, 1)
    last = steps(last, right_sum, left_sum, pair_sum)
    last.value, feed_sum = chain(last.value, feed_sum)
    feed_kept, feed_sent = split_feed(feed_sum)
    feed_arrived = flip(feed_sent, "y")
    last = steps(last, three_sum)
    last.value, enc_second = chain(last.value, enc_second)
    last = steps(last, right_sum)
    last.value, rows_first = chain(last.value, grad_rows[:half])
    rows_first = send_back(rows_first, 0)
    last = steps(last, left_sum, three_sum)
    last.value, (rows_first, rows_second) = chain(last.value, (rows_first, grad_rows[half:]))
    rows_second = send_back(rows_second, 1)
    last = steps(last, pair_sum)
    last.value, feed_arrived = chain(last.value, feed_arrived)
    last = steps(last, right_sum, left_sum, pair_sum)
    grad_encoder = order_back(enc_first, enc_second)
    grad_tokens = order_back(rows_first, rows_second).astype(jnp.float32)
    three, pair = three_sum.finish(), pair_sum.finish()
    left, right = left_sum.finish(), right_sum.finish()
    up_sum, down_sum = merge_feed(feed_kept, feed_arrived)
    small = right[:, 3 * D // 2 :]
    return (
        layer_out,
        grad_tokens,
        grad_encoder.astype(jnp.float32),
        jnp.concatenate([left, right[:, : 3 * D // 2]], 1),
        three[:, :D],
        three[:, D : 2 * D],
        pair,
        three[:, 2 * D :],
        up_sum,
        down_sum,
        small[:, :12],
        small[:, 13:17].reshape(-1),
        small[:, 12],
    )


def solution(mesh):
    contexts = mesh.shape["ctx"]
    count = contexts // (T_SIZE * PAIR)
    fine = Mesh(
        mesh.devices.reshape(T_SIZE, count, PAIR, PAIR, PAIR), ("t", "s", "y", "x", "core")
    )
    fsdp, ctx = ("x", "core"), ("t", "s", "y")
    in_specs = (
        P(None, ROWS, None),
        P(None, ROWS, None),
        P(fsdp, None, None),
        P(fsdp, None, ctx),
        P(fsdp, None, None),
        P(None, ROWS, None),
        P(fsdp, None),
        P(fsdp, None),
        P(fsdp, None),
        P(fsdp, None),
        P(fsdp, None),
        P(fsdp, None),
        P(fsdp, None),
        P(fsdp, None),
        P(fsdp),
        P(fsdp),
    )
    out_specs = (P(None, ROWS, None),) * 3 + (P(BLOCKS, None),) * 8 + (P(BLOCKS),) * 2
    return jax.shard_map(
        functools.partial(on_device, count),
        mesh=fine,
        in_specs=in_specs,
        out_specs=out_specs,
        check_vma=False,
    )
```

```python
import functools

import jax
import jax.numpy as jnp
from jax import lax
from jax.experimental import pallas as pl
from jax.experimental.pallas import tpu as pltpu
from jax.sharding import Mesh
from jax.sharding import PartitionSpec as P

D = 1024
HD = 64
ENC = 1024
NSEQ = 3
MICRO = 2
DEPTH = 6

EPSILON = 1e-05
MASKED = -1e30
SCALE = HD ** (-0.5)
T_SIZE = 4
PAIR = 2
GROUP = ("y", "core")
ROWS = ("x", "core", "t", "s", "y")
BLOCKS = ("t", "s", "y", "x", "core")
MEMBERS = 4
WIDTH = D // MEMBERS
HEADS = WIDTH // HD
VMEM_LIMIT = 56 * 1024 * 1024
RESIDUAL = (3.0 * DEPTH) ** 0.25
COST = pl.CostEstimate(flops=0, bytes_accessed=0, transcendentals=0)


def norm_forward(resid, gain, offset):
    average = jnp.mean(resid, -1, keepdims=True)
    centered = resid - average
    inverse = lax.rsqrt(jnp.mean(centered * centered, -1, keepdims=True) + EPSILON)
    normed = centered * inverse
    return (normed * gain + offset, normed, inverse)


def norm_backward(grad_out, normed, inverse, gain):
    grad_normed = grad_out * gain
    first_mean = jnp.mean(grad_normed, -1, keepdims=True)
    second_mean = jnp.mean(grad_normed * normed, -1, keepdims=True)
    grad_resid = inverse * (grad_normed - first_mean - normed * second_mean)
    return (grad_resid, jnp.sum(grad_out * normed, 0), jnp.sum(grad_out, 0))


def column_sum(left, right):
    return lax.dot_general(
        left, right, (((0,), (0,)), ((), ())), preferred_element_type=jnp.float32
    )


def input_grad(grad_rows, weight):
    return lax.dot_general(
        grad_rows, weight, (((1,), (1,)), ((), ())), preferred_element_type=jnp.float32
    )


def linear(inputs, weight):
    return jnp.dot(inputs, weight, preferred_element_type=jnp.float32)


def pack_routes():
    straight, crossed = [], []
    for t in range(T_SIZE):
        for core in range(PAIR):
            here = t * PAIR + core
            straight.append((here, (2 * core + (t & 1)) * PAIR + (t >> 1)))
            crossed.append((here, (2 * core + 1 - (t & 1)) * PAIR + (t >> 1)))
    return straight, crossed


def to_packs(parts):
    straight, crossed = pack_routes()
    parity = lax.axis_index("t") & 1
    first = lax.dynamic_index_in_dim(parts, parity, 0, keepdims=False)
    second = lax.dynamic_index_in_dim(parts, 1 - parity, 0, keepdims=False)
    return (
        lax.ppermute(first, ("t", "core"), straight),
        lax.ppermute(second, ("t", "core"), crossed),
    )


def send_back(part, place):
    route = pack_routes()[place]
    return lax.ppermute(part, ("t", "core"), [(to, source) for source, to in route])


def order_back(first, second):
    parity = lax.axis_index("t") & 1
    return jnp.stack(
        [jnp.where(parity == 0, first, second), jnp.where(parity == 0, second, first)], 0
    )


def from_packs(first, second):
    return order_back(send_back(first, 0), send_back(second, 1))


def group_route(step):
    return [(member, member ^ step) for member in range(MEMBERS)]


def group_index():
    return lax.axis_index("y") * PAIR + lax.axis_index("core")


def join_kernel(parts, me_ref, *refs):
    matrix_ref = refs[-1]
    for step, block_ref in enumerate(refs[:-1]):
        for part in range(parts):
            start = pl.multiple_of(part * D + (me_ref[0] ^ step) * WIDTH, WIDTH)
            matrix_ref[:, pl.ds(start, WIDTH)] = block_ref[:, part * WIDTH : (part + 1) * WIDTH]


def join_members_kernel(blocks_ref, matrix_ref):
    rows = matrix_ref.shape[0]
    for member in range(MEMBERS):
        for part in range(matrix_ref.shape[1] // D):
            start = part * D + member * WIDTH
            matrix_ref[:, start : start + WIDTH] = blocks_ref[
                member * rows : (member + 1) * rows, part * WIDTH : (part + 1) * WIDTH
            ]


def in_vmem(count):
    return [pl.BlockSpec(memory_space=pltpu.VMEM)] * count


def small_kernel(body, scalars, operands, outs, work=0):
    return pl.pallas_call(
        body,
        in_specs=[pl.BlockSpec(memory_space=pltpu.SMEM)] * len(scalars) + in_vmem(len(operands)),
        out_specs=in_vmem(len(outs)),
        out_shape=outs,
        compiler_params=pltpu.CompilerParams(vmem_limit_bytes=VMEM_LIMIT),
        cost_estimate=COST,
    )(*scalars, *operands)


def fetch(weight):
    return lax.all_gather(weight, ("x", "core"), axis=0, tiled=True)


SWAP = [(0, 1), (1, 0)]


def stack_feed(up, down):
    return jnp.concatenate([down] + [up[:, part * D : (part + 1) * D] for part in range(4)], 0)


def up_specs(column):
    def block(i, p):
        place = column(i, p)
        return (MEMBERS + place // 2, place % 2)

    return [pl.BlockSpec((D // MEMBERS, FEED_TILE), block)] * MEMBERS


def shard_index():
    return (lax.axis_index("x") * PAIR + lax.axis_index("core"))[None]


def product(rows_ref, weight_ref, start=0, width=None):
    columns = slice(start, weight_ref.shape[1] if width is None else start + width)
    if len(rows_ref.shape) == 2:
        return linear(rows_ref[...], weight_ref[:, columns])
    total = None
    for member in range(MEMBERS):
        lines = slice(member * WIDTH, (member + 1) * WIDTH)
        term = linear(rows_ref[member], weight_ref[lines, columns])
        total = term if total is None else total + term
    return total


def back_product(grads_ref, weight_ref, lines=slice(None), offset=0):
    if len(grads_ref.shape) == 2:
        return input_grad(
            grads_ref[...], weight_ref[lines, offset : offset + grads_ref.shape[1]]
        )
    total = None
    for member in range(MEMBERS):
        columns = slice(offset + member * WIDTH, offset + (member + 1) * WIDTH)
        term = input_grad(grads_ref[member], weight_ref[lines, columns])
        total = term if total is None else total + term
    return total


def put_heads(rows_ref, weight_ref, bias_ref, out_ref, offset=0):
    count = out_ref.shape[0] // MEMBERS
    for member in range(MEMBERS):
        for part in range(out_ref.shape[1] // WIDTH):
            start = part * D + member * WIDTH
            value = product(rows_ref, weight_ref, offset + start, WIDTH)
            value = value + bias_ref[:, start : start + WIDTH]
            out_ref[
                member * count : (member + 1) * count, part * WIDTH : (part + 1) * WIDTH
            ] = value.astype(jnp.bfloat16)


def put_back_heads(grads_ref, weight_ref, out_ref):
    count = out_ref.shape[0] // MEMBERS
    for member in range(MEMBERS):
        value = back_product(grads_ref, weight_ref, slice(member * WIDTH, (member + 1) * WIDTH))
        out_ref[member * count : (member + 1) * count, :] = value.astype(jnp.bfloat16)


def heads_kernel(rows_ref, weight_ref, bias_ref, out_ref):
    put_heads(rows_ref, weight_ref, bias_ref, out_ref)


def project_heads(rows, weight, bias):
    shape = jax.ShapeDtypeStruct((rows.shape[0] * MEMBERS, weight.shape[1] // MEMBERS), jnp.bfloat16)
    return small_kernel(heads_kernel, [], [rows, weight, bias[None, :]], [shape])[0]


def own_heads_kernel(me_ref, rows_ref, weight_ref, bias_ref, *outs):
    for step, out_ref in reversed(list(enumerate(outs))):
        for part in range(out_ref.shape[1] // WIDTH):
            start = pl.multiple_of(part * D + (me_ref[0] ^ step) * WIDTH, WIDTH)
            value = linear(rows_ref[...], weight_ref[:, pl.ds(start, WIDTH)])
            value = value + bias_ref[:, pl.ds(start, WIDTH)]
            out_ref[:, part * WIDTH : (part + 1) * WIDTH] = value.astype(jnp.bfloat16)


def project_blocks(rows, weight, bias):
    shape = jax.ShapeDtypeStruct((rows.shape[0], weight.shape[1] // MEMBERS), jnp.bfloat16)
    work = 2 * rows.shape[0] * weight.size
    return small_kernel(
        own_heads_kernel, [group_index()[None]], [rows, weight, bias[None, :]], [shape] * MEMBERS,
        work,
    )


def norm_kernel(
    rows_ref, weight_ref, bias_ref, base_ref, gain_ref, offset_ref, *refs
):
    outs = refs if len(refs) == 4 else refs[1:]
    resid = (
        RESIDUAL * base_ref[...].astype(jnp.float32)
        + product(rows_ref, weight_ref, 0, D)
        + bias_ref[...]
    )
    normed, unit, inverse = norm_forward(resid, gain_ref[...], offset_ref[...])
    outs[0][...] = normed
    outs[1][...] = normed.astype(jnp.bfloat16)
    outs[2][...] = unit
    outs[3][...] = inverse
    if len(refs) > 4:
        put_heads(outs[1], weight_ref, refs[0], outs[4], D)


def project_norm(rows, weight, bias, base, gain, offset, after=()):
    count = base.shape[0]
    outs = [
        jax.ShapeDtypeStruct((count, D), jnp.float32),
        jax.ShapeDtypeStruct((count, D), jnp.bfloat16),
        jax.ShapeDtypeStruct((count, D), jnp.float32),
        jax.ShapeDtypeStruct((count, 1), jnp.float32),
    ]
    if after:
        outs.append(jax.ShapeDtypeStruct((count * MEMBERS, WIDTH), jnp.bfloat16))
    return small_kernel(
        norm_kernel, [],
        [rows, weight, bias[None, :], base, gain[None, :], offset[None, :]]
        + [row[None, :] for row in after],
        outs,
    )


FEED_TILE = 512


def feed_column(step, me, tiles):
    return (me ^ (step // tiles)) * tiles + step % tiles


def up_kernel(me_ref, rows_ref, *refs):
    shards, (bias_ref, slope_ref, hidden_ref) = refs[:MEMBERS], refs[MEMBERS:]
    depth = shards[0].shape[0]
    active = bias_ref[...]
    for index, shard in enumerate(shards):
        start = pl.multiple_of((me_ref[0] ^ index) * depth, depth)
        active = active + linear(rows_ref[:, pl.ds(start, depth)], shard[...])
    cumulative = 0.5 * (1.0 + lax.erf(active * 0.7071067811865476))
    density = jnp.exp(-0.5 * active * active) * 0.3989422804014327
    slope_ref[...] = cumulative + active * density
    hidden_ref[...] = (active * cumulative).astype(jnp.bfloat16)


def feed_up_gelu(rows, shards, bias):
    count, width = rows.shape[0], 4 * D
    column = lambda i, p: (0, i)
    return pl.pallas_call(
        up_kernel,
        grid_spec=pltpu.PrefetchScalarGridSpec(
            num_scalar_prefetch=1,
            grid=(width // FEED_TILE,),
            in_specs=[pl.BlockSpec((count, D), lambda i, p: (0, 0))]
            + up_specs(lambda i, p: i)
            + [pl.BlockSpec((1, FEED_TILE), column)],
            out_specs=[pl.BlockSpec((count, FEED_TILE), column)] * 2,
        ),
        out_shape=[
            jax.ShapeDtypeStruct((count, width), jnp.float32),
            jax.ShapeDtypeStruct((count, width), jnp.bfloat16),
        ],
        compiler_params=pltpu.CompilerParams(vmem_limit_bytes=VMEM_LIMIT),
        cost_estimate=COST,
    )(shard_index(), rows, *shards, bias[None, :])


def put_norm_back(grads, unit, inverse, gain, resid_ref, low_ref, sums_ref):
    resid, gain_sum, offset_sum = norm_backward(grads, unit, inverse, gain)
    low = resid.astype(jnp.bfloat16)
    resid_ref[...] = resid
    low_ref[...] = low
    sums_ref[0:1, :] = gain_sum[None, :]
    sums_ref[1:2, :] = offset_sum[None, :]
    sums_ref[2:3, :] = jnp.sum(low.astype(jnp.float32), 0)[None, :]
    sums_ref[3:8, :] = jnp.zeros((5, D), jnp.float32)


def down_kernel(tiles, me_ref, hidden_ref, *refs):
    shards = refs[:MEMBERS]
    bias_ref, base_ref, gain_ref, offset_ref, grads_ref = refs[MEMBERS : MEMBERS + 5]
    layer_ref, resid_ref, low_ref, sums_ref, total_ref = refs[MEMBERS + 5 :]
    step = pl.program_id(0)

    @pl.when(step == 0)
    def _():
        total_ref[...] = RESIDUAL * base_ref[...] + bias_ref[...]

    for index, shard in enumerate(shards):

        @pl.when(step // tiles == index)
        def _(shard=shard):
            total_ref[...] += linear(hidden_ref[...], shard[...])

    @pl.when(step == pl.num_programs(0) - 1)
    def _():
        layer, unit, inverse = norm_forward(total_ref[...], gain_ref[...], offset_ref[...])
        layer_ref[...] = layer.astype(jnp.bfloat16)
        put_norm_back(
            grads_ref[...].astype(jnp.float32), unit, inverse, gain_ref[...], resid_ref, low_ref,
            sums_ref,
        )


def one_block(array):
    return pl.BlockSpec(array.shape, lambda i, p: (0,) * len(array.shape))


def down_specs(tiles):
    return [
        pl.BlockSpec((FEED_TILE, D), lambda i, p, s=s: (jnp.clip(i - s * tiles, 0, tiles - 1), 0))
        for s in range(MEMBERS)
    ]


def feed_down_norm(hidden, shards, bias, base, gain, offset, grads):
    count = base.shape[0]
    tiles = D // FEED_TILE
    fixed = [bias[None, :], base, gain[None, :], offset[None, :], grads]
    outs = [
        jax.ShapeDtypeStruct((count, D), jnp.bfloat16),
        jax.ShapeDtypeStruct((count, D), jnp.float32),
        jax.ShapeDtypeStruct((count, D), jnp.bfloat16),
        jax.ShapeDtypeStruct((8, D), jnp.float32),
    ]
    return pl.pallas_call(
        functools.partial(down_kernel, tiles),
        grid_spec=pltpu.PrefetchScalarGridSpec(
            num_scalar_prefetch=1,
            grid=(MEMBERS * tiles,),
            in_specs=[
                pl.BlockSpec((count, FEED_TILE), lambda i, p: (0, feed_column(i, p[0], tiles)))
            ]
            + down_specs(tiles)
            + [one_block(array) for array in fixed],
            out_specs=[one_block(out) for out in outs],
            scratch_shapes=[pltpu.VMEM((count, D), jnp.float32)],
        ),
        out_shape=outs,
        compiler_params=pltpu.CompilerParams(vmem_limit_bytes=VMEM_LIMIT),
        cost_estimate=COST,
    )(shard_index(), hidden, *shards, *fixed)


def feed_back_kernel(tiles, me_ref, slope_ref, *refs):
    downs, ups, refs = refs[:MEMBERS], refs[MEMBERS : 2 * MEMBERS], refs[2 * MEMBERS :]
    grads_ref, resid_ref, unit_ref, inverse_ref, gain_ref, out_ref = refs[:6]
    du_ref, bias_ref, next_resid_ref, next_low_ref, sums_ref, heads_ref, total_ref = refs[6:]
    step = pl.program_id(0)
    depth = ups[0].shape[0]

    @pl.when(step == 0)
    def _():
        total_ref[...] = RESIDUAL * resid_ref[...]

    slope = slope_ref[...]
    for index, shard in enumerate(downs):

        @pl.when(step // tiles == index)
        def _(shard=shard):
            du_ref[...] = (back_product(grads_ref, shard) * slope).astype(jnp.bfloat16)

    du = du_ref[...]
    bias_ref[...] = jnp.sum(du.astype(jnp.float32), 0, keepdims=True)
    for index, shard in enumerate(ups):
        start = pl.multiple_of((me_ref[0] ^ index) * depth, depth)
        total_ref[:, pl.ds(start, depth)] += input_grad(du, shard[...])

    @pl.when(step == pl.num_programs(0) - 1)
    def _():
        put_norm_back(
            total_ref[...], unit_ref[...], inverse_ref[...], gain_ref[...], next_resid_ref,
            next_low_ref, sums_ref,
        )
        put_back_heads(next_low_ref, out_ref, heads_ref)


def feed_back(slope, shards, grads, resid, unit, inverse, gain, out_weight):
    count, width = slope.shape
    tiles = D // FEED_TILE
    fixed = [grads, resid, unit, inverse, gain[None, :], out_weight]
    column = lambda i, p: (0, feed_column(i, p[0], tiles))
    outs = [
        jax.ShapeDtypeStruct((count, width), jnp.bfloat16),
        jax.ShapeDtypeStruct((1, width), jnp.float32),
        jax.ShapeDtypeStruct((count, D), jnp.float32),
        jax.ShapeDtypeStruct((count, D), jnp.bfloat16),
        jax.ShapeDtypeStruct((8, D), jnp.float32),
        jax.ShapeDtypeStruct((count * MEMBERS, WIDTH), jnp.bfloat16),
    ]
    return pl.pallas_call(
        functools.partial(feed_back_kernel, tiles),
        grid_spec=pltpu.PrefetchScalarGridSpec(
            num_scalar_prefetch=1,
            grid=(MEMBERS * tiles,),
            in_specs=[pl.BlockSpec((count, FEED_TILE), column)]
            + down_specs(tiles)
            + up_specs(lambda i, p: feed_column(i, p[0], tiles))
            + [one_block(array) for array in fixed],
            out_specs=[
                pl.BlockSpec((count, FEED_TILE), column), pl.BlockSpec((1, FEED_TILE), column)
            ]
            + [one_block(out) for out in outs[2:]],
            scratch_shapes=[pltpu.VMEM((count, D), jnp.float32)],
        ),
        out_shape=outs,
        compiler_params=pltpu.CompilerParams(vmem_limit_bytes=VMEM_LIMIT),
        cost_estimate=COST,
    )(shard_index(), slope, *shards, *shards, *fixed)


def norm_back_kernel(
    grads_ref, weight_ref, resid_ref, unit_ref, inverse_ref, gain_ref,
    next_resid_ref, next_low_ref, sums_ref, heads_ref,
):
    total = RESIDUAL * resid_ref[...] + back_product(grads_ref, weight_ref, offset=D)
    put_norm_back(
        total, unit_ref[...], inverse_ref[...], gain_ref[...], next_resid_ref, next_low_ref, sums_ref
    )
    put_back_heads(next_low_ref, weight_ref, heads_ref)


def back_norm(grads, weight, resid, unit, inverse, gain):
    count = resid.shape[0]
    outs = [
        jax.ShapeDtypeStruct((count, D), jnp.float32),
        jax.ShapeDtypeStruct((count, D), jnp.bfloat16),
        jax.ShapeDtypeStruct((8, D), jnp.float32),
        jax.ShapeDtypeStruct((count * MEMBERS, WIDTH), jnp.bfloat16),
    ]
    return small_kernel(
        norm_back_kernel, [], [grads, weight, resid, unit, inverse, gain[None, :]], outs
    )


def back_kernel(grads_ref, weight_ref, resid_ref, out_ref):
    value = RESIDUAL * resid_ref[...] + back_product(grads_ref, weight_ref)
    out_ref[...] = value.astype(out_ref.dtype)


def back_project(grads, weight, resid):
    count, width = grads.shape
    rows = 256
    return pl.pallas_call(
        back_kernel,
        grid=(weight.shape[0] // rows,),
        in_specs=[
            pl.BlockSpec((count, width), lambda i: (0, 0)),
            pl.BlockSpec((rows, width), lambda i: (i, 0)),
            pl.BlockSpec((count, rows), lambda i: (0, i)),
        ],
        out_specs=pl.BlockSpec((count, rows), lambda i: (0, i)),
        out_shape=jax.ShapeDtypeStruct((count, weight.shape[0]), jnp.bfloat16),
        compiler_params=pltpu.CompilerParams(vmem_limit_bytes=VMEM_LIMIT),
        cost_estimate=COST,
    )(grads, weight, resid)


def to_members(blocks):
    return lax.all_to_all(blocks, GROUP, 0, 0, tiled=True)


def by_member(blocks):
    return blocks.reshape(MEMBERS, blocks.shape[0] // MEMBERS, blocks.shape[1])


def as_columns(blocks):
    shape = (blocks.shape[0] // MEMBERS, blocks.shape[1] * MEMBERS)
    return small_kernel(
        join_members_kernel, [], [blocks], [jax.ShapeDtypeStruct(shape, blocks.dtype)]
    )[0]


def chain(first, second):
    return lax.optimization_barrier((first, second))


def exchange(blocks):
    return [
        block if step == 0 else lax.ppermute(block, GROUP, group_route(step))
        for step, block in enumerate(blocks)
    ]


def during_members(blocks, work, inputs):
    blocks, inputs = chain(blocks, inputs)
    results, received = chain(work(*inputs), to_members(blocks))
    return received, results


def cut(matrix):
    rows = matrix.shape[0] // MEMBERS
    return [matrix[step * rows : (step + 1) * rows] for step in range(MEMBERS)]


def sort_kernel(rank_ref, blocks_ref, sorted_ref):
    rows = blocks_ref.shape[0] // MEMBERS
    for place in range(MEMBERS):
        wanted = lax.broadcasted_iota(jnp.int32, (rows, rows * MEMBERS), 0) + place * rows
        pick = (rank_ref[...] == wanted).astype(jnp.bfloat16)
        sorted_ref[place * rows : (place + 1) * rows, :] = linear(pick, blocks_ref[...]).astype(
            jnp.bfloat16
        )


def put_unsorted(ranks, parts, block_ref, lines):
    rows = ranks.shape[0]
    wanted = lax.broadcasted_iota(jnp.int32, (rows, rows * MEMBERS), 1)
    pick = (ranks == wanted).astype(jnp.bfloat16)
    start = 0
    for sorted_ref in parts:
        end = start + sorted_ref.shape[1]
        block_ref[lines, start:end] = linear(pick, sorted_ref[...]).astype(jnp.bfloat16)
        start = end


def unsort_kernel(rank_ref, *refs):
    blocks_ref = refs[-1]
    rows = blocks_ref.shape[0] // MEMBERS
    for member in range(MEMBERS):
        lines = slice(member * rows, (member + 1) * rows)
        put_unsorted(rank_ref[lines, :], refs[:-1], blocks_ref, lines)


def unsort_blocks_kernel(me_ref, rank_ref, *refs):
    for step, block_ref in enumerate(refs[-MEMBERS:]):
        rows = block_ref.shape[0]
        start = pl.multiple_of((me_ref[0] ^ step) * rows, rows)
        put_unsorted(rank_ref[pl.ds(start, rows), :], refs[:-MEMBERS], block_ref, slice(None))


def unsort_blocks(parts, rank):
    rows, width = parts[0].shape[0] // MEMBERS, sum(part.shape[1] for part in parts)
    shape = jax.ShapeDtypeStruct((rows, width), jnp.bfloat16)
    return small_kernel(
        unsort_blocks_kernel, [group_index()[None]], [rank[:, None], *parts], [shape] * MEMBERS
    )


def sort_rows(blocks, rank):
    shape = jax.ShapeDtypeStruct(blocks.shape, jnp.bfloat16)
    work = 2 * blocks.size * blocks.shape[0]
    return small_kernel(sort_kernel, [], [rank[None, :], blocks], [shape], work)[0]


def unsort_rows(parts, rank):
    width = sum(part.shape[1] for part in parts)
    shape = jax.ShapeDtypeStruct((parts[0].shape[0], width), jnp.bfloat16)
    work = 2 * shape.size * shape.shape[0]
    return small_kernel(unsort_kernel, [], [rank[:, None], *parts], [shape], work)[0]


def assemble_kernel(places_ref, *refs):
    blocks, whole_ref = refs[:-1], refs[-1]
    for place, block_ref in enumerate(blocks):
        size = block_ref.shape[0] // 2
        for half in range(2):
            start = pl.multiple_of(places_ref[2 * place + half], 128)
            whole_ref[pl.ds(start, size), :] = block_ref[half * size : (half + 1) * size, :]


def assemble(blocks, places):
    shape = jax.ShapeDtypeStruct((len(blocks) * blocks[0].shape[0], blocks[0].shape[1]), jnp.bfloat16)
    return small_kernel(assemble_kernel, [places], blocks, [shape])[0]


def gather_sequence(matrix, count):
    if count == 1:
        return matrix
    return lax.all_gather(matrix, "s", axis=0, tiled=True)


def scatter_sequence(matrix, count):
    if count == 1:
        return matrix
    return lax.psum_scatter(matrix, "s", scatter_dimension=0, tiled=True)


def own_bits():
    t_index = lax.axis_index("t")
    return {
        "t1": t_index >> 1,
        "t0": t_index & 1,
        "y": lax.axis_index("y"),
        "x": lax.axis_index("x"),
        "core": lax.axis_index("core"),
    }


def flip(block, name):
    if name in ("t1", "t0"):
        step = 2 if name == "t1" else 1
        return lax.ppermute(block, "t", [(i, i ^ step) for i in range(T_SIZE)])
    return lax.ppermute(block, name, [(i, i ^ 1) for i in range(PAIR)])


def relative_index(total, count, order):
    rows = total // (32 * count)
    place = jnp.arange(total, dtype=jnp.int32)
    bits, mine = {"r": place % rows, "s": place // rows % count}, own_bits()
    for index, name in enumerate(order):
        bits[name] = (place // (rows * count) >> (len(order) - 1 - index) & 1) ^ mine[name]
    row = (bits["t1"] * PAIR + bits["t0"]) * count + bits["s"]
    for name in ("y", "x", "core"):
        row = row * PAIR + bits[name]
    return row * rows + bits["r"]


def relative_columns(matrix, count, order):
    index = relative_index(matrix.shape[1], count, order)
    pick = jnp.arange(matrix.shape[1], dtype=jnp.int32)[:, None] == index[None, :]
    return linear(matrix, pick.astype(jnp.bfloat16)).astype(jnp.bfloat16)


def put_grads(pairs, outs):
    half, start = outs[0].shape[0], 0
    for left_ref, right in pairs:
        end = start + right.shape[1]
        for out_ref, lines in zip(outs, (slice(half, 2 * half), slice(0, half))):
            value = column_sum(left_ref[:, lines], right)
            out_ref[:, start:end] = value.astype(jnp.bfloat16)
        start = end
    return start


def total_rows(rows):
    return jnp.sum(rows.astype(jnp.float32), 0, keepdims=True)


def three_lefts_kernel(*refs):
    for rows_ref, out_ref in zip(refs[:3], refs[4:]):
        out_ref[...] = back_product(rows_ref, refs[3]).astype(jnp.bfloat16)


def three_lefts(attended, normed, crossed, pick):
    shape = jax.ShapeDtypeStruct(normed.shape, jnp.bfloat16)
    return small_kernel(three_lefts_kernel, [], [attended, normed, crossed, pick], [shape] * 3)


def three_kernel(
    out_left, query_left, cross_left, out_grads, query_blocks, cross_grads,
    sent_ref, kept_ref, sums_ref, columns_ref,
):
    rows = columns_ref.shape[0]
    for member in range(MEMBERS):
        columns_ref[:, member * WIDTH : (member + 1) * WIDTH] = query_blocks[
            member * rows : (member + 1) * rows, :
        ]
    pairs = [(out_left, out_grads), (query_left, columns_ref), (cross_left, cross_grads)]
    put_grads([(left, right[...]) for left, right in pairs], [sent_ref, kept_ref])
    sums_ref[...] = total_rows(columns_ref[...])


def three_grads(out_left, query_left, cross_left, out_grads, query_blocks, cross_grads):
    operands = [out_left, query_left, cross_left, out_grads, query_blocks, cross_grads]
    return pl.pallas_call(
        three_kernel,
        in_specs=in_vmem(6),
        out_specs=in_vmem(3),
        out_shape=[jax.ShapeDtypeStruct((D // 2, 3 * D), jnp.bfloat16)] * 2
        + [jax.ShapeDtypeStruct((1, D), jnp.float32)],
        scratch_shapes=[pltpu.VMEM(out_grads.shape, jnp.bfloat16)],
        compiler_params=pltpu.CompilerParams(vmem_limit_bytes=VMEM_LIMIT),
        cost_estimate=COST,
    )(*operands)


def encoder_kernel(
    me_ref, left_ref, weight_ref, *refs
):
    blocks, refs = refs[:MEMBERS], refs[MEMBERS:]
    sent_ref, kept_ref, first_ref, second_ref, sums_ref, grads_ref = refs
    join_kernel(2, me_ref, *blocks, grads_ref)
    put_grads([(left_ref, grads_ref[...])], [sent_ref, kept_ref])
    half = first_ref.shape[0]
    first_ref[...] = input_grad(grads_ref[:half, :], weight_ref[...]).astype(jnp.bfloat16)
    second_ref[...] = input_grad(grads_ref[half:, :], weight_ref[...]).astype(jnp.bfloat16)
    sums_ref[...] = total_rows(grads_ref[:, D:])


def encoder_grads(me, left, weight, blocks):
    rows = left.shape[0]
    return pl.pallas_call(
        encoder_kernel,
        in_specs=[pl.BlockSpec(memory_space=pltpu.SMEM)] + in_vmem(2 + MEMBERS),
        out_specs=in_vmem(5),
        out_shape=[jax.ShapeDtypeStruct((D // 2, 2 * D), jnp.bfloat16)] * 2
        + [jax.ShapeDtypeStruct((rows // 2, D), jnp.bfloat16)] * 2
        + [jax.ShapeDtypeStruct((1, D), jnp.float32)],
        scratch_shapes=[pltpu.VMEM((rows, 2 * D), jnp.bfloat16)],
        compiler_params=pltpu.CompilerParams(vmem_limit_bytes=VMEM_LIMIT),
        cost_estimate=COST,
    )(me, left, weight, *blocks)


def self_in_kernel(
    me_ref, left_ref, right_ref, pick_ref, one_ref, two_ref, three_ref, up_ref, query_ref,
    value_ref, *refs
):
    blocks, refs = refs[:MEMBERS], refs[MEMBERS:]
    left_sent, left_kept, right_sent, right_kept, grads_ref, small_ref = refs
    join_kernel(3, me_ref, *blocks, grads_ref)
    middle = grads_ref.shape[1] // 2
    put_grads([(left_ref, grads_ref[:, :middle])], [left_sent, left_kept])
    start = put_grads([(right_ref, grads_ref[:, middle:])], [right_sent, right_kept])

    small_ref[...] = jnp.zeros_like(small_ref)
    rows = [one_ref[0:1, :], two_ref[0:1, :], three_ref[0:1, :]]
    rows += [one_ref[1:2, :], two_ref[1:2, :], three_ref[1:2, :]]
    rows += [total_rows(grads_ref[:, :D]), total_rows(grads_ref[:, 2 * D :]), query_ref[...]]
    rows += [value_ref[...], two_ref[2:3, :], three_ref[2:3, :], one_ref[2:3, :]]
    for place, row in enumerate(rows):
        small_ref[place : place + 1, :] = row
    small_ref[13:17, :] = up_ref[...]
    half = right_sent.shape[0]
    low = small_ref[...].astype(jnp.bfloat16)
    for out_ref, lines in ((right_sent, slice(half, 2 * half)), (right_kept, slice(0, half))):
        out_ref[:, start:] = input_grad(pick_ref[lines, :], low).astype(jnp.bfloat16)


def self_in_grads(me, left, right, pick, one, two, three, up, query, value, blocks):
    rows = left.shape[0]
    half, middle = D // 2, 3 * D // 2
    outs = [jax.ShapeDtypeStruct((half, middle), jnp.bfloat16)] * 2
    outs += [jax.ShapeDtypeStruct((half, middle + 128), jnp.bfloat16)] * 2
    outs += [jax.ShapeDtypeStruct((rows, 3 * D), jnp.bfloat16)]
    operands = [left, right, pick, one, two, three, up.reshape(D, 4).T, query, value, *blocks]
    results = pl.pallas_call(
        self_in_kernel,
        in_specs=[pl.BlockSpec(memory_space=pltpu.SMEM)] + in_vmem(len(operands)),
        out_specs=in_vmem(len(outs)),
        out_shape=outs,
        scratch_shapes=[pltpu.VMEM((128, D), jnp.float32)],
        compiler_params=pltpu.CompilerParams(vmem_limit_bytes=VMEM_LIMIT),
        cost_estimate=COST,
    )(me, *operands)
    return results[:2], results[2:4], results[4]


class Halving:
    def __init__(self, parts, count, order):
        sent, self.value = parts
        self.count, self.order = count, list(order)
        self.send(sent)

    def send(self, block):
        self.sent = block.astype(jnp.bfloat16)
        self.pending = flip(self.sent, self.order.pop(0))

    def step(self):
        total = self.value.astype(jnp.float32) + self.pending.astype(jnp.float32)
        half = total.shape[0] // 2
        self.value = total[:half].astype(jnp.bfloat16)
        self.send(total[half:])

    def finish(self):
        total = self.value.astype(jnp.float32) + self.pending.astype(jnp.float32)
        if self.count > 1:
            total = lax.psum_scatter(
                total.astype(jnp.bfloat16), "s", scatter_dimension=0, tiled=True
            ).astype(jnp.float32)
        return total


def feed_grads_kernel(hidden_ref, grads_ref, rows_ref, active_grads_ref, out_ref):
    others, _, _, rows, _ = out_ref.shape

    @pl.when(pl.program_id(0) == 0)
    def _():
        value = column_sum(hidden_ref[...], grads_ref[...]).astype(jnp.bfloat16)
        value = value.reshape(PAIR, others, 4, rows, D)
        for y_index in range(PAIR):
            out_ref[:, y_index] = value[y_index]

    @pl.when(pl.program_id(0) == 1)
    def _():
        for part in range(4):
            value = column_sum(rows_ref[...], active_grads_ref[:, part * D : (part + 1) * D])
            value = value.astype(jnp.bfloat16).reshape(PAIR, others, rows, D)
            for y_index in range(PAIR):
                out_ref[:, y_index, part] = value[y_index]


def feed_grads(hidden, grads, rows, active_grads, count):
    blocks = 32 * count
    lines = D // blocks
    size = rows.shape[0]
    if count > 1:
        parts = [column_sum(hidden, grads).astype(jnp.bfloat16).reshape(-1, PAIR, 4, 4, lines, D)]
        for part in range(4):
            up = column_sum(rows, active_grads[:, part * D : (part + 1) * D])
            parts.append(up.astype(jnp.bfloat16).reshape(-1, PAIR, 4, 1, lines, D))
        return jnp.swapaxes(jnp.concatenate(parts, 3), 1, 2).reshape(-1, PAIR, 8, lines, D)
    return pl.pallas_call(
        feed_grads_kernel,
        grid=(2, T_SIZE),
        in_specs=[
            pl.BlockSpec((size, D), lambda p, i: (0, jnp.where(p == 0, i, T_SIZE - 1))),
            pl.BlockSpec((size, D), lambda p, i: (0, 0)),
            pl.BlockSpec((size, D // T_SIZE), lambda p, i: (0, jnp.where(p == 0, 0, i))),
            pl.BlockSpec((size, 4 * D), lambda p, i: (0, 0)),
        ],
        out_specs=pl.BlockSpec((4, PAIR, 4, lines, D), lambda p, i: (i, 0, p, 0, 0)),
        out_shape=jax.ShapeDtypeStruct((blocks // PAIR, PAIR, 8, lines, D), jnp.bfloat16),
        compiler_params=pltpu.CompilerParams(vmem_limit_bytes=VMEM_LIMIT),
        cost_estimate=COST,
    )(hidden, grads, rows, active_grads)


def reduce_feed(parts):
    return lax.psum_scatter(parts, ("t", "s", "x", "core"), scatter_dimension=0, tiled=True)[0]


def split_feed(halves):
    mine = lax.axis_index("y")
    return [
        lax.dynamic_index_in_dim(halves, place, 0, keepdims=False) for place in (mine, 1 - mine)
    ]


def merge_feed(kept, arrived):
    total = kept.astype(jnp.float32) + arrived.astype(jnp.float32)
    return jnp.concatenate([total[4 + part] for part in range(4)], 1), total[:4].reshape(-1, D)


def forward_kernel(
    chunk, flags_ref, q_ref, k_ref, v_ref, low_ref, high_ref, key_ref, out_ref, exact_ref, log_ref,
    masked_ref, top_ref, sum_ref, fade_ref, total_ref,
):
    step = pl.program_id(0)
    chunks = k_ref.shape[0] // chunk
    rows = q_ref.shape[0]
    lane = lax.broadcasted_iota(jnp.int32, (rows, 128), 1)
    for head in range(HEADS):
        pair = q_ref[:, (head // 2) * 128 : (head // 2 + 1) * 128] * SCALE
        masked_ref[head] = jnp.where((lane >= HD) == (head % 2 == 1), pair, 0).astype(jnp.bfloat16)
    top_ref[...] = jnp.full_like(top_ref, MASKED)
    sum_ref[...] = jnp.ones_like(sum_ref)
    sum_ref[:HEADS, :] = jnp.zeros((HEADS, rows), jnp.float32)
    fade_ref[...] = jnp.zeros_like(fade_ref)
    total_ref[...] = jnp.zeros_like(total_ref)

    def one_chunk(index, carry):
        @pl.when(flags_ref[step * chunks + index] != 0)
        def _():
            start = pl.multiple_of(index * chunk, chunk)
            here = pl.ds(start, chunk)
            keys = key_ref[here, :]
            allow = (keys >= low_ref[...]) & (keys <= high_ref[...])
            bias = jnp.where(allow, 0.0, MASKED)
            def pair_of(head):
                return slice((head // 2) * 128, (head // 2 + 1) * 128)

            scores = [
                lax.dot_general(
                    k_ref[here, pair_of(head)],
                    masked_ref[head],
                    (((1,), (1,)), ((), ())),
                    preferred_element_type=jnp.float32,
                ) + bias
                for head in range(HEADS)
            ]
            befores = [top_ref[head : head + 1, :] for head in range(HEADS)]
            afters = [
                jnp.maximum(before, jnp.max(score, 0, keepdims=True))
                for before, score in zip(befores, scores)
            ]
            exponents = [jnp.exp(score - after) for score, after in zip(scores, afters)]
            chances = [exponent.astype(jnp.bfloat16) for exponent in exponents]
            for head in range(HEADS):
                fade = jnp.exp(befores[head] - afters[head])
                top_ref[head : head + 1, :] = afters[head]
                fade_ref[head : head + 1, :] = fade
                sum_ref[head : head + 1, :] = sum_ref[head : head + 1, :] * fade + jnp.sum(
                    exponents[head], 0, keepdims=True
                )
            fades = fade_ref[...].T
            for head in range(HEADS):
                columns = slice((head // 2) * 128, (head // 2 + 1) * 128)
                total_ref[head] = total_ref[head] * fades[:, head : head + 1] + column_sum(
                    chances[head], v_ref[here, columns]
                )

        return carry

    lax.fori_loop(0, chunks, one_chunk, 0)
    shares = (1.0 / sum_ref[...]).T
    for head in range(0, HEADS, 2):
        columns = slice((head // 2) * 128, (head // 2 + 1) * 128)
        exact = jnp.where(
            lane < HD,
            total_ref[head] * shares[:, head : head + 1],
            total_ref[head + 1] * shares[:, head + 1 : head + 2],
        )
        exact_ref[:, columns] = exact
        out_ref[:, columns] = exact.astype(jnp.bfloat16)
    log_ref[:HEADS, :] = top_ref[:HEADS, :] + jnp.log(sum_ref[:HEADS, :])
    log_ref[HEADS:, :] = jnp.zeros((8 - HEADS, rows), jnp.float32)


def attend_forward(queries, keys, values, low, high, key_ids, flags, block, chunk):
    count, depth = queries[0].shape[0], keys[0].shape[0]
    whole = functools.partial(pl.BlockSpec, pipeline_mode=pl.Buffered(1))
    return pl.pallas_call(
        functools.partial(forward_kernel, chunk),
        grid_spec=pltpu.PrefetchScalarGridSpec(
            num_scalar_prefetch=1,
            grid=(count // block,),
            in_specs=[
                pl.BlockSpec((block, WIDTH), lambda i, f, c=queries[1]: (i, c)),
                whole((depth, WIDTH), lambda i, f, c=keys[1]: (0, c)),
                whole((depth, WIDTH), lambda i, f, c=values[1]: (0, c)),
                pl.BlockSpec((1, block), lambda i, f: (0, i)),
                pl.BlockSpec((1, block), lambda i, f: (0, i)),
                whole((depth, 1), lambda i, f: (0, 0)),
            ],
            out_specs=[
                pl.BlockSpec((block, WIDTH), lambda i, f: (i, 0)),
                pl.BlockSpec((block, WIDTH), lambda i, f: (i, 0)),
                pl.BlockSpec((8, block), lambda i, f: (0, i)),
            ],
            scratch_shapes=[
                pltpu.VMEM((HEADS, block, 128), jnp.bfloat16),
                pltpu.VMEM((8, block), jnp.float32),
                pltpu.VMEM((8, block), jnp.float32),
                pltpu.VMEM((8, block), jnp.float32),
                pltpu.VMEM((HEADS, block, 128), jnp.float32),
            ],
        ),
        out_shape=[
            jax.ShapeDtypeStruct((count, WIDTH), jnp.bfloat16),
            jax.ShapeDtypeStruct((count, WIDTH), jnp.float32),
            jax.ShapeDtypeStruct((8, count), jnp.float32),
        ],
        compiler_params=pltpu.CompilerParams(vmem_limit_bytes=VMEM_LIMIT),
        cost_estimate=COST,
    )(
        flags.reshape(-1), queries[0], keys[0], values[0], low[None, :], high[None, :],
        key_ids[:, None],
    )


def backward_kernel(
    chunk, flags_ref, places_ref, q_ref, k_ref, v_ref, g_ref, log_ref, exact_ref, low_ref, high_ref, key_ref,
    dq_ref, *refs,
):
    pair_refs, (q_masked, g_masked, delta_ref, turned_ref, dq_sum, dk_sum, dv_sum) = (
        refs[:-7], refs[-7:]
    )
    step = pl.program_id(0)
    chunks = k_ref.shape[0] // chunk
    rows = q_ref.shape[0]
    lane = lax.broadcasted_iota(jnp.int32, (rows, 128), 1)

    @pl.when(step == 0)
    def _():
        dk_sum[...] = jnp.zeros_like(dk_sum)
        dv_sum[...] = jnp.zeros_like(dv_sum)

        def turn(index, carry):
            start = pl.multiple_of(index * chunk, chunk)
            turned_ref[:, pl.ds(start, chunk)] = k_ref[pl.ds(start, chunk), :].T
            return carry

        lax.fori_loop(0, chunks, turn, 0)

    for head in range(HEADS):
        columns = slice((head // 2) * 128, (head // 2 + 1) * 128)
        chosen = (lane >= HD) == (head % 2 == 1)
        q_masked[head] = jnp.where(chosen, q_ref[:, columns] * SCALE, 0).astype(jnp.bfloat16)
        g_masked[head] = jnp.where(chosen, g_ref[:, columns], 0).astype(jnp.bfloat16)
    dq_sum[...] = jnp.zeros_like(dq_sum)
    members = lax.broadcasted_iota(jnp.int32, (8, WIDTH), 1) // HD
    members = (members == lax.broadcasted_iota(jnp.int32, (8, WIDTH), 0)).astype(jnp.float32)
    delta_ref[...] = lax.dot_general(
        members,
        g_ref[...].astype(jnp.float32) * exact_ref[...],
        (((1,), (1,)), ((), ())),
        precision=lax.Precision.HIGHEST,
        preferred_element_type=jnp.float32,
    )

    def one_chunk(index, carry):
        @pl.when(flags_ref[step * chunks + index] != 0)
        def _():
            start = pl.multiple_of(index * chunk, chunk)
            here = pl.ds(start, chunk)
            keys = key_ref[here, :]
            allow = (keys >= low_ref[...]) & (keys <= high_ref[...])
            bias = jnp.where(allow, 0.0, MASKED)

            def pair_of(head):
                return slice((head // 2) * 128, (head // 2 + 1) * 128)

            def against(keys_ref, head, masked):
                return lax.dot_general(
                    keys_ref[here, pair_of(head)],
                    masked[head],
                    (((1,), (1,)), ((), ())),
                    preferred_element_type=jnp.float32,
                )

            heads = range(HEADS)
            scores = [against(k_ref, head, q_masked) for head in heads]
            grads = [against(v_ref, head, g_masked) for head in heads]
            chances = [
                jnp.exp(scores[head] + bias - log_ref[head : head + 1, :]) for head in heads
            ]
            slopes = [
                (chances[head] * (grads[head] - delta_ref[head : head + 1, :])).astype(jnp.bfloat16)
                for head in heads
            ]
            chances = [chance.astype(jnp.bfloat16) for chance in chances]
            for head in heads:
                dv_sum[here, pair_of(head)] += linear(chances[head], g_masked[head])
            for head in heads:
                dk_sum[here, pair_of(head)] += linear(slopes[head], q_masked[head])
            for head in heads:
                lines = slice(head * HD, (head + 1) * HD)
                dq_sum[lines, :] += linear(turned_ref[lines, here], slopes[head])

        return carry

    lax.fori_loop(0, chunks, one_chunk, 0)
    dq_ref[...] = (dq_sum[...] * SCALE).T.astype(jnp.bfloat16)

    @pl.when(step == pl.num_programs(0) - 1)
    def _():
        for place, pair_ref in enumerate(pair_refs):
            size = pair_ref.shape[0] // 2
            for half in range(2):
                start = pl.multiple_of(places_ref[2 * place + half], 128)
                lines = slice(half * size, (half + 1) * size)
                pair_ref[lines, :WIDTH] = dk_sum[pl.ds(start, size), :].astype(jnp.bfloat16)
                pair_ref[lines, WIDTH:] = dv_sum[pl.ds(start, size), :].astype(jnp.bfloat16)


def attend_backward(
    queries, keys, values, grads, logs, exact, low, high, key_ids, flags, block, chunk, places
):
    splits = places.shape[0] // 2
    count, depth = queries[0].shape[0], keys[0].shape[0]
    whole = functools.partial(pl.BlockSpec, pipeline_mode=pl.Buffered(1))
    return pl.pallas_call(
        functools.partial(backward_kernel, chunk),
        grid_spec=pltpu.PrefetchScalarGridSpec(
            num_scalar_prefetch=2,
            grid=(count // block,),
            in_specs=[
                pl.BlockSpec((block, WIDTH), lambda i, f, p, c=queries[1]: (i, c)),
                whole((depth, WIDTH), lambda i, f, p, c=keys[1]: (0, c)),
                whole((depth, WIDTH), lambda i, f, p, c=values[1]: (0, c)),
                pl.BlockSpec((block, WIDTH), lambda i, f, p: (i, 0)),
                pl.BlockSpec((8, block), lambda i, f, p: (0, i)),
                pl.BlockSpec((block, WIDTH), lambda i, f, p: (i, 0)),
                pl.BlockSpec((1, block), lambda i, f, p: (0, i)),
                pl.BlockSpec((1, block), lambda i, f, p: (0, i)),
                whole((depth, 1), lambda i, f, p: (0, 0)),
            ],
            out_specs=[
                pl.BlockSpec((block, WIDTH), lambda i, f, p: (i, 0)),
            ]
            + [whole((depth // splits, 2 * WIDTH), lambda i, f, p: (0, 0))] * splits,
            scratch_shapes=[
                pltpu.VMEM((HEADS, block, 128), jnp.bfloat16),
                pltpu.VMEM((HEADS, block, 128), jnp.bfloat16),
                pltpu.VMEM((8, block), jnp.float32),
                pltpu.VMEM((WIDTH, depth), jnp.bfloat16),
                pltpu.VMEM((WIDTH, block), jnp.float32),
                pltpu.VMEM((depth, WIDTH), jnp.float32),
                pltpu.VMEM((depth, WIDTH), jnp.float32),
            ],
        ),
        out_shape=[
            jax.ShapeDtypeStruct((count, WIDTH), jnp.bfloat16),
        ]
        + [jax.ShapeDtypeStruct((depth // splits, 2 * WIDTH), jnp.bfloat16)] * splits,
        compiler_params=pltpu.CompilerParams(vmem_limit_bytes=VMEM_LIMIT),
        cost_estimate=COST,
    )(
        flags.reshape(-1), places, queries[0], keys[0], values[0], grads, logs, exact, low[None, :],
        high[None, :], key_ids[:, None],
    )


def needed_chunks(low, high, key_ids, block, chunk):
    first = jnp.min(low.reshape(-1, block), 1)[:, None]
    last = jnp.max(high.reshape(-1, block), 1)[:, None]
    smallest = jnp.min(key_ids.reshape(-1, chunk), 1)[None, :]
    largest = jnp.max(key_ids.reshape(-1, chunk), 1)[None, :]
    return ((largest >= first) & (smallest <= last)).astype(jnp.int32)


def on_device(
    count,
    tokens,
    encoder,
    seq_lengths,
    slot_ids,
    enc_lengths,
    cotangent,
    self_in,
    self_out,
    cross_query,
    cross_pair,
    cross_out,
    feed_up,
    feed_down,
    vectors,
    feed_bias,
    self_bias,
):

    full_self_in = fetch(self_in)
    facts = jnp.concatenate([slot_ids[0], seq_lengths[0], enc_lengths[0]], 1)
    slots = slot_ids.shape[2]
    facts_one, facts_two = to_packs(facts)
    tokens_in = jnp.concatenate(to_packs(tokens), 0)
    small = jnp.concatenate([vectors.T, feed_bias.reshape(D // 4, 4).T, self_bias[None, :]], 0)
    own_ids = jnp.concatenate([facts_one[:slots], facts_two[:slots]])
    ids = lax.all_gather(own_ids, GROUP, axis=0, tiled=True)
    ids, small = chain(ids, small)
    full_small = lax.all_gather(small, ("x", "core"), axis=1, tiled=True)
    vec = full_small[:12].astype(jnp.float32)
    bias_row = full_small[12:16].T.reshape(4 * D).astype(jnp.float32)
    self_bias_row = full_small[16].astype(jnp.float32)
    zero_row = jnp.zeros((D,), jnp.float32)
    facts_one, (self_out, cross_query) = chain(facts_one, (self_out, cross_query))
    full_out_query = fetch(jnp.concatenate([self_out, cross_query], 1))
    encoder_in = jnp.concatenate(to_packs(encoder), 0)
    tokens_in, (cross_pair, cross_out) = chain(tokens_in, (cross_pair, cross_out))
    full_cross_pair = fetch(cross_pair)
    full_cross_out = fetch(cross_out)

    lengths = facts_one[slots : slots + NSEQ]
    limits = facts_one[slots + NSEQ : slots + 2 * NSEQ]
    ends = jnp.cumsum(lengths)
    key_ids = gather_sequence(ids, count)
    rank = jnp.sum((ids[None, :] < ids[:, None]).astype(jnp.int32), 1)
    places = jnp.arange(ids.shape[0], dtype=jnp.int32)
    sorted_ids = jnp.sum(jnp.where(places[:, None] == rank[None, :], ids[None, :], 0), 1)
    key_order = gather_sequence(sorted_ids, count)
    seq_of = jnp.sum((sorted_ids[:, None] >= ends[None, :]).astype(jnp.int32), 1)
    starts = jnp.concatenate([jnp.zeros((1,), jnp.int32), ends[:-1]])
    picked = seq_of[:, None] == jnp.arange(NSEQ, dtype=jnp.int32)[None, :]
    self_low = jnp.sum(jnp.where(picked, starts[None, :], 0), 1)
    self_high = sorted_ids
    cross_low = seq_of * ENC
    cross_high = cross_low + jnp.sum(jnp.where(picked, limits[None, :], 0), 1) - 1
    enc_rows = encoder.shape[1]
    micro = lax.axis_index("t") & 1
    starts_of = []
    for index_s in range(count):
        for step in range(MEMBERS):
            core = lax.axis_index("core") ^ (step & 1)
            y_index = lax.axis_index("y") ^ (step >> 1)
            for part in range(2):
                t_index = 2 * core + (micro ^ part)
                starts_of.append(((t_index * count + index_s) * PAIR + y_index) * enc_rows)
    enc_places = jnp.stack(starts_of)
    enc_ids = jnp.arange(NSEQ * ENC, dtype=jnp.int32)
    if count > 1:
        enc_ids = (enc_places[:, None] + jnp.arange(enc_rows, dtype=jnp.int32)[None, :]).reshape(-1)
        enc_places = jnp.array([0, NSEQ * ENC // 2], jnp.int32)
    self_places = jnp.array([0, key_order.shape[0] // 2], jnp.int32)
    block = 256
    self_chunk, cross_chunk = 256, 512 if count == 1 else 384
    self_flags = needed_chunks(self_low, self_high, key_order, block, self_chunk)
    cross_flags = needed_chunks(cross_low, cross_high, enc_ids, block, cross_chunk)

    orders = {
        "x": ("core", "x", "y", "t0", "t1"),
        "y": ("core", "y", "x", "t0", "t1"),
    }

    def relative(matrix, name):
        return relative_columns(matrix, count, orders[name])

    qkv = project_heads(tokens_in, full_self_in, jnp.concatenate([vec[6], zero_row, vec[7]]))
    feed_own = stack_feed(feed_up, feed_down)
    own_heads = sort_rows(to_members(qkv), rank)
    if count > 1:
        pairs = gather_sequence(own_heads[:, WIDTH:], count)
        self_keys, self_values = (pairs, 0), (pairs, 1)
    else:
        self_keys, self_values = (own_heads, 1), (own_heads, 2)
    tokens_x, tokens_y = relative(tokens_in, "x"), relative(tokens_in, "y")
    encoder_y = relative(encoder_in, "y")
    index = relative_index(D, count, orders["y"])
    pick_y = (index[:, None] == jnp.arange(D, dtype=jnp.int32)[None, :]).astype(jnp.bfloat16)
    (tokens_x, tokens_y, encoder_y, pick_y, own_heads), (encoder_in, cotangent) = chain(
        (tokens_x, tokens_y, encoder_y, pick_y, own_heads), (encoder_in, cotangent)
    )
    grad_in = jnp.concatenate(to_packs(cotangent), 0)
    attended_heads, exact_self, log_self = attend_forward(
        (own_heads, 0), self_keys, self_values, self_low, self_high, key_order, self_flags,
        block, self_chunk,
    )
    attended_heads, feed_own = chain(attended_heads, feed_own)
    feed_far = lax.ppermute(feed_own, "x", SWAP)
    enc_pairs = project_blocks(
        encoder_in, full_cross_pair, jnp.concatenate([zero_row, vec[9]])
    )
    attended = to_members(unsort_rows([attended_heads], rank))
    attended, enc_pairs = chain(attended, enc_pairs)
    if count == 1:
        enc_heads = assemble(exchange(enc_pairs), enc_places)
    else:
        enc_heads = gather_sequence(jnp.concatenate(exchange(enc_pairs), 0), count)
    normed_one, normed_one_low, unit_one, inverse_one, cross_queries = project_norm(
        by_member(attended), full_out_query, self_bias_row, tokens_in, vec[0], vec[3],
        after=(vec[8],),
    )
    cross_heads = sort_rows(to_members(cross_queries), rank)
    crossed_heads, exact_cross, log_cross = attend_forward(
        (cross_heads, 0), (enc_heads, 0), (enc_heads, 1), cross_low, cross_high, enc_ids,
        cross_flags, block, cross_chunk,
    )
    cross_heads, (feed_own, full_cross_out) = chain(cross_heads, (feed_own, full_cross_out))
    feed_near = lax.ppermute(feed_own, "core", SWAP)
    crossed_heads, grad_in = chain(crossed_heads, grad_in)
    crossed = to_members(unsort_rows([crossed_heads], rank))
    crossed, feed_far = chain(crossed, feed_far)
    feed_shards = [feed_own, feed_near, feed_far, lax.ppermute(feed_far, "core", SWAP)]
    normed_two, normed_two_low, unit_two, inverse_two = project_norm(
        by_member(crossed), full_cross_out, vec[10], normed_one, vec[1], vec[4]
    )
    slope, hidden = feed_up_gelu(normed_two_low, feed_shards, bias_row)
    layer_low, grad_three, grad_branch, sums_three = feed_down_norm(
        hidden, feed_shards, vec[11], normed_two, vec[2], vec[5], grad_in
    )
    half = tokens_in.shape[0] // 2

    grad_pre, bias_up, grad_two, grad_crossed_out, sums_two, grad_crossed = feed_back(
        slope, feed_shards, grad_branch, grad_three, unit_two, inverse_two, vec[1],
        full_cross_out,
    )
    received, (feed_parts, layer_low) = during_members(
        grad_crossed, lambda layer, *rows: (feed_grads(*rows, count), layer),
        (layer_low, hidden, grad_branch, normed_two_low, grad_pre),
    )
    layer_out = from_packs(layer_low[:half], layer_low[half:])
    feed_sum = reduce_feed(feed_parts)
    grad_crossed_heads = sort_rows(received, rank)
    dq_heads, *enc_pair_grads = attend_backward(
        (cross_heads, 0), (enc_heads, 0), (enc_heads, 1), grad_crossed_heads, log_cross,
        exact_cross, cross_low, cross_high, enc_ids, cross_flags, block, cross_chunk, enc_places,
    )
    layer_out, dq_heads = chain(layer_out, dq_heads)
    if count > 1:
        enc_pair_grads = cut(scatter_sequence(enc_pair_grads[0], count))
    dq_blocks, (enc_pair_grads, lefts) = during_members(
        unsort_rows([dq_heads], rank),
        lambda pairs, *rows: (pairs, three_lefts(*rows, pick_y)),
        (enc_pair_grads, by_member(attended), normed_one_low, by_member(crossed)),
    )
    enc_blocks = exchange(enc_pair_grads)
    grad_one, grad_attended_out, sums_one, grad_attended = back_norm(
        by_member(dq_blocks), full_out_query, grad_two, unit_one, inverse_one, vec[0]
    )

    received, (*three_parts, query_sums) = during_members(
        grad_attended,
        lambda blocks: three_grads(
            *lefts, grad_attended_out, blocks, grad_crossed_out
        ),
        (dq_blocks,),
    )
    three_sum = Halving(three_parts, count, orders["y"])
    grad_attended_heads = sort_rows(received, rank)
    dq_heads, pair_heads = attend_backward(
        (own_heads, 0), self_keys, self_values, grad_attended_heads, log_self, exact_self,
        self_low, self_high, key_order, self_flags, block, self_chunk, self_places,
    )
    pair_heads = scatter_sequence(pair_heads, count)

    dq_heads, three_sum.pending = chain(dq_heads, three_sum.pending)
    three_sum.step()
    dq_heads, three_sum.value = chain(dq_heads, three_sum.value)

    blocks, (me, enc_blocks) = chain(
        unsort_blocks([dq_heads, pair_heads], rank), (group_index()[None], enc_blocks)
    )
    received = exchange(blocks)
    *pair_parts, enc_first, enc_rest, value_sums = encoder_grads(
        me, encoder_y, full_cross_pair, enc_blocks
    )
    (pair_parts, enc_first, enc_rest), received = chain((pair_parts, enc_first, enc_rest), received)
    pair_sum = Halving(pair_parts, count, orders["y"])
    enc_first = send_back(enc_first, 0)
    left_parts, right_parts, grad_qkv = self_in_grads(
        group_index()[None], tokens_x, tokens_y, pick_y, sums_one, sums_two, sums_three, bias_up,
        query_sums, value_sums, received,
    )
    left_sum = Halving(left_parts, count, orders["x"])
    right_sum = Halving(right_parts, count, orders["y"])
    def steps(last, *halvings):
        for halving in halvings:
            last.value, halving.pending = chain(last.value, halving.pending)
            halving.step()
            last = halving
        return last

    last = right_sum
    last.value, grad_qkv = chain(last.value, grad_qkv)
    grad_rows = back_project(grad_qkv, full_self_in, grad_one)
    last.value, grad_rows = chain(last.value, grad_rows)
    last = steps(last, left_sum, right_sum, pair_sum, three_sum)
    last.value, (enc_first, enc_rest) = chain(last.value, (enc_first, enc_rest))
    enc_second = send_back(enc_rest, 1)
    last = steps(last, right_sum, left_sum, three_sum, pair_sum)
    last.value, feed_sum = chain(last.value, feed_sum)
    feed_kept, feed_sent = split_feed(feed_sum)
    feed_arrived = flip(feed_sent, "y")
    last.value, enc_second = chain(last.value, enc_second)
    last = steps(last, right_sum)
    last.value, rows_first = chain(last.value, grad_rows[:half])
    rows_first = send_back(rows_first, 0)
    last = steps(last, left_sum, three_sum)
    last.value, (rows_first, rows_second) = chain(last.value, (rows_first, grad_rows[half:]))
    rows_second = send_back(rows_second, 1)
    last = steps(last, pair_sum)
    last.value, feed_arrived = chain(last.value, feed_arrived)
    last = steps(last, right_sum, left_sum, pair_sum)
    grad_encoder = order_back(enc_first, enc_second)
    grad_tokens = order_back(rows_first, rows_second).astype(jnp.float32)
    three, pair = three_sum.finish(), pair_sum.finish()
    left, right = left_sum.finish(), right_sum.finish()
    up_sum, down_sum = merge_feed(feed_kept, feed_arrived)
    small = right[:, 3 * D // 2 :]
    return (
        layer_out,
        grad_tokens,
        grad_encoder.astype(jnp.float32),
        jnp.concatenate([left, right[:, : 3 * D // 2]], 1),
        three[:, :D],
        three[:, D : 2 * D],
        pair,
        three[:, 2 * D :],
        up_sum,
        down_sum,
        small[:, :12],
        small[:, 13:17].reshape(-1),
        small[:, 12],
    )


def solution(mesh):
    contexts = mesh.shape["ctx"]
    count = contexts // (T_SIZE * PAIR)
    fine = Mesh(
        mesh.devices.reshape(T_SIZE, count, PAIR, PAIR, PAIR), ("t", "s", "y", "x", "core")
    )
    fsdp, ctx = ("x", "core"), ("t", "s", "y")
    in_specs = (
        P(None, ROWS, None),
        P(None, ROWS, None),
        P(fsdp, None, None),
        P(fsdp, None, ctx),
        P(fsdp, None, None),
        P(None, ROWS, None),
        P(fsdp, None),
        P(fsdp, None),
        P(fsdp, None),
        P(fsdp, None),
        P(fsdp, None),
        P(fsdp, None),
        P(fsdp, None),
        P(fsdp, None),
        P(fsdp),
        P(fsdp),
    )
    out_specs = (P(None, ROWS, None),) * 3 + (P(BLOCKS, None),) * 8 + (P(BLOCKS),) * 2
    return jax.shard_map(
        functools.partial(on_device, count),
        mesh=fine,
        in_specs=in_specs,
        out_specs=out_specs,
        check_vma=False,
    )
```
